32 devices in a mesh: section: 2 (over core), dp: 4 (over z), tensor: 4 (over y, x).
Axes of the slice: x: 2, y: 2, z: 4, core: 2. Of those that a mesh axis runs over, the one named last changes fastest.
Arguments:
- inputs: bfloat16 [96, 160, 768], P(('dp', 'tensor')), may hold values from -6 to 6
- lengths: int32 [96], P('dp'), may hold values from 95 to 160, as said below
- cotangent: bfloat16 [96, 160, 768], P(('dp', 'tensor')), may hold values from -6 to 6
- w_qkv: bfloat16 [2, 3, 768, 768], P('section', None, None, 'tensor'), may hold values from -0.21875 to 0.21875
- qv_bias: float32 [2, 2, 12, 64], P('section', None, 'tensor'), may hold values from -3 to 3
- w_out: bfloat16 [2, 768, 768], P('section', 'tensor'), may hold values from -1.25 to 1.25
- out_bias: float32 [2, 768], P('section'), may hold values from -2 to 2
- ln1_gain: float32 [2, 768], P('section'), may hold values from 0.25 to 1.75
- ln1_bias: float32 [2, 768], P('section'), may hold values from -2 to 2
- w_up: bfloat16 [2, 768, 3072], P('section', None, 'tensor'), may hold values from -0.21875 to 0.21875
- up_bias: float32 [2, 48, 64], P('section', 'tensor'), may hold values from -3 to 3
- w_down: bfloat16 [2, 3072, 768], P('section', 'tensor'), may hold values from -0.15625 to 0.15625
- down_bias: float32 [2, 768], P('section'), may hold values from -2 to 2
- ln2_gain: float32 [2, 768], P('section'), may hold values from 0.25 to 1.75
- ln2_bias: float32 [2, 768], P('section'), may hold values from -2 to 2
Outputs:
- layer_outputs: bfloat16 [2, 96, 160, 768], P('section', ('dp', 'tensor'))
- input_grads: bfloat16 [2, 96, 160, 768], P('section', ('dp', 'tensor'))
- grad_qkv: float32 [2, 3, 768, 768], P('section', None, 'dp', 'tensor')
- grad_qv_bias: float32 [2, 2, 12, 64], P('section', None, 'tensor', 'dp')
- grad_out: float32 [2, 768, 768], P('section', 'tensor', 'dp')
- grad_up: float32 [2, 768, 3072], P('section', 'dp', 'tensor')
- grad_up_bias: float32 [2, 48, 64], P('section', 'tensor', 'dp')
- grad_down: float32 [2, 3072, 768], P('section', 'tensor', 'dp')
- grad_vectors: float32 [2, 6, 768], P('section', None, ('dp', 'tensor'))
- chain_rms: float32 [2, 3, 96], P('section', None, ('dp', 'tensor'))
The draws below stay inside these ranges and needn't reach their ends.
Inputs may be any that keep to these rules, and one draw needn't show every extreme that they name: `lengths`: among the 24 chains of one index of dp, one chain has exactly 160 valid residues and another exactly 95.
All inputs are finite; a program needn't handle non-finite values.
Results may differ from the reference program's by a relative error of at most 0.025.
Values may be sent and summed in bfloat16 or wider, within the bound.
A program may use at most 192 MiB of HBM per device.

```python
import jax
import jax.numpy as jnp
from jax import lax

D = 768
HEADS = 12
HD = 64
FF = 3072
L = 160
MIN_LEN = 95
CH_DEV = 24
CHAINS = 96
LAYERS = 2


def draw_lengths(key, part):
    key = jax.random.fold_in(key, 11)
    groups = CHAINS // CH_DEV
    random_len = jax.random.randint(jax.random.fold_in(key, 1), (groups, CH_DEV), MIN_LEN, L + 1)
    longest_at = jax.random.randint(jax.random.fold_in(key, 2), (groups, 1), 0, CH_DEV)
    offset_by = jax.random.randint(jax.random.fold_in(key, 3), (groups, 1), 1, CH_DEV)
    shortest_at = (longest_at + offset_by) % CH_DEV
    slot_ids = jnp.arange(CH_DEV)[None, :]
    chosen = jnp.where(slot_ids == longest_at, L, jnp.where(slot_ids == shortest_at, MIN_LEN, random_len))
    return chosen.reshape(CHAINS).astype(jnp.int32)


def spiked(entries, own_key, source, target, parts, factor):
    owner, partner = [(jnp.arange(entries.shape[axis_at]) // (entries.shape[axis_at] // parts)).reshape([-1 if axis == axis_at else 1 for axis in range(entries.ndim)]) for axis_at in (source, target)]
    chosen = jax.random.permutation(own_key, parts)[partner]
    strong = (owner == chosen) | (owner == (partner + parts // 2) % parts)
    return jnp.where(strong, factor * entries, entries)


def block_scale(stream_key, shape, split, least, top_value):
    loudness = 1.0
    for axis_at, blocks in split:
        heights = jax.random.uniform(jax.random.fold_in(jax.random.fold_in(stream_key, 6), axis_at), (blocks,), jnp.float32, least / len(split), top_value / len(split))
        loudness = loudness * jnp.repeat(jnp.exp(heights), shape[axis_at] // blocks).reshape((-1,) + (1,) * (len(shape) - 1 - axis_at))
    return loudness


def normal_values(key, extent, scale, reach, cuts=(), held_as=jnp.bfloat16):
    factor_of = block_scale(key, extent, cuts, -0.22, 0.18) if cuts else 1.0
    array = jax.random.normal(key, extent, jnp.float32) * scale * factor_of
    return jnp.minimum(jnp.maximum(array, -reach), reach).astype(held_as)


def bell_draw_with(own_key, extent, scale, most, cuts, heavy, held_as=jnp.bfloat16):
    values = scale * jax.random.normal(own_key, extent, jnp.float32)
    if cuts:
        values = values * block_scale(own_key, extent, cuts, -0.22, 0.18)
    return jnp.clip(spiked(values, jax.random.fold_in(own_key, 3), *heavy), -most, most).astype(held_as)


def setup_inputs(seed: int = 0) -> dict:
    key_list = jax.random.split(jax.random.key(seed), 16)
    inputs = bell_draw_with(key_list[0], (CHAINS, L, D), 1.0, 6.0, ((0, 16),), (0, 2, 16, 2.0))
    lengths = draw_lengths(jax.random.fold_in(key_list[15], 71), 0)
    cotangent = bell_draw_with(key_list[2], (CHAINS, L, D), 1.0, 6.0, ((0, 16),), (0, 2, 16, 2.0))
    w_qkv = normal_values(key_list[3], (LAYERS, 3, D, D), D ** -0.5, 0.21875, ((0, 2), (3, 4)))
    qv_bias = normal_values(key_list[4], (LAYERS, 2, HEADS, HD), 0.5, 3.0, ((0, 2), (2, 4)), jnp.float32)
    w_out = normal_values(key_list[5], (LAYERS, D, D), (D // 32) ** -0.5, 1.25, ((0, 2), (1, 4)))
    out_bias = normal_values(key_list[6], (LAYERS, D), 0.3, 2.0, ((0, 2),), jnp.float32)
    ln1_gain = jnp.clip(1.0 + 0.15 * jax.random.normal(key_list[7], (LAYERS, D), jnp.float32), 0.25, 1.75)
    ln1_bias = normal_values(key_list[8], (LAYERS, D), 0.3, 2.0, ((0, 2),), jnp.float32)
    w_up = normal_values(key_list[9], (LAYERS, D, FF), D ** -0.5, 0.21875, ((0, 2), (2, 4)))
    up_bias = normal_values(key_list[10], (LAYERS, FF // HD, HD), 0.5, 3.0, ((0, 2), (1, 4)), jnp.float32)
    w_down = normal_values(key_list[11], (LAYERS, FF, D), (FF // 2) ** -0.5, 0.15625, ((0, 2), (1, 4)))
    down_bias = normal_values(key_list[12], (LAYERS, D), 0.3, 2.0, ((0, 2),), jnp.float32)
    ln2_gain = jnp.clip(1.0 + 0.15 * jax.random.normal(key_list[13], (LAYERS, D), jnp.float32), 0.25, 1.75)
    ln2_bias = normal_values(key_list[14], (LAYERS, D), 0.3, 2.0, ((0, 2),), jnp.float32)
    return dict(inputs=inputs, lengths=lengths, cotangent=cotangent, w_qkv=w_qkv, qv_bias=qv_bias, w_out=w_out, out_bias=out_bias, ln1_gain=ln1_gain, ln1_bias=ln1_bias, w_up=w_up, up_bias=up_bias, w_down=w_down, down_bias=down_bias, ln2_gain=ln2_gain, ln2_bias=ln2_bias)


@jax.custom_vjp
def low(v):
    return lax.optimization_barrier(v.astype(jnp.bfloat16)).astype(jnp.float32)

@jax.custom_vjp
def low_back(v):
    return v

def low_keep(v):
    return (low(v), None)

def low_pass(kept, grad):
    return (grad,)

def back_keep(v):
    return (v, None)

def back_low(kept, grad):
    return (low(grad),)
low.defvjp(low_keep, low_pass)
low_back.defvjp(back_keep, back_low)
EXACT_PRECISION = lax.Precision.HIGHEST
EPS_NORM = 1e-12
EPS_ROOT = 1e-06
MASK_FILL = -1000000000.0

def both_round(values):
    return low_back(low(values))

def norm_rows(values, norm_gain, norm_bias):
    centred = values - lax.optimization_barrier(jnp.mean(values, axis=-1, keepdims=True))
    spread = lax.optimization_barrier(jnp.mean(centred * centred, axis=-1, keepdims=True))
    return centred * lax.rsqrt(spread + EPS_NORM) * norm_gain + norm_bias

def token_rms(values):
    return jnp.sqrt(lax.optimization_barrier(jnp.mean(values * values, axis=-1)) + EPS_ROOT)

def layer_forward(hidden, key_alive, layer_params):
    w_qkv, qv_bias, w_out, out_bias, ln1_gain, ln1_bias, w_up, up_bias, w_down, down_bias, ln2_gain, ln2_bias = layer_params
    chains, seq_len, model_width = hidden.shape
    projected = jnp.einsum('csd,tde->tcse', low(hidden), w_qkv, precision=EXACT_PRECISION)
    query_rows = both_round(projected[0] + qv_bias[0].reshape(-1))
    key_rows = both_round(projected[1])
    value_rows = both_round(projected[2] + qv_bias[1].reshape(-1))
    head_shape = (chains, seq_len, HEADS, HD)
    raw_scores = low_back(jnp.einsum('cqhd,ckhd->chqk', query_rows.reshape(head_shape), key_rows.reshape(head_shape), precision=EXACT_PRECISION))
    scores = raw_scores * HD ** (-0.5) + jnp.where(key_alive, 0.0, MASK_FILL)[:, None, None, :]
    row_top = lax.optimization_barrier(jnp.max(scores, axis=-1, keepdims=True))
    weights = jnp.exp(scores - row_top)
    attn_probs = weights / lax.optimization_barrier(jnp.sum(weights, axis=-1, keepdims=True))
    mixed = jnp.einsum('chqk,ckhd->cqhd', low(attn_probs), value_rows.reshape(head_shape), precision=EXACT_PRECISION)
    context = both_round(mixed.reshape(chains, seq_len, model_width))
    attn_out = low_back(jnp.einsum('cse,ed->csd', context, w_out, precision=EXACT_PRECISION)) + out_bias
    normed = norm_rows(hidden + attn_out, ln1_gain, ln1_bias)
    pre_act = low_back(jnp.einsum('csd,df->csf', low(normed), w_up, precision=EXACT_PRECISION) + up_bias.reshape(-1))
    activ = low(jax.nn.gelu(pre_act, approximate=False))
    ffn_out = low_back(jnp.einsum('csf,fd->csd', activ, w_down, precision=EXACT_PRECISION)) + down_bias
    result = norm_rows(normed + ffn_out, ln2_gain, ln2_bias)
    return (result, attn_out, ffn_out)

def one_block(weights_all, block):
    block_in, block_len, block_probe = block
    key_alive = jnp.arange(L)[None, :] < block_len[:, None]
    alive = key_alive.astype(jnp.float32)
    counts = block_len.astype(jnp.float32)
    hidden = block_in
    layer_outs = []
    layer_sums = []
    for layer in range(LAYERS):
        layer_params = tuple((item[layer] for item in weights_all))
        hidden = low_back(hidden + block_probe[layer])
        result, attn_out, ffn_out = layer_forward(hidden, key_alive, layer_params)
        layer_sums.append(jnp.stack([lax.optimization_barrier(jnp.sum(token_rms(item) * alive, axis=1)) / counts for item in (hidden, attn_out, ffn_out)]))
        hidden = low(result)
        layer_outs.append(hidden)
    return (jnp.stack(layer_outs), jnp.stack(layer_sums))

def reference(inputs, lengths, cotangent, w_qkv, qv_bias, w_out, out_bias, ln1_gain, ln1_bias, w_up, up_bias, w_down, down_bias, ln2_gain, ln2_bias):
    params = tuple((item.astype(jnp.float32) for item in (w_qkv, qv_bias, w_out, out_bias, ln1_gain, ln1_bias, w_up, up_bias, w_down, down_bias, ln2_gain, ln2_bias)))
    blocks = CHAINS // CH_DEV
    shaped = (blocks, CH_DEV, L, D)
    block_inputs = inputs.astype(jnp.float32).reshape(shaped)
    block_cot = cotangent.astype(jnp.float32).reshape(shaped)
    block_lengths = lengths.reshape(blocks, CH_DEV)
    probes = jnp.zeros((blocks, LAYERS, CH_DEV, L, D), jnp.float32)
    stepper = jax.checkpoint(one_block)

    def forward(weights_all, probe_all):

        def mapped(block):
            return stepper(weights_all, block)
        layer_outs, layer_sums = lax.map(mapped, (block_inputs, block_lengths, probe_all))
        return (layer_outs[:, -1], (layer_outs, layer_sums))
    final_out, pullback, aux = jax.vjp(forward, params, probes, has_aux=True)
    layer_outs, layer_sums = aux
    grad_params, grad_probes = pullback(block_cot)
    layer_outputs = layer_outs.transpose(1, 0, 2, 3, 4).reshape(LAYERS, CHAINS, L, D).astype(jnp.bfloat16)
    input_grads = grad_probes.transpose(1, 0, 2, 3, 4).reshape(LAYERS, CHAINS, L, D).astype(jnp.bfloat16)
    chain_rms = layer_sums.transpose(1, 2, 0, 3).reshape(LAYERS, 3, CHAINS)
    grad_vectors = jnp.stack([grad_params[3], grad_params[4], grad_params[5], grad_params[9], grad_params[10], grad_params[11]], axis=1)
    return (layer_outputs, input_grads, grad_params[0], grad_params[1], grad_params[2], grad_params[6], grad_params[7], grad_params[8], grad_vectors, chain_rms)
```

```python
import functools

import jax
import jax.numpy as jnp
from jax import lax
from jax.experimental import pallas as pl
from jax.experimental.pallas import tpu as pltpu
from jax.sharding import PartitionSpec as P


f32, bf16 = jnp.float32, jnp.bfloat16
D, FB, HB, HS = 768, 768, 192, 64
NT = (((1,), (1,)), ((), ()))
NN = (((1,), (0,)), ((), ()))
TN = (((0,), (0,)), ((), ()))
def dot(a, b, dims=NN):
    return lax.dot_general(a, b, dims, preferred_element_type=f32)

EPS_NORM, EPS_ROOT = 1e-12, 1e-6
ROOT_HALF, INV_ROOT_TWO_PI = 0.7071067811865476, 0.3989422804014327

def rows(i, n):
    return pl.ds(pl.multiple_of(i * n, n), n)

def attn_fwd_block(r, x_ref, wa_ref, sp_ref, kb_ref, qkv_ref, a_ref, c_ref, acc_ref, nch, L):
    def chain(c, _):
        rs = rows(c, L)
        p = dot(x_ref[rs, :], wa_ref[:, 0:3 * HB]) + sp_ref[1:2, 0:3 * HB]
        qkv = p.astype(bf16)
        qkv_ref[rs, :] = qkv
        kb = kb_ref[pl.ds(c, 1), :]
        outs = []
        for i in range(HB // HS):
            q = qkv[:, i * HS:(i + 1) * HS]
            k = qkv[:, HB + i * HS:HB + (i + 1) * HS]
            v = qkv[:, 2 * HB + i * HS:2 * HB + (i + 1) * HS]
            s = dot(q, k, NT) * (HS ** -0.5) + kb
            e = jnp.exp(s - jnp.max(s, axis=-1, keepdims=True))
            a = (e / jnp.sum(e, axis=-1, keepdims=True)).astype(bf16)
            a_ref[c, i] = a
            outs.append(dot(a, v).astype(bf16))
        ctx = jnp.concatenate(outs, axis=1)
        c_ref[rs, :] = ctx
        acc_ref[rs, :] += dot(ctx, wa_ref[:, 3 * HB:4 * HB], NT)
        return 0
    lax.fori_loop(0, nch, chain, 0)

def mean_last(v):
    return jnp.mean(v, axis=-1, keepdims=True)

def rms_rows(v):
    return jnp.sqrt(mean_last(v * v) + EPS_ROOT)

def norm_step(x, gain, bias):
    c = x - mean_last(x)
    inv = lax.rsqrt(mean_last(c * c) + EPS_NORM)
    u = c * inv
    return u * gain + bias, u, inv

RB = 32
def ln1_fwd(x_ref, acc_ref, sp_ref, u_ref, inv_ref, nlow_ref, rms_ref, M):
    def body(i, _):
        rs = rows(i, RB)
        h = x_ref[rs, :].astype(f32)
        att = acc_ref[rs, :] + sp_ref[2:3, :]
        n, u, inv = norm_step(h + att, sp_ref[3:4, :], sp_ref[4:5, :])
        u_ref[rs, :] = u
        inv_ref[rs, :] = inv
        nlow_ref[rs, :] = n.astype(bf16)
        rms_ref[0, rs, :] = rms_rows(h)
        rms_ref[1, rs, :] = rms_rows(att)
        return 0
    lax.fori_loop(0, M // RB, body, 0)

def ffn_fwd_block(r, nlow_ref, wu_ref, wd_ref, sp_ref, g_ref, gp_ref, acc_ref, nch, L, first):
    def chain(c, _):
        rs = rows(c, L)
        n = nlow_ref[rs, :]
        for j in range(FB // 256):
            js = slice(256 * j, 256 * (j + 1))
            z = dot(n, wu_ref[:, js]) + sp_ref[0:1, js]
            cdf = 0.5 * (1.0 + lax.erf(z * ROOT_HALF))
            g_ref[rs, js] = (z * cdf).astype(bf16)
            gp_ref[rs, js] = (cdf + z * (INV_ROOT_TWO_PI * jnp.exp(-0.5 * z * z))).astype(bf16)
        t = dot(g_ref[rs, :], wd_ref[...])
        if first:
            acc_ref[rs, :] = t
        else:
            acc_ref[rs, :] += t
        return 0
    lax.fori_loop(0, nch, chain, 0)

def ln2_fwd(u1_ref, acc_ref, sp_ref, u_ref, inv_ref, y_ref, rms_ref, M):
    def body(i, _):
        rs = rows(i, RB)
        n = u1_ref[rs, :] * sp_ref[3:4, :] + sp_ref[4:5, :]
        ffn = acc_ref[rs, :] + sp_ref[5:6, :]
        y, u, inv = norm_step(n + ffn, sp_ref[6:7, :], sp_ref[7:8, :])
        u_ref[rs, :] = u
        inv_ref[rs, :] = inv
        y_ref[rs, :] = y.astype(bf16)
        rms_ref[2, rs, :] = rms_rows(ffn)
        return 0
    lax.fori_loop(0, M // RB, body, 0)

def norm_back(dn, u, inv, gain):
    du = dn * gain
    return inv * (du - mean_last(du) - u * mean_last(du * u))

def ln2_bwd(dy_ref, u_ref, inv_ref, sp_ref, dx_ref, df_ref, vec_ref, M):
    def body(i, carry):
        a, b, c = carry
        rs = rows(i, RB)
        dy = dy_ref[rs, :].astype(f32)
        u = u_ref[rs, :]
        dx = norm_back(dy, u, inv_ref[rs, :], sp_ref[6:7, :])
        dx_ref[rs, :] = dx
        df_ref[rs, :] = dx.astype(bf16)
        return (a + part8(dx), b + part8(dy * u), c + part8(dy))
    z = jnp.zeros((8, D), f32)
    a, b, c = lax.fori_loop(0, M // RB, body, (z, z, z))
    vec_ref[3:4, :] = jnp.sum(a, axis=0, keepdims=True)
    vec_ref[4:5, :] = jnp.sum(b, axis=0, keepdims=True)
    vec_ref[5:6, :] = jnp.sum(c, axis=0, keepdims=True)

def part8(v):
    t = v[0:8]
    for i in range(1, v.shape[0] // 8):
        t = t + v[8 * i:8 * (i + 1)]
    return t

def ffn_bwd_block(r, df_ref, wu_ref, wd_ref, gp_ref, dz_ref, dx_ref, ub_ref, nch, L):
    def chain(c, tot):
        rs = rows(c, L)
        df = df_ref[rs, :]
        tots = []
        for j in range(FB // 256):
            js = slice(256 * j, 256 * (j + 1))
            dg = dot(df, wd_ref[js, :], NT)
            dz = (dg * gp_ref[rs, js].astype(f32)).astype(bf16)
            dz_ref[rs, js] = dz
            tots.append(tot[:, js] + part8(dz.astype(f32)))
        dx_ref[rs, :] += dot(dz_ref[rs, :], wu_ref[...], NT)
        return jnp.concatenate(tots, axis=1)
    tot = lax.fori_loop(0, nch, chain, jnp.zeros((8, FB), f32))
    ub_ref[...] = jnp.sum(tot, axis=0, keepdims=True)

def ln1_bwd(dn_ref, u_ref, inv_ref, sp_ref, da_ref, vec_ref, M):
    def body(i, carry):
        a, b, c = carry
        rs = rows(i, RB)
        dn = dn_ref[rs, :]
        u = u_ref[rs, :]
        dx = norm_back(dn, u, inv_ref[rs, :], sp_ref[3:4, :])
        dn_ref[rs, :] = dx
        da_ref[rs, :] = dx.astype(bf16)
        return (a + part8(dx), b + part8(dn * u), c + part8(dn))
    z = jnp.zeros((8, D), f32)
    a, b, c = lax.fori_loop(0, M // RB, body, (z, z, z))
    vec_ref[0:1, :] = jnp.sum(a, axis=0, keepdims=True)
    vec_ref[1:2, :] = jnp.sum(b, axis=0, keepdims=True)
    vec_ref[2:3, :] = jnp.sum(c, axis=0, keepdims=True)

def attn_bwd_block(r, da_ref, wa_ref, qkv_ref, a_ref, dqkv_ref, dx_ref, qb_ref, nch, L):
    def chain(c, tot):
        rs = rows(c, L)
        dc = dot(da_ref[rs, :], wa_ref[:, 3 * HB:4 * HB]).astype(bf16)
        qkv = qkv_ref[rs, :]
        dqs, dks, dvs = [], [], []
        for i in range(HB // HS):
            q = qkv[:, i * HS:(i + 1) * HS]
            k = qkv[:, HB + i * HS:HB + (i + 1) * HS]
            v = qkv[:, 2 * HB + i * HS:2 * HB + (i + 1) * HS]
            dci = dc[:, i * HS:(i + 1) * HS]
            a = a_ref[c, i]
            af = a.astype(f32)
            dvs.append(dot(a, dci, TN))
            dr = dot(dci, v, NT)
            ds = (af * (dr - jnp.sum(af * dr, axis=-1, keepdims=True)) * (HS ** -0.5)).astype(bf16)
            dqs.append(dot(ds, k))
            dks.append(dot(ds, q, TN))
        dqkv = jnp.concatenate(dqs + dks + dvs, axis=1).astype(bf16)
        dqkv_ref[rs, :] = dqkv
        dx_ref[rs, :] += dot(dqkv, wa_ref[:, 0:3 * HB], NT)
        return tot + part8(dqkv.astype(f32))
    tot = lax.fori_loop(0, nch, chain, jnp.zeros((8, 3 * HB), f32))
    qb_ref[...] = jnp.sum(tot, axis=0, keepdims=True)

def wgrad(xt_ref, y_ref, out_ref, cols, out0):
    W = 192
    def body(i, _):
        rs = rows(i, W)
        out_ref[rs, out0:out0 + cols] = dot(xt_ref[rs, :], y_ref[...]).astype(bf16)
        return 0
    lax.fori_loop(0, D // W, body, 0)
MESH = pl.DeviceIdType.MESH
HALF = 384
KA, KU, KD = 0, 1, 2

def up_block(nlow_ref, wu_ref, sp_ref, g_ref, gp_ref, nch, L):
    def chain(c, _):
        rs = rows(c, L)
        n = nlow_ref[rs, :]
        for j in range(FB // 256):
            js = slice(256 * j, 256 * (j + 1))
            z = dot(n, wu_ref[:, js]) + sp_ref[0:1, js]
            cdf = 0.5 * (1.0 + lax.erf(z * ROOT_HALF))
            g_ref[rs, js] = (z * cdf).astype(bf16)
            gp_ref[rs, js] = (cdf + z * (INV_ROOT_TWO_PI * jnp.exp(-0.5 * z * z))).astype(bf16)
        return 0
    lax.fori_loop(0, nch, chain, 0)

def down_block(g_ref, wd_ref, acc_ref, nch, L):
    def chain(c, _):
        rs = rows(c, L)
        acc_ref[rs, :] += dot(g_ref[rs, :], wd_ref[...])
        return 0
    lax.fori_loop(0, nch, chain, 0)

def k1_kernel(nch, L,
              wa_in, wu_in, wd_in, sp_in, x_in, kb_ref, live_ref,
              w_out, sp_out, qkv_out, a_out, c_out, u_out, inv_out, g_out, gp_out, y_out, rms_out,
              wv, spv, xb, qkv, a, c, u, inv, g, gp, nlow, acc, rms, rmsv,
              recv, send, sp_recv, sp_send, loc, wsave, ssave, go):
    M = nch * L
    s = lax.axis_index("section")
    t = lax.axis_index("tensor")
    xn = {"tensor": t + 1 - 2 * lax.rem(t, 2)}
    yn = {"tensor": t + 2 - 4 * lax.rem(t // 2, 2)}
    sib = {"section": 1 - s}
    srcs = (wa_in, wu_in, wd_in)

    def remote(src, dst, ss, rs, dev):
        return pltpu.make_async_remote_copy(src_ref=src, dst_ref=dst, send_sem=ss, recv_sem=rs, device_id=dev, device_id_type=MESH)

    def part(l, k, p):
        if p < 3:
            return wv.at[l, k, p]
        return wv.at[l, k, 3, pl.ds((p - 3) * HALF, HALF)]

    def wait_part(l, k, p):
        ref = part(l, k, p)
        pltpu.make_async_copy(ref, ref, recv.at[l, k, p]).wait()

    def own_sends(l, k):
        return [remote(srcs[k], wv.at[l, k, 1], send.at[k, 0], recv.at[l, k, 1], xn),
                remote(srcs[k], wv.at[l, k, 2], send.at[k, 1], recv.at[l, k, 2], yn)]
    def own_local(l, k):
        return [remote(srcs[k], wv.at[l, k, 0], send.at[k, 4], recv.at[l, k, 0], sib)]
    def fwd_y(l, k):
        return remote(wv.at[l, k, 1, pl.ds(0, HALF)], wv.at[l, k, 3, pl.ds(0, HALF)], send.at[k, 2], recv.at[l, k, 3], yn)
    def fwd_x(l, k):
        return remote(wv.at[l, k, 2, pl.ds(HALF, HALF)], wv.at[l, k, 3, pl.ds(HALF, HALF)], send.at[k, 3], recv.at[l, k, 4], xn)
    def to_sib(l, k, p):
        return remote(part(l, k, p), part(l, k, p), send.at[k, 4 + p], recv.at[l, k, p], sib)

    def save_w(l, k, p):
        dst = w_out.at[l, k, p] if p < 3 else w_out.at[l, k, 3, pl.ds((p - 3) * HALF, HALF)]
        return pltpu.make_async_copy(part(l, k, p), dst, wsave.at[l, k, p])

    def arrive(l, k, p):
        wait_part(l, k, p)
        @pl.when(s == l)
        def _():
            if p == 1:
                fwd_y(l, k).start()
            if p == 2:
                fwd_x(l, k).start()
            if p > 0:
                to_sib(l, k, p).start()
        save_w(l, k, p).start()

    def sp_wait(l, p):
        pltpu.make_async_copy(spv.at[l, p], spv.at[l, p], sp_recv.at[l, p]).wait()
    def sp_sends(l):
        return [remote(sp_in, spv.at[l, 1], sp_send.at[0], sp_recv.at[l, 1], xn),
                remote(sp_in, spv.at[l, 2], sp_send.at[1], sp_recv.at[l, 2], yn),
                remote(sp_in, spv.at[l, 0], sp_send.at[2], sp_recv.at[l, 0], sib)]
    def sp_fwd(l):
        return remote(spv.at[l, 1], spv.at[l, 3], sp_send.at[3], sp_recv.at[l, 3], yn)
    def sp_sib(l, p):
        return remote(spv.at[l, p], spv.at[l, p], sp_send.at[3 + p], sp_recv.at[l, p], sib)

    barrier = pltpu.get_barrier_semaphore()
    for dev in (xn, yn, sib):
        pl.semaphore_signal(barrier, inc=1, device_id=dev, device_id_type=MESH)
    pl.semaphore_wait(barrier, 3)

    for l in range(2):
        @pl.when(s == l)
        def _():
            for d in sp_sends(l):
                d.start()
            pltpu.make_async_copy(sp_in, spv.at[l, 0], sp_recv.at[l, 0]).start()
            if l == 0:
                for d in own_sends(l, KA):
                    d.start()
            for k in range(3):
                pltpu.make_async_copy(srcs[k], wv.at[l, k, 0], recv.at[l, k, 0]).start()
                for d in own_local(l, k):
                    d.start()
            if l == 0:
                for k in (KU, KD):
                    for d in own_sends(l, k):
                        d.start()
    xcopy = pltpu.make_async_copy(x_in, xb, loc.at[0])
    xcopy.start()
    for l in range(2):
        sp_wait(l, 0)
        sp_wait(l, 1)
        @pl.when(s == l)
        def _():
            sp_fwd(l).start()
            sp_sib(l, 1).start()
        sp_wait(l, 2)
        @pl.when(s == l)
        def _():
            sp_sib(l, 2).start()
        sp_wait(l, 3)
        @pl.when(s == l)
        def _():
            sp_sib(l, 3).start()
    xcopy.wait()
    spsave = pltpu.make_async_copy(spv, sp_out, loc.at[1])
    spsave.start()

    def saves(l, which):
        pairs = {0: (qkv, qkv_out.at[l]), 1: (a, a_out.at[l]), 2: (c, c_out.at[l]), 3: (u.at[0], u_out.at[l, 0]),
                 4: (inv, inv_out.at[l]), 5: (g, g_out.at[l]), 6: (gp, gp_out.at[l]), 7: (u.at[1], u_out.at[l, 1]), 8: (xb, y_out.at[l])}
        src, dst = pairs[which]
        return pltpu.make_async_copy(src, dst, ssave.at[which])

    def layer(l, _):
        acc[...] = jnp.zeros_like(acc)
        @pl.when(l == 1)
        def _():
            for w in (0, 1, 2):
                saves(0, w).wait()

        def attn_step(r, _):
            @pl.when(r == 0)
            def _():
                arrive(l, KA, 0)
            @pl.when(r == 1)
            def _():
                arrive(l, KA, 1)
                arrive(l, KA, 2)
            @pl.when(r == 3)
            def _():
                arrive(l, KU, 1)
                arrive(l, KU, 2)
                arrive(l, KA, 3)
                arrive(l, KA, 4)
            attn_fwd_block(r, xb, wv.at[l, KA, r], spv.at[l, r], kb_ref, qkv.at[r], a.at[r], c.at[r], acc, nch, L)
            return 0
        lax.fori_loop(0, 4, attn_step, 0)
        for w in (0, 1, 2):
            saves(l, w).start()
        @pl.when(l == 1)
        def _():
            for w in (3, 4, 5, 6, 7):
                saves(0, w).wait()
        ln1_fwd(xb, acc, spv.at[l, 0], u.at[0], inv.at[0], nlow, rms, M)
        saves(l, 3).start()

        def up_step(r, _):
            @pl.when(r == 0)
            def _():
                arrive(l, KU, 0)
            @pl.when(r == 3)
            def _():
                arrive(l, KD, 1)
                arrive(l, KD, 2)
                @pl.when((l == 0) & (s == 0))
                def _():
                    pl.semaphore_signal(go, inc=1, device_id=sib, device_id_type=MESH)
                @pl.when((l == 0) & (s == 1))
                def _():
                    pl.semaphore_wait(go, 1)
                    for k in range(3):
                        for d in own_sends(1, k):
                            d.start()
                arrive(l, KU, 3)
                arrive(l, KU, 4)
            up_block(nlow, wv.at[l, KU, r], spv.at[l, r], g.at[r], gp.at[r], nch, L)
            return 0
        lax.fori_loop(0, 4, up_step, 0)
        saves(l, 5).start()
        saves(l, 6).start()
        acc[...] = jnp.zeros_like(acc)
        @pl.when(l == 1)
        def _():
            saves(0, 8).wait()

        def down_step(r, _):
            @pl.when(r == 0)
            def _():
                arrive(l, KD, 0)
            @pl.when(r == 3)
            def _():
                arrive(l, KD, 3)
                arrive(l, KD, 4)
            down_block(g.at[r], wv.at[l, KD, r], acc, nch, L)
            return 0
        lax.fori_loop(0, 4, down_step, 0)
        ln2_fwd(u.at[0], acc, spv.at[l, 0], u.at[1], inv.at[1], xb, rms, M)
        for w in (4, 7, 8):
            saves(l, w).start()
        for k in range(3):
            for ch in range(nch):
                rs = slice(ch * L, (ch + 1) * L)
                v = jnp.sum(rms[k, rs, :] * live_ref[rs, :], axis=0, keepdims=True)
                rmsv[l, pl.ds(k * nch + ch, 1), :] = jnp.broadcast_to(v, (1, 128))
        return 0
    lax.fori_loop(0, 2, layer, 0)
    for w in range(9):
        saves(1, w).wait()
    rc = pltpu.make_async_copy(rmsv, rms_out, loc.at[0])
    rc.start()
    rc.wait()
    spsave.wait()
    for l in range(2):
        for k in range(3):
            for p in range(5):
                save_w(l, k, p).wait()
        @pl.when(s == l)
        def _():
            for k in range(3):
                for d in own_sends(l, k) + own_local(l, k) + [fwd_y(l, k), fwd_x(l, k)] + [to_sib(l, k, p) for p in range(1, 5)]:
                    d.wait_send()
            for d in sp_sends(l) + [sp_fwd(l)] + [sp_sib(l, p) for p in range(1, 4)]:
                d.wait_send()

def run_k1(nch, L, wa, wu, wd, sp, x, kb, live):
    M = nch * L
    S = jax.ShapeDtypeStruct
    V = pltpu.VMEM
    any_ = pl.BlockSpec(memory_space=pl.ANY)
    vm = pl.BlockSpec(memory_space=pltpu.VMEM)
    outs = (S((2, 3, 4, D, 768), bf16), S((2, 4, 8, D), f32), S((2, 4, M, 3 * HB), bf16), S((2, 4, nch, 3, L, L), bf16), S((2, 4, M, HB), bf16),
            S((2, 2, M, D), f32), S((2, 2, M, 1), f32), S((2, 4, M, FB), bf16), S((2, 4, M, FB), bf16), S((2, M, D), bf16), S((2, 16, 128), f32))
    DMA = pltpu.SemaphoreType.DMA
    return pl.pallas_call(
        functools.partial(k1_kernel, nch, L),
        out_shape=outs,
        in_specs=[any_] * 5 + [vm] * 2,
        out_specs=[any_] * len(outs),
        scratch_shapes=[V((2, 3, 4, D, 768), bf16), V((2, 4, 8, D), f32), V((M, D), bf16), V((4, M, 3 * HB), bf16), V((4, nch, 3, L, L), bf16), V((4, M, HB), bf16),
                        V((2, M, D), f32), V((2, M, 1), f32), V((4, M, FB), bf16), V((4, M, FB), bf16), V((M, D), bf16), V((M, D), f32), V((3, M, 1), f32), V((2, 16, 128), f32),
                        DMA((2, 3, 5)), DMA((3, 9)), DMA((2, 4)), DMA((7,)), DMA((2,)), DMA((2, 3, 5)), DMA((9,)), pltpu.SemaphoreType.REGULAR],
        compiler_params=pltpu.CompilerParams(collective_id=0, has_side_effects=True, vmem_limit_bytes=60 << 20),
        name="gather_forward",
    )(wa, wu, wd, sp, x, kb, live)

def bwd_kernel(nch, L, dy, x, wa, wu, wd, sp, qkv, a, c, u, inv, g, gp, dh, gd, gu, ga, vec, ub, qb, dx, df, dz, dqkv, xt, ct):
    M = nch * L
    ln2_bwd(dy, u.at[1], inv.at[1], sp.at[0], dx, df, vec, M)
    xt[...] = df[...].T
    def down_grad(r, _):
        wgrad(xt, g.at[r], gd.at[r], FB, 0)
        return 0
    lax.fori_loop(0, 4, down_grad, 0)
    def normed(i, _):
        rs = rows(i, RB)
        ct[rs, :] = (u[0, rs, :] * sp[0, 3:4, :] + sp[0, 4:5, :]).astype(bf16)
        return 0
    lax.fori_loop(0, M // RB, normed, 0)
    xt[...] = ct[...].T
    def ffn(r, _):
        ffn_bwd_block(r, df, wu.at[r], wd.at[r], gp.at[r], dz, dx, ub.at[r], nch, L)
        wgrad(xt, dz, gu.at[r], FB, 0)
        return 0
    lax.fori_loop(0, 4, ffn, 0)
    ln1_bwd(dx, u.at[0], inv.at[0], sp.at[0], df, vec, M)
    xt[...] = df[...].T
    def out_grad(r, _):
        wgrad(xt, c.at[r], ga.at[r], HB, 3 * HB)
        return 0
    lax.fori_loop(0, 4, out_grad, 0)
    xt[...] = x[...].T
    def attn(r, _):
        attn_bwd_block(r, df, wa.at[r], qkv.at[r], a.at[r], dqkv, dx, qb.at[r], nch, L)
        wgrad(xt, dqkv, ga.at[r], 3 * HB, 0)
        return 0
    lax.fori_loop(0, 4, attn, 0)
    dh[...] = dx[...].astype(bf16)


def run_bwd(nch, L, l, *ops):
    M = nch * L
    S = jax.ShapeDtypeStruct
    V = pltpu.VMEM
    return pl.pallas_call(
        functools.partial(bwd_kernel, nch, L),
        out_shape=(S((M, D), bf16), S((4, D, FB), bf16), S((4, D, FB), bf16), S((4, D, FB), bf16), S((8, D), f32), S((4, 1, FB), f32), S((4, 1, 3 * HB), f32)),
        scratch_shapes=[V((M, D), f32), V((M, D), bf16), V((M, FB), bf16), V((M, 3 * HB), bf16), V((D, M), bf16), V((M, D), bf16)],
        compiler_params=pltpu.CompilerParams(vmem_limit_bytes=62 << 20),
        name="backward",
    )(*ops)


def on_device(inputs, lengths, cotangent, w_qkv, qv_bias, w_out, out_bias, ln1_gain, ln1_bias, w_up, up_bias, w_down, down_bias, ln2_gain, ln2_bias):
    s = lax.axis_index("section")
    t = lax.axis_index("tensor")
    n_dp = lax.axis_size("dp")
    chains, L, _ = inputs.shape
    nch = chains // 2
    M = nch * L
    wa = jnp.concatenate([w_qkv[0, 0], w_qkv[0, 1], w_qkv[0, 2], w_out[0].T], axis=1)
    z = jnp.zeros((HB,), f32)
    sp = jnp.stack([up_bias[0].reshape(-1), jnp.concatenate([qv_bias[0, 0].reshape(-1), z, qv_bias[0, 1].reshape(-1), z]),
                    out_bias[0], ln1_gain[0], ln1_bias[0], down_bias[0], ln2_gain[0], ln2_bias[0]])
    x = lax.dynamic_slice_in_dim(inputs, s * nch, nch, 0).reshape(M, D)
    dy = lax.dynamic_slice_in_dim(cotangent, s * nch, nch, 0).reshape(M, D)
    own_len = lax.dynamic_slice_in_dim(lengths, t * chains, chains, 0)
    my_len = lax.dynamic_slice_in_dim(own_len, s * nch, nch, 0)
    alive = jnp.arange(L)[None] < my_len[:, None]
    kb = jnp.where(alive, 0.0, -1e9).astype(f32)
    live = alive.astype(f32).reshape(M, 1)
    w_all, sp_all, qkv, a, c, u, inv, g, gp, y, rms = run_k1(nch, L, wa, w_up[0], w_down[0], sp, x, kb, live)

    def swap(v):
        return lax.ppermute(v, "section", [(0, 1), (1, 0)])

    def own_other(v0, v1):
        return jnp.where(s == 0, v0, v1), jnp.where(s == 0, v1, v0)

    def both_halves(v0, v1, axis):
        own, other = own_other(v0, v1)
        got = swap(other)
        return jnp.where(s == 0, jnp.concatenate([own, got], axis), jnp.concatenate([got, own], axis))

    grads = []
    d = dy
    dhs = [None, None]
    for l in (1, 0):
        xin = x if l == 0 else y[0]
        d, gd, gu, ga, vec, ub, qb = run_bwd(nch, L, l, d, xin, w_all[l, 0], w_all[l, 1], w_all[l, 2], sp_all[l], qkv[l], a[l], c[l], u[l], inv[l], g[l], gp[l])
        dhs[l] = d
        grads.append((gd, gu, ga, vec, ub, qb))
    l1, l0 = grads
    total = []
    for i in range(6):
        own, other = own_other(l0[i], l1[i])
        total.append(own.astype(f32) + swap(other).astype(f32))
    gd, gu, ga, vec, ub, qb = total
    order = jnp.bitwise_xor(jnp.arange(4), t)

    def scatter(v, shape):
        v = jnp.take(v, order, axis=0)
        v = v.reshape((4, n_dp, D // n_dp) + v.shape[2:])
        v = jnp.moveaxis(v, 0, 1).reshape((n_dp * 4, D // n_dp) + v.shape[3:])
        return lax.psum_scatter(v.astype(bf16), ("dp", "tensor"), scatter_dimension=0, tiled=True)[0].astype(f32)
    gd = scatter(gd, None)
    gu = scatter(gu, None)
    ga = scatter(ga, None)
    dd = D // n_dp
    vec = lax.psum_scatter(vec[:6], ("dp", "tensor"), scatter_dimension=1, tiled=True)
    ub = jnp.take(lax.psum(ub[:, 0], "dp"), order, axis=0)
    ub = lax.psum_scatter(ub, "tensor", scatter_dimension=0, tiled=True).reshape(FB // HS, HS)
    qb = jnp.take(lax.psum(qb[:, 0], "dp"), order, axis=0)
    qb = lax.psum_scatter(qb, "tensor", scatter_dimension=0, tiled=True).reshape(3, HB // HS, HS)
    j = lax.axis_index("dp")
    part = HS // n_dp
    ub = lax.dynamic_slice_in_dim(ub, j * part, part, 1)
    qb = lax.dynamic_slice_in_dim(qb, j * part, part, 2)[0::2]
    y0, y1 = y[0].reshape(nch, L, D), y[1].reshape(nch, L, D)
    d0, d1 = dhs[0].reshape(nch, L, D), dhs[1].reshape(nch, L, D)
    outs = both_halves(y0, y1, 0)
    dins = both_halves(d0, d1, 0)
    sums = rms[:, :3 * nch, 0].reshape(2, 3, nch)
    sums = both_halves(sums[0], sums[1], 1) / own_len.astype(f32)
    gq = ga[:, :3 * HB].reshape(dd, 3, HB).transpose(1, 0, 2)
    return (outs[None], dins[None], gq[None], qb[None], ga[:, 3 * HB:].T[None], gu[None], ub[None], gd.T[None], vec[None], sums[None])


def solution(mesh):
    in_specs = (
        P(("dp", "tensor"), None, None),
        P("dp"),
        P(("dp", "tensor"), None, None),
        P("section", None, None, "tensor"),
        P("section", None, "tensor", None),
        P("section", "tensor", None),
        P("section", None),
        P("section", None),
        P("section", None),
        P("section", None, "tensor"),
        P("section", "tensor", None),
        P("section", "tensor", None),
        P("section", None),
        P("section", None),
        P("section", None),
    )
    out_specs = (
        P("section", ("dp", "tensor"), None, None),
        P("section", ("dp", "tensor"), None, None),
        P("section", None, "dp", "tensor"),
        P("section", None, "tensor", "dp"),
        P("section", "tensor", "dp"),
        P("section", "dp", "tensor"),
        P("section", "tensor", "dp"),
        P("section", "tensor", "dp"),
        P("section", None, ("dp", "tensor")),
        P("section", None, ("dp", "tensor")),
    )
    return jax.shard_map(on_device, mesh=mesh, in_specs=in_specs, out_specs=out_specs, check_vma=False)
```

```python
import functools

import jax
import jax.numpy as jnp
from jax import lax
from jax.experimental import pallas as pl
from jax.experimental.pallas import tpu as pltpu
from jax.sharding import PartitionSpec as P


f32, bf16 = jnp.float32, jnp.bfloat16
D, FB, HB, HS = 768, 768, 192, 64
NT = (((1,), (1,)), ((), ()))
NN = (((1,), (0,)), ((), ()))
TN = (((0,), (0,)), ((), ()))
EPS_NORM, EPS_ROOT = 1e-12, 1e-6
MASK_FILL = -1e9
ROOT_HALF, INV_ROOT_TWO_PI = 0.7071067811865476, 0.3989422804014327
MESH = pl.DeviceIdType.MESH
KA, KU, KD = 0, 1, 2
HPB = HB // HS


def dot(a, b, dims=NN):
    return lax.dot_general(a, b, dims, preferred_element_type=f32)


def rows(i, n):
    return pl.ds(pl.multiple_of(i * n, n), n)


def mean_last(v):
    return jnp.mean(v, axis=-1, keepdims=True)


def rms_rows(v):
    return jnp.sqrt(mean_last(v * v) + EPS_ROOT)


def norm_step(x, gain, bias):
    c = x - mean_last(x)
    inv = lax.rsqrt(mean_last(c * c) + EPS_NORM)
    u = c * inv
    return u * gain + bias, u, inv


def norm_back(dn, u, inv, gain):
    du = dn * gain
    return inv * (du - mean_last(du) - u * mean_last(du * u))


def part8(v):
    t = v[0:8]
    for i in range(1, v.shape[0] // 8):
        t = t + v[8 * i:8 * (i + 1)]
    return t


def col_sum(v):
    return jnp.sum(part8(v), axis=0, keepdims=True)


def row_block(M):
    for n in (96, 80, 64, 48, 32, 16):
        if M % n == 0:
            return n
    return M


def attn_fwd_block(x_ref, wa_ref, sp_ref, kb_ref, qkv_ref, a_ref, c_ref, acc_ref, nch, L):
    qkv_ref[...] = (dot(x_ref[...], wa_ref[:, 0:3 * HB]) + sp_ref[1:2, 0:3 * HB]).astype(bf16)
    for c in range(nch):
        rs = slice(c * L, (c + 1) * L)
        qkv = qkv_ref[rs, :]
        kb = kb_ref[c:c + 1, :]

        def head(t, i):
            return qkv[:, t * HB + i * HS:t * HB + (i + 1) * HS]
        scores = [dot(head(0, i), head(1, i), NT) * (HS ** -0.5) + kb for i in range(HPB)]
        probs = []
        for i in range(HPB):
            e = jnp.exp(scores[i] - jnp.max(scores[i], axis=-1, keepdims=True))
            a = (e / jnp.sum(e, axis=-1, keepdims=True)).astype(bf16)
            a_ref[c, i] = a
            probs.append(a)
        c_ref[rs, :] = jnp.concatenate([dot(probs[i], head(2, i)).astype(bf16) for i in range(HPB)], axis=1)
    acc_ref[...] += dot(c_ref[...], wa_ref[:, 3 * HB:4 * HB], NT)


def ln1_fwd(x_ref, acc_ref, sp_ref, u_ref, inv_ref, nlow_ref, rms_ref, M):
    rb = M // 3 if M % 48 == 0 else M

    def body(i, _):
        rs = rows(i, rb)
        h = x_ref[rs, :].astype(f32)
        att = acc_ref[rs, :] + sp_ref[2:3, :]
        n, u, inv = norm_step(h + att, sp_ref[3:4, :], sp_ref[4:5, :])
        u_ref[rs, :] = u
        inv_ref[rs, :] = inv
        nlow_ref[rs, :] = n.astype(bf16)
        rms_ref[0, rs, :] = rms_rows(h)
        rms_ref[1, rs, :] = rms_rows(att)
        return 0
    lax.fori_loop(0, M // rb, body, 0)


def up_block(nlow_ref, wu_ref, sp_ref, g_ref, gp_ref):
    for j in range(FB // 256):
        js = slice(256 * j, 256 * (j + 1))
        z = dot(nlow_ref[...], wu_ref[:, js]) + sp_ref[0:1, js]
        cdf = 0.5 * (1.0 + lax.erf(z * ROOT_HALF))
        g_ref[:, js] = (z * cdf).astype(bf16)
        gp_ref[:, js] = cdf + z * (INV_ROOT_TWO_PI * jnp.exp(-0.5 * z * z))


def down_block(g_ref, wd_ref, acc_ref):
    acc_ref[...] += dot(g_ref[...], wd_ref[...])


def ln2_fwd(u1_ref, acc_ref, sp_ref, u_ref, inv_ref, y_ref, rms_ref, M):
    rb = M // 3 if M % 48 == 0 else M

    def body(i, _):
        rs = rows(i, rb)
        n = u1_ref[rs, :] * sp_ref[3:4, :] + sp_ref[4:5, :]
        ffn = acc_ref[rs, :] + sp_ref[5:6, :]
        y, u, inv = norm_step(n + ffn, sp_ref[6:7, :], sp_ref[7:8, :])
        u_ref[rs, :] = u
        inv_ref[rs, :] = inv
        y_ref[rs, :] = y.astype(bf16)
        rms_ref[2, rs, :] = rms_rows(ffn)
        return 0
    lax.fori_loop(0, M // rb, body, 0)


def norm_bwd(dy_ref, u_ref, inv_ref, gain, dx_ref, low_ref, sm_ref, row, M):
    rb = row_block(M)

    def body(i, carry):
        a, b, c = carry
        rs = rows(i, rb)
        dy = dy_ref[rs, :].astype(f32)
        u = u_ref[rs, :]
        dx = norm_back(dy, u, inv_ref[rs, :], gain)
        dx_ref[rs, :] = dx
        low_ref[rs, :] = dx.astype(bf16)
        return (a + part8(dx), b + part8(dy * u), c + part8(dy))
    z = jnp.zeros((8, D), f32)
    sums = lax.fori_loop(0, M // rb, body, (z, z, z))
    for k in range(3):
        sm_ref[row + k:row + k + 1, :] = jnp.sum(sums[k], axis=0, keepdims=True)


def ffn_bwd_block(df_ref, wu_ref, wd_ref, gp_ref, dz_ref, dx_ref, ub_ref):
    for j in range(FB // 256):
        js = slice(256 * j, 256 * (j + 1))
        dz = (dot(df_ref[...], wd_ref[js, :], NT) * gp_ref[:, js]).astype(bf16)
        dz_ref[:, js] = dz
        ub_ref[:, js] = col_sum(dz.astype(f32))
    dx_ref[...] += dot(dz_ref[...], wu_ref[...], NT)


def attn_bwd_block(da_ref, wa_ref, qkv_ref, a_ref, dc_ref, dqkv_ref, dx_ref, qb_ref, nch, L):
    dc_ref[...] = dot(da_ref[...], wa_ref[:, 3 * HB:4 * HB]).astype(bf16)
    for c in range(nch):
        rs = slice(c * L, (c + 1) * L)
        qkv = qkv_ref[rs, :]
        dc = dc_ref[rs, :]

        def head(t, i):
            return qkv[:, t * HB + i * HS:t * HB + (i + 1) * HS]
        dcs = [dc[:, i * HS:(i + 1) * HS] for i in range(HPB)]
        probs = [a_ref[c, i] for i in range(HPB)]
        drs = [dot(dcs[i], head(2, i), NT) for i in range(HPB)]
        dss = []
        for i in range(HPB):
            af = probs[i].astype(f32)
            t = af * drs[i]
            dss.append(((t - af * jnp.sum(t, axis=-1, keepdims=True)) * (HS ** -0.5)).astype(bf16))
        dqs = [dot(dss[i], head(1, i)) for i in range(HPB)]
        dks = [dot(dss[i], head(0, i), TN) for i in range(HPB)]
        dvs = [dot(probs[i], dcs[i], TN) for i in range(HPB)]
        dqkv_ref[rs, :] = jnp.concatenate(dqs + dks + dvs, axis=1).astype(bf16)
    dx_ref[...] += dot(dqkv_ref[...], wa_ref[:, 0:3 * HB], NT)
    qb_ref[:, 0:3 * HB] = col_sum(dqkv_ref[...].astype(f32))
HALF = 384


def k1_kernel(nch, L,
              wa_in, wu_in, wd_in, sp_in, x_in, kb_ref, live_ref,
              w_out, sp_out, qkv_out, a_out, c_out, u_out, inv_out, g_out, gp_out, y_out, rms_out,
              wv, spv, xb, qkv, a, c, u, inv, g, gp, nlow, acc, rms, rmsv,
              recv, send, sp_recv, sp_send, loc, wsave, ssave, go):
    M = nch * L
    s = lax.axis_index("section")
    t = lax.axis_index("tensor")
    xn = {"tensor": t + 1 - 2 * lax.rem(t, 2)}
    yn = {"tensor": t + 2 - 4 * lax.rem(t // 2, 2)}
    sib = {"section": 1 - s}
    srcs = (wa_in, wu_in, wd_in)

    def remote(src, dst, ss, rs, dev):
        return pltpu.make_async_remote_copy(src_ref=src, dst_ref=dst, send_sem=ss, recv_sem=rs, device_id=dev, device_id_type=MESH)

    def part(l, k, p):
        if p < 3:
            return wv.at[l, k, p]
        return wv.at[l, k, 3, pl.ds((p - 3) * HALF, HALF)]

    def wait_part(l, k, p):
        ref = part(l, k, p)
        pltpu.make_async_copy(ref, ref, recv.at[l, k, p]).wait()

    def own_sends(l, k):
        return [remote(srcs[k], wv.at[l, k, 1], send.at[k, 0], recv.at[l, k, 1], xn),
                remote(srcs[k], wv.at[l, k, 2], send.at[k, 1], recv.at[l, k, 2], yn)]
    def own_local(l, k):
        return [remote(srcs[k], wv.at[l, k, 0], send.at[k, 4], recv.at[l, k, 0], sib)]
    def fwd_y(l, k):
        return remote(wv.at[l, k, 1, pl.ds(0, HALF)], wv.at[l, k, 3, pl.ds(0, HALF)], send.at[k, 2], recv.at[l, k, 3], yn)
    def fwd_x(l, k):
        return remote(wv.at[l, k, 2, pl.ds(HALF, HALF)], wv.at[l, k, 3, pl.ds(HALF, HALF)], send.at[k, 3], recv.at[l, k, 4], xn)
    def to_sib(l, k, p):
        return remote(part(l, k, p), part(l, k, p), send.at[k, 4 + p], recv.at[l, k, p], sib)

    def save_w(l, k, p):
        dst = w_out.at[l, k, p] if p < 3 else w_out.at[l, k, 3, pl.ds((p - 3) * HALF, HALF)]
        return pltpu.make_async_copy(part(l, k, p), dst, wsave.at[l, k, p])

    def arrive(l, k, p):
        wait_part(l, k, p)
        @pl.when(s == l)
        def _():
            if p == 1:
                fwd_y(l, k).start()
            if p == 2:
                fwd_x(l, k).start()
            if p > 0:
                to_sib(l, k, p).start()
        save_w(l, k, p).start()

    def sp_wait(l, p):
        pltpu.make_async_copy(spv.at[l, p], spv.at[l, p], sp_recv.at[l, p]).wait()
    def sp_sends(l):
        return [remote(sp_in, spv.at[l, 1], sp_send.at[0], sp_recv.at[l, 1], xn),
                remote(sp_in, spv.at[l, 2], sp_send.at[1], sp_recv.at[l, 2], yn),
                remote(sp_in, spv.at[l, 0], sp_send.at[2], sp_recv.at[l, 0], sib)]
    def sp_fwd(l):
        return remote(spv.at[l, 1], spv.at[l, 3], sp_send.at[3], sp_recv.at[l, 3], yn)
    def sp_sib(l, p):
        return remote(spv.at[l, p], spv.at[l, p], sp_send.at[3 + p], sp_recv.at[l, p], sib)

    barrier = pltpu.get_barrier_semaphore()
    for dev in (xn, yn, sib):
        pl.semaphore_signal(barrier, inc=1, device_id=dev, device_id_type=MESH)
    pl.semaphore_wait(barrier, 3)

    for l in range(2):
        @pl.when(s == l)
        def _():
            for d in sp_sends(l):
                d.start()
            pltpu.make_async_copy(sp_in, spv.at[l, 0], sp_recv.at[l, 0]).start()
            if l == 0:
                for d in own_sends(l, KA):
                    d.start()
            for k in range(3):
                pltpu.make_async_copy(srcs[k], wv.at[l, k, 0], recv.at[l, k, 0]).start()
                for d in own_local(l, k):
                    d.start()
            if l == 0:
                for k in (KU, KD):
                    for d in own_sends(l, k):
                        d.start()
    xcopy = pltpu.make_async_copy(x_in, xb, loc.at[0])
    xcopy.start()
    for l in range(2):
        sp_wait(l, 0)
        sp_wait(l, 1)
        @pl.when(s == l)
        def _():
            sp_fwd(l).start()
            sp_sib(l, 1).start()
        sp_wait(l, 2)
        @pl.when(s == l)
        def _():
            sp_sib(l, 2).start()
        sp_wait(l, 3)
        @pl.when(s == l)
        def _():
            sp_sib(l, 3).start()
    xcopy.wait()
    spsave = pltpu.make_async_copy(spv, sp_out, loc.at[1])
    spsave.start()

    def saves(l, which):
        pairs = {0: (qkv, qkv_out.at[l]), 1: (a, a_out.at[l]), 2: (c, c_out.at[l]), 3: (u.at[0], u_out.at[l, 0]),
                 4: (inv, inv_out.at[l]), 5: (g, g_out.at[l]), 6: (gp, gp_out.at[l]), 7: (u.at[1], u_out.at[l, 1]), 8: (xb, y_out.at[l])}
        src, dst = pairs[which]
        return pltpu.make_async_copy(src, dst, ssave.at[which])

    def layer(l, _):
        acc[...] = jnp.zeros_like(acc)
        @pl.when(l == 1)
        def _():
            for w in (0, 1, 2):
                saves(0, w).wait()

        def attn_step(r, _):
            @pl.when(r == 0)
            def _():
                arrive(l, KA, 0)
            @pl.when(r == 1)
            def _():
                arrive(l, KA, 1)
                arrive(l, KA, 2)
            @pl.when(r == 3)
            def _():
                arrive(l, KU, 1)
                arrive(l, KU, 2)
                arrive(l, KA, 3)
                arrive(l, KA, 4)
            attn_fwd_block(xb, wv.at[l, KA, r], spv.at[l, r], kb_ref, qkv.at[r], a.at[r], c.at[r], acc, nch, L)
            return 0
        lax.fori_loop(0, 4, attn_step, 0)
        for w in (0, 1, 2):
            saves(l, w).start()
        @pl.when(l == 1)
        def _():
            for w in (3, 4, 5, 6, 7):
                saves(0, w).wait()
        ln1_fwd(xb, acc, spv.at[l, 0], u.at[0], inv.at[0], nlow, rms, M)
        saves(l, 3).start()

        def up_step(r, _):
            @pl.when(r == 0)
            def _():
                arrive(l, KU, 0)
            @pl.when(r == 3)
            def _():
                arrive(l, KD, 1)
                arrive(l, KD, 2)
                @pl.when((l == 0) & (s == 0))
                def _():
                    pl.semaphore_signal(go, inc=1, device_id=sib, device_id_type=MESH)
                @pl.when((l == 0) & (s == 1))
                def _():
                    pl.semaphore_wait(go, 1)
                    for k in range(3):
                        for d in own_sends(1, k):
                            d.start()
                arrive(l, KU, 3)
                arrive(l, KU, 4)
            up_block(nlow, wv.at[l, KU, r], spv.at[l, r], g.at[r], gp.at[r])
            return 0
        lax.fori_loop(0, 4, up_step, 0)
        saves(l, 5).start()
        saves(l, 6).start()
        acc[...] = jnp.zeros_like(acc)
        @pl.when(l == 1)
        def _():
            saves(0, 8).wait()

        def down_step(r, _):
            @pl.when(r == 0)
            def _():
                arrive(l, KD, 0)
            @pl.when(r == 3)
            def _():
                arrive(l, KD, 3)
                arrive(l, KD, 4)
            down_block(g.at[r], wv.at[l, KD, r], acc)
            return 0
        lax.fori_loop(0, 4, down_step, 0)
        ln2_fwd(u.at[0], acc, spv.at[l, 0], u.at[1], inv.at[1], xb, rms, M)
        for w in (4, 7, 8):
            saves(l, w).start()
        for k in range(3):
            for ch in range(nch):
                rs = slice(ch * L, (ch + 1) * L)
                v = jnp.sum(rms[k, rs, :] * live_ref[rs, :], axis=0, keepdims=True)
                rmsv[l, pl.ds(k * nch + ch, 1), :] = jnp.broadcast_to(v, (1, 128))
        return 0
    lax.fori_loop(0, 2, layer, 0)
    for w in range(9):
        saves(1, w).wait()
    rc = pltpu.make_async_copy(rmsv, rms_out, loc.at[0])
    rc.start()
    rc.wait()
    spsave.wait()
    for l in range(2):
        for k in range(3):
            for p in range(5):
                save_w(l, k, p).wait()
        @pl.when(s == l)
        def _():
            for k in range(3):
                for d in own_sends(l, k) + own_local(l, k) + [fwd_y(l, k), fwd_x(l, k)] + [to_sib(l, k, p) for p in range(1, 5)]:
                    d.wait_send()
            for d in sp_sends(l) + [sp_fwd(l)] + [sp_sib(l, p) for p in range(1, 4)]:
                d.wait_send()

def run_k1(nch, L, wa, wu, wd, sp, x, kb, live):
    M = nch * L
    S = jax.ShapeDtypeStruct
    V = pltpu.VMEM
    any_ = pl.BlockSpec(memory_space=pl.ANY)
    vm = pl.BlockSpec(memory_space=pltpu.VMEM)
    outs = (S((2, 3, 4, D, 768), bf16), S((2, 4, 8, D), f32), S((2, 4, M, 3 * HB), bf16), S((2, 4, nch, 3, L, L), bf16), S((2, 4, M, HB), bf16),
            S((2, 2, M, D), f32), S((2, 2, M, 1), f32), S((2, 4, M, FB), bf16), S((2, 4, M, FB), f32), S((2, M, D), bf16), S((2, 16, 128), f32))
    DMA = pltpu.SemaphoreType.DMA
    return pl.pallas_call(
        functools.partial(k1_kernel, nch, L),
        out_shape=outs,
        in_specs=[any_] * 5 + [vm] * 2,
        out_specs=[any_] * len(outs),
        scratch_shapes=[V((2, 3, 4, D, 768), bf16), V((2, 4, 8, D), f32), V((M, D), bf16), V((4, M, 3 * HB), bf16), V((4, nch, 3, L, L), bf16), V((4, M, HB), bf16),
                        V((2, M, D), f32), V((2, M, 1), f32), V((4, M, FB), bf16), V((4, M, FB), f32), V((M, D), bf16), V((M, D), f32), V((3, M, 1), f32), V((2, 16, 128), f32),
                        DMA((2, 3, 5)), DMA((3, 9)), DMA((2, 4)), DMA((7,)), DMA((2,)), DMA((2, 3, 5)), DMA((9,)), pltpu.SemaphoreType.REGULAR],
        compiler_params=pltpu.CompilerParams(collective_id=0, has_side_effects=True, vmem_limit_bytes=62 << 20),
        name="gather_forward",
    )(wa, wu, wd, sp, x, kb, live)

NJ = 4


def k2_kernel(nch, L, n_dp, zin,
              w_in, sp_in, qkv_in, a_in, c_in, u_in, inv_in, g_in, gp_in, y_in, x_in, dy_in, rms_in,
              f_out, sm_out, lo_out, dh_out, rm_out,
              wd, wu, wa, gp, g, qkv, a, c, u, inv, xin, dyv, spv, dx, low, low2, dc, dqkv, xt, xt2,
              pbuf, dbuf, qbuf, xbuf, ybuf, zbuf, fbuf, sm, smr,
              st_g, st_f, st_a, ld, dsend, drecv, xsend, xrecv, ysend, yrecv, zsend, zrecv, fsend, frecv, fl, msend, mrecv, osend, orecv, ol,
              dcred, xcred, ycred):
    M = nch * L
    sub = D // (NJ * 4)
    s = lax.axis_index("section")
    t = lax.axis_index("tensor")
    j = lax.axis_index("dp")
    xn = {"tensor": t + 1 - 2 * lax.rem(t, 2)}
    yn = {"tensor": t + 2 - 4 * lax.rem(t // 2, 2)}
    sib = {"section": 1 - s}
    zn = [{"dp": lax.rem(j + d, n_dp)} for d in range(1, n_dp)] if zin else []

    def remote(src, dst, ss, rs, dev):
        return pltpu.make_async_remote_copy(src_ref=src, dst_ref=dst, send_sem=ss, recv_sem=rs, device_id=dev, device_id_type=MESH)

    def arrived(ref, sem):
        pltpu.make_async_copy(ref, ref, sem).wait()

    def where_of(m):
        li = m // 4
        return 1 - li, 3 - (m - 4 * li), lax.rem(m, 2)

    def g_copies(m):
        l, r, b = where_of(m)
        return [pltpu.make_async_copy(g_in.at[l, r], g.at[b], st_g.at[b])]

    def f_copies(m):
        l, r, b = where_of(m)
        return [pltpu.make_async_copy(w_in.at[l, KD, r], wd.at[b], st_f.at[b, 0]),
                pltpu.make_async_copy(w_in.at[l, KU, r], wu.at[b], st_f.at[b, 1]),
                pltpu.make_async_copy(gp_in.at[l, r], gp.at[b], st_f.at[b, 2])]

    def a_copies(m):
        l, r, b = where_of(m)
        return [pltpu.make_async_copy(w_in.at[l, KA, r], wa.at[b], st_a.at[b, 0]),
                pltpu.make_async_copy(qkv_in.at[l, r], qkv.at[b], st_a.at[b, 1]),
                pltpu.make_async_copy(a_in.at[l, r], a.at[b], st_a.at[b, 2]),
                pltpu.make_async_copy(c_in.at[l, r], c.at[b], st_a.at[b, 3])]

    def begin(copies):
        for d in copies:
            d.start()

    def finish(copies):
        for d in copies:
            d.wait()

    def u_copies(l, i):
        return [pltpu.make_async_copy(u_in.at[l, i], u.at[i], ld.at[2 * i]), pltpu.make_async_copy(inv_in.at[l, i], inv.at[i], ld.at[2 * i + 1])]

    def x_copy(src):
        return [pltpu.make_async_copy(src, xin, ld.at[4])]

    first = [pltpu.make_async_copy(dy_in, dyv, ld.at[5]), pltpu.make_async_copy(sp_in, spv, ld.at[6])]
    begin(first)
    begin(u_copies(1, 1))
    begin(g_copies(0))
    begin(u_copies(1, 0))
    begin(g_copies(1))
    begin(f_copies(0))
    begin(f_copies(1))
    begin(x_copy(y_in.at[0]))
    begin(a_copies(0))
    begin(a_copies(1))

    barrier = pltpu.get_barrier_semaphore()
    for dev in [xn, yn, sib] + zn:
        pl.semaphore_signal(barrier, inc=1, device_id=dev, device_id_type=MESH)
    pl.semaphore_wait(barrier, 3 + len(zn))

    def out_send(src, dst, i):
        return remote(src.at[1 - s], dst.at[s], osend.at[i], orecv.at[i], sib)

    def out_keep(src, dst, i):
        return pltpu.make_async_copy(src.at[s], dst.at[s], ol.at[i])
    for src, dst, i in ((y_in, lo_out, 0), (rms_in, rm_out, 1)):
        out_send(src, dst, i).start()
        out_keep(src, dst, i).start()

    def d_copy(r):
        return remote(pbuf.at[r, 1 - s], dbuf.at[r], dsend.at[r], drecv.at[r], sib)

    def put(n, r, parts):
        @pl.when(n > 0)
        def _():
            d_copy(r).wait_send()
        for k in range(NJ):
            for h in range(2):
                for ab in range(2):
                    lo = ((k * 2 + h) * 2 + ab) * sub
                    pbuf[r, h, ab, k] = parts[lo:lo + sub, :].astype(bf16)

        @pl.when(n > 0)
        def _():
            pl.semaphore_wait(dcred, 1)
        d_copy(r).start()

    def x_copies(n):
        b = lax.rem(n, 3)
        return [remote(qbuf.at[n, 0, 3], xbuf.at[b, 1], xsend.at[n, 1], xrecv.at[n, 1], xn),
                remote(qbuf.at[n, 1, 3], xbuf.at[b, 3], xsend.at[n, 3], xrecv.at[n, 3], yn),
                remote(qbuf.at[n, 1, 2], xbuf.at[b, 2], xsend.at[n, 2], xrecv.at[n, 2], yn),
                remote(qbuf.at[n, 0, 1], xbuf.at[b, 0], xsend.at[n, 0], xrecv.at[n, 0], xn)]

    def d_add(n, r):
        arrived(dbuf.at[r], drecv.at[r])

        def one(ab, _):
            qbuf[n, ab, r] = (pbuf[r, s, ab].astype(f32) + dbuf[r, ab].astype(f32)).astype(bf16)
            return 0
        lax.fori_loop(0, 2, one, 0)

        @pl.when(n < 5)
        def _():
            pl.semaphore_signal(dcred, inc=1, device_id=sib, device_id_type=MESH)
        cs = x_copies(n)

        @pl.when(r == 3)
        def _():
            @pl.when(n >= 3)
            def _():
                pl.semaphore_wait(xcred, 1)
                pl.semaphore_wait(ycred, 1)
            cs[0].start()
            cs[1].start()

        @pl.when(r == 2)
        def _():
            cs[2].start()

        @pl.when(r == 1)
        def _():
            cs[3].start()

    def slots(n, step):
        def body(ri, _):
            step(ri, 3 - ri)

            @pl.when(ri > 0)
            def _():
                d_add(n, 4 - ri)
            return 0
        lax.fori_loop(0, 4, body, 0)
        d_add(n, 0)

    def y_copies(n):
        return [remote(qbuf.at[n, 0, 2], ybuf.at[n, 0], ysend.at[n, 0], yrecv.at[n, 0], yn),
                remote(qbuf.at[n, 1, 1], ybuf.at[n, 1], ysend.at[n, 1], yrecv.at[n, 1], xn)]

    def add_to(n, ab, r, ref):
        qbuf[n, ab, r] = (qbuf[n, ab, r].astype(f32) + ref[...].astype(f32)).astype(bf16)

    def ev_x(n):
        b = lax.rem(n, 3)
        arrived(xbuf.at[b, 1], xrecv.at[n, 1])
        add_to(n, 0, 2, xbuf.at[b, 1])
        cs = y_copies(n)
        cs[0].start()
        arrived(xbuf.at[b, 3], xrecv.at[n, 3])
        add_to(n, 1, 1, xbuf.at[b, 3])
        cs[1].start()
        arrived(xbuf.at[b, 0], xrecv.at[n, 0])
        add_to(n, 0, 0, xbuf.at[b, 0])
        arrived(xbuf.at[b, 2], xrecv.at[n, 2])
        add_to(n, 1, 0, xbuf.at[b, 2])

        @pl.when(n < 3)
        def _():
            pl.semaphore_signal(xcred, inc=1, device_id=xn, device_id_type=MESH)
            pl.semaphore_signal(ycred, inc=1, device_id=yn, device_id_type=MESH)

    def z_copies(n):
        return [remote(qbuf.at[n, :, 0, lax.rem(j + d, n_dp)], zbuf.at[n, d - 1], zsend.at[n, d - 1], zrecv.at[n, d - 1], zn[d - 1]) for d in range(1, n_dp)]

    def q_copy(n):
        li = n // 3
        return pltpu.make_async_copy(qbuf.at[n, :, 0], f_out.at[1 - li, 2 - (n - 3 * li)], fl.at[n])

    def ev_y(n):
        for i in range(2):
            arrived(ybuf.at[n, i], yrecv.at[n, i])
            add_to(n, i, 0, ybuf.at[n, i])
        if zin:
            begin(z_copies(n))
        else:
            q_copy(n).start()

    def f_keep(n):
        return pltpu.make_async_copy(fbuf.at[n], f_out.at[2 - lax.rem(n, 3), s], fl.at[lax.rem(n, 3)])

    def f_send(n):
        return remote(fbuf.at[n], f_out.at[2 - lax.rem(n, 3), s], fsend.at[lax.rem(n, 3)], frecv.at[lax.rem(n, 3)], sib)

    def ev_z(n):
        if not zin:
            return
        tot = qbuf[n, :, 0, j].astype(f32)
        for d in range(n_dp - 1):
            arrived(zbuf.at[n, d], zrecv.at[n, d])
            tot = tot + zbuf[n, d].astype(f32)
        fbuf[n] = tot
        mine = (1 - n // 3) == s

        @pl.when(mine)
        def _():
            f_keep(n).start()

        @pl.when(jnp.logical_not(mine))
        def _():
            f_send(n).start()

    def m_copy(i):
        if i == 0:
            return remote(sm.at[1 - s], smr.at[0], msend.at[0], mrecv.at[0], sib)
        return remote(sm.at[s], smr.at[i], msend.at[i], mrecv.at[i], xn if i == 1 else yn)

    def m_z(d):
        return remote(sm.at[s], smr.at[2 + d], msend.at[2 + d], mrecv.at[2 + d], zn[d - 1])

    def m_add(i, flip):
        arrived(smr.at[i], mrecv.at[i])
        if i in (1, 2):
            m_copy(i).wait_send()
        sm[s, 0:8, :] += smr[i, 0:8, :]
        for r in range(4):
            for base in (8, 12):
                sm[s, base + r:base + r + 1, :] += smr[i, base + (r ^ flip):base + (r ^ flip) + 1, :]

    finish(first)
    sm[...] = jnp.zeros_like(sm)

    def layer(li, _):
        l = 1 - li
        n0 = 3 * li
        spl = spv.at[l, 0]
        sml = sm.at[l]
        finish(u_copies(l, 1))
        norm_bwd(dyv, u.at[1], inv.at[1], spl[6:7, :], dx, low, sml, 3, M)

        @pl.when(li == 0)
        def _():
            begin(u_copies(0, 1))
        xt[...] = low[...].T

        def down_step(ri, r):
            m = 4 * li + ri
            finish(g_copies(m))
            put(n0, r, dot(xt[...], g[lax.rem(m, 2)]))

            @pl.when(m + 2 < 8)
            def _():
                begin(g_copies(m + 2))
        slots(n0, down_step)

        @pl.when(li == 1)
        def _():
            ev_y(1)
        finish(u_copies(l, 0))
        low2[...] = (u[0] * spl[3:4, :] + spl[4:5, :]).astype(bf16)
        xt[...] = low2[...].T

        def up_step(ri, r):
            m = 4 * li + ri
            b = lax.rem(m, 2)
            finish(f_copies(m))
            ffn_bwd_block(low, wu.at[b], wd.at[b], gp.at[b], low2, dx, sml.at[pl.ds(8 + r, 1)])
            put(n0 + 1, r, dot(xt[...], low2[...]))

            @pl.when(m + 2 < 8)
            def _():
                begin(f_copies(m + 2))
        slots(n0 + 1, up_step)

        @pl.when(li == 1)
        def _():
            ev_x(2)
            ev_z(0)
        norm_bwd(dx, u.at[0], inv.at[0], spl[3:4, :], dx, low, sml, 0, M)

        @pl.when(li == 0)
        def _():
            begin(u_copies(0, 0))
        xt2[...] = low[...].T
        finish(x_copy(x_in))
        xt[...] = xin[...].T

        @pl.when(li == 0)
        def _():
            begin(x_copy(x_in))

        def attn_step(ri, r):
            m = 4 * li + ri
            b = lax.rem(m, 2)
            finish(a_copies(m))
            attn_bwd_block(low, wa.at[b], qkv.at[b], a.at[b], dc, dqkv, dx, sml.at[pl.ds(12 + r, 1)], nch, L)
            put(n0 + 2, r, jnp.concatenate([dot(xt[...], dqkv[...]), dot(xt2[...], c[b])], axis=1))

            @pl.when(m + 2 < 8)
            def _():
                begin(a_copies(m + 2))

            @pl.when((li == 0) & (ri == 1))
            def _():
                ev_x(0)

            @pl.when((li == 0) & (ri == 3))
            def _():
                ev_x(1)
                ev_y(0)

            @pl.when((li == 1) & (ri == 3))
            def _():
                ev_x(3)
        slots(n0 + 2, attn_step)
        dyv[...] = dx[...].astype(bf16)
        own = l == s

        @pl.when(own)
        def _():
            dh_keep().start()

        @pl.when(jnp.logical_not(own))
        def _():
            dh_send().start()

        @pl.when(own & (li == 0))
        def _():
            dh_keep().wait()

        @pl.when(jnp.logical_not(own) & (li == 0))
        def _():
            dh_send().wait_send()
        return 0

    def dh_keep():
        return pltpu.make_async_copy(dyv, dh_out.at[s], ol.at[2])

    def dh_send():
        return remote(dyv, dh_out.at[s], osend.at[2], orecv.at[2], sib)

    lax.fori_loop(0, 2, layer, 0)

    m_copy(0).start()
    ev_y(2)
    m_add(0, 0)
    m_copy(1).start()
    ev_z(1)
    ev_x(4)
    m_add(1, 1)
    m_copy(2).start()
    ev_y(3)
    ev_z(2)
    m_add(2, 2)
    if zin:
        for d in range(1, n_dp):
            m_z(d).start()
    ev_x(5)
    ev_y(4)
    ev_z(3)
    ev_y(5)
    ev_z(4)
    if zin:
        for d in range(1, n_dp):
            m_z(d).wait_send()
        for d in range(1, n_dp):
            m_add(2 + d, 0)
    smc = pltpu.make_async_copy(sm.at[s], sm_out, ld.at[5])
    smc.start()
    ev_z(5)

    smc.wait()
    m_copy(0).wait_send()
    for r in range(4):
        d_copy(r).wait_send()
    for n in range(6):
        for d in x_copies(n) + y_copies(n):
            d.wait_send()
        if zin:
            for d in z_copies(n):
                d.wait_send()
        else:
            q_copy(n).wait()
    for src, dst, i in ((y_in, lo_out, 0), (rms_in, rm_out, 1)):
        out_send(src, dst, i).wait()
        out_keep(src, dst, i).wait()
    @pl.when(s == 0)
    def _():
        dh_keep().wait()
    @pl.when(s == 1)
    def _():
        dh_send().wait_send()
    arrived(dh_out.at[1 - s], orecv.at[2])
    if zin:
        for k in range(3):
            arrived(f_out.at[2 - k, 1 - s], frecv.at[k])
            f_keep(k).wait()
            f_send(k).wait_send()


def run_k2(nch, L, n_dp, *ops):
    M = nch * L
    zin = n_dp == 4
    sub = D // (NJ * 4)
    S = jax.ShapeDtypeStruct
    V = pltpu.VMEM
    any_ = pl.BlockSpec(memory_space=pl.ANY)
    outs = (S((3, 2, 2, sub, 768), f32) if zin else S((2, 3, 2, NJ, sub, 768), bf16), S((16, 768), f32), S((2, M, D), bf16), S((2, M, D), bf16), S((2, 16, 128), f32))
    DMA = pltpu.SemaphoreType.DMA
    REG = pltpu.SemaphoreType.REGULAR
    bufs = [V((2, D, 768), bf16), V((2, D, 768), bf16), V((2, D, 768), bf16), V((2, M, FB), f32), V((2, M, FB), bf16), V((2, M, 3 * HB), bf16), V((2, nch, HPB, L, L), bf16), V((2, M, HB), bf16),
            V((2, M, D), f32), V((2, M, 1), f32), V((M, D), bf16), V((M, D), bf16), V((2, 4, 8, D), f32), V((M, D), f32), V((M, D), bf16), V((M, D), bf16), V((M, HB), bf16), V((M, 3 * HB), bf16), V((D, M), bf16), V((D, M), bf16),
            V((4, 2, 2, NJ, sub, 768), bf16), V((4, 2, NJ, sub, 768), bf16), V((6, 2, 4, NJ, sub, 768), bf16), V((3, 4, NJ, sub, 768), bf16), V((6, 2, NJ, sub, 768), bf16),
            V((6, 3, 2, sub, 768) if zin else (8, 128), bf16), V((6, 2, sub, 768) if zin else (8, 128), f32), V((2, 16, 768), f32), V((6, 16, 768), f32)]
    sems = [DMA((2,)), DMA((2, 3)), DMA((2, 4)), DMA((7,)), DMA((4,)), DMA((4,)), DMA((6, 4)), DMA((6, 4)), DMA((6, 2)), DMA((6, 2)), DMA((6, 3)), DMA((6, 3)), DMA((3,)), DMA((3,)), DMA((6,)), DMA((6,)), DMA((6,)),
            DMA((3,)), DMA((3,)), DMA((3,)), REG, REG, REG]
    return pl.pallas_call(
        functools.partial(k2_kernel, nch, L, n_dp, zin),
        out_shape=outs,
        in_specs=[any_] * 13,
        out_specs=[any_] * len(outs),
        scratch_shapes=bufs + sems,
        compiler_params=pltpu.CompilerParams(collective_id=1, has_side_effects=True, vmem_limit_bytes=63 << 20),
        name="backward_reduce",
    )(*ops)

def on_device(inputs, lengths, cotangent, w_qkv, qv_bias, w_out, out_bias, ln1_gain, ln1_bias, w_up, up_bias, w_down, down_bias, ln2_gain, ln2_bias):
    s = lax.axis_index("section")
    t = lax.axis_index("tensor")
    j = lax.axis_index("dp")
    n_dp = lax.axis_size("dp")
    chains, L, _ = inputs.shape
    nch = chains // 2
    M = nch * L
    wa = jnp.concatenate([w_qkv[0, 0], w_qkv[0, 1], w_qkv[0, 2], w_out[0].T], axis=1)
    z = jnp.zeros((HB,), f32)
    sp = jnp.stack([up_bias[0].reshape(-1), jnp.concatenate([qv_bias[0, 0].reshape(-1), z, qv_bias[0, 1].reshape(-1), z]),
                    out_bias[0], ln1_gain[0], ln1_bias[0], down_bias[0], ln2_gain[0], ln2_bias[0]])
    x = lax.dynamic_slice_in_dim(inputs, s * nch, nch, 0).reshape(M, D)
    dy = lax.dynamic_slice_in_dim(cotangent, s * nch, nch, 0).reshape(M, D)
    own_len = lax.dynamic_slice_in_dim(lengths, t * chains, chains, 0)
    my_len = lax.dynamic_slice_in_dim(own_len, s * nch, nch, 0)
    alive = jnp.arange(L)[None] < my_len[:, None]
    kb = jnp.where(alive, 0.0, MASK_FILL).astype(f32)
    live = alive.astype(f32).reshape(M, 1)
    w_all, sp_all, qkv, a, c, u, inv, g, gp, y, rms = run_k1(nch, L, wa, w_up[0], w_down[0], sp, x, kb, live)
    grads, sm, lo, dh, rm = run_k2(nch, L, n_dp, w_all, sp_all, qkv, a, c, u, inv, g, gp, y, x, dy, rms)
    if n_dp == 4:
        grads = grads.reshape(3, D // n_dp, 768)
    else:
        mine = grads[s].astype(f32)
        got = lax.ppermute(grads[1 - s], "section", [(0, 1), (1, 0)]).astype(f32)
        both = jnp.stack([jnp.where(s == 0, mine, got), jnp.where(s == 0, got, mine)])
        both = both.transpose(1, 3, 0, 2, 4, 5).reshape(3, D, 768)
        grads = lax.psum_scatter(both, "dp", scatter_dimension=1, tiled=True)
        sm = lax.psum(sm, "dp")
    ga, gu, gd = grads[0], grads[1], grads[2]
    dd = D // n_dp
    part = HS // n_dp
    share = D // (n_dp * 4)
    vec = lax.dynamic_slice_in_dim(sm[:6], (j * 4 + t) * share, share, 1)
    ub = lax.dynamic_slice_in_dim(sm[8].reshape(FB // HS, HS), j * part, part, 1)
    qb = lax.dynamic_slice_in_dim(sm[12, :3 * HB].reshape(3, HPB, HS), j * part, part, 2)[0::2]
    sums = rm[:, :3 * nch, 0].reshape(2, 3, nch).transpose(1, 0, 2).reshape(3, chains) / own_len.astype(f32)
    gq = ga[:, :3 * HB].reshape(dd, 3, HB).transpose(1, 0, 2)
    return (lo.reshape(1, chains, L, D), dh.reshape(1, chains, L, D), gq[None], qb[None], ga[:, 3 * HB:].T[None], gu[None], ub[None], gd.T[None], vec[None], sums[None])


def solution(mesh):
    in_specs = (
        P(("dp", "tensor"), None, None),
        P("dp"),
        P(("dp", "tensor"), None, None),
        P("section", None, None, "tensor"),
        P("section", None, "tensor", None),
        P("section", "tensor", None),
        P("section", None),
        P("section", None),
        P("section", None),
        P("section", None, "tensor"),
        P("section", "tensor", None),
        P("section", "tensor", None),
        P("section", None),
        P("section", None),
        P("section", None),
    )
    out_specs = (
        P("section", ("dp", "tensor"), None, None),
        P("section", ("dp", "tensor"), None, None),
        P("section", None, "dp", "tensor"),
        P("section", None, "tensor", "dp"),
        P("section", "tensor", "dp"),
        P("section", "dp", "tensor"),
        P("section", "tensor", "dp"),
        P("section", "tensor", "dp"),
        P("section", None, ("dp", "tensor")),
        P("section", None, ("dp", "tensor")),
    )
    return jax.shard_map(on_device, mesh=mesh, in_specs=in_specs, out_specs=out_specs, check_vma=False)
```

```python
import functools

import jax
import jax.numpy as jnp
from jax import lax
from jax.experimental import pallas as pl
from jax.experimental.pallas import tpu as pltpu
from jax.sharding import PartitionSpec as P


f32, bf16 = jnp.float32, jnp.bfloat16
D, FB, HB, HS = 768, 768, 192, 64
NT = (((1,), (1,)), ((), ()))
NN = (((1,), (0,)), ((), ()))
TN = (((0,), (0,)), ((), ()))
EPS_NORM, EPS_ROOT = 1e-12, 1e-6
MASK_FILL = -1e9
ROOT_HALF, INV_ROOT_TWO_PI = 0.7071067811865476, 0.3989422804014327
MESH = pl.DeviceIdType.MESH
KA, KU, KD = 0, 1, 2
HPB = HB // HS


def dot(a, b, dims=NN):
    return lax.dot_general(a, b, dims, preferred_element_type=f32)


def rows(i, n):
    return pl.ds(pl.multiple_of(i * n, n), n)


def mean_last(v):
    return jnp.mean(v, axis=-1, keepdims=True)


def rms_rows(v):
    return jnp.sqrt(mean_last(v * v) + EPS_ROOT)


def norm_step(x, gain, bias):
    c = x - mean_last(x)
    inv = lax.rsqrt(mean_last(c * c) + EPS_NORM)
    u = c * inv
    return u * gain + bias, u, inv


def norm_back(dn, u, inv, gain):
    du = dn * gain
    return inv * (du - mean_last(du) - u * mean_last(du * u))


def part8(v):
    t = v[0:8]
    for i in range(1, v.shape[0] // 8):
        t = t + v[8 * i:8 * (i + 1)]
    return t


def col_sum(v):
    return jnp.sum(part8(v), axis=0, keepdims=True)


def row_block(M):
    for n in (96, 80, 64, 48, 32, 16):
        if M % n == 0:
            return n
    return M


def attn_fwd_block(x_ref, wa_ref, sp_ref, kb_ref, qkv_ref, a_ref, c_ref, acc_ref, nch, L):
    qkv_ref[...] = (dot(x_ref[...], wa_ref[:, 0:3 * HB]) + sp_ref[1:2, 0:3 * HB]).astype(bf16)
    for c in range(nch):
        rs = slice(c * L, (c + 1) * L)
        qkv = qkv_ref[rs, :]
        kb = kb_ref[c:c + 1, :]

        def head(t, i):
            return qkv[:, t * HB + i * HS:t * HB + (i + 1) * HS]
        scores = [dot(head(0, i), head(1, i), NT) * (HS ** -0.5) + kb for i in range(HPB)]
        probs = []
        for i in range(HPB):
            e = jnp.exp(scores[i] - jnp.max(scores[i], axis=-1, keepdims=True))
            a = (e / jnp.sum(e, axis=-1, keepdims=True)).astype(bf16)
            a_ref[c, i] = a
            probs.append(a)
        c_ref[rs, :] = jnp.concatenate([dot(probs[i], head(2, i)).astype(bf16) for i in range(HPB)], axis=1)
    acc_ref[...] += dot(c_ref[...], wa_ref[:, 3 * HB:4 * HB], NT)


def ln1_fwd(x_ref, acc_ref, sp_ref, u_ref, inv_ref, nlow_ref, rms_ref, M):
    rb = M // 3 if M % 48 == 0 else M

    def body(i, _):
        rs = rows(i, rb)
        h = x_ref[rs, :].astype(f32)
        att = acc_ref[rs, :] + sp_ref[2:3, :]
        n, u, inv = norm_step(h + att, sp_ref[3:4, :], sp_ref[4:5, :])
        u_ref[rs, :] = u
        inv_ref[rs, :] = inv
        nlow_ref[rs, :] = n.astype(bf16)
        rms_ref[0, rs, :] = rms_rows(h)
        rms_ref[1, rs, :] = rms_rows(att)
        return 0
    lax.fori_loop(0, M // rb, body, 0)


def up_block(nlow_ref, wu_ref, sp_ref, g_ref, gp_ref):
    for j in range(FB // 256):
        js = slice(256 * j, 256 * (j + 1))
        z = dot(nlow_ref[...], wu_ref[:, js]) + sp_ref[0:1, js]
        cdf = 0.5 * (1.0 + lax.erf(z * ROOT_HALF))
        g_ref[:, js] = (z * cdf).astype(bf16)
        gp_ref[:, js] = cdf + z * (INV_ROOT_TWO_PI * jnp.exp(-0.5 * z * z))


def down_block(g_ref, wd_ref, acc_ref):
    acc_ref[...] += dot(g_ref[...], wd_ref[...])


def ln2_fwd(u1_ref, acc_ref, sp_ref, u_ref, inv_ref, y_ref, rms_ref, M):
    rb = M // 3 if M % 48 == 0 else M

    def body(i, _):
        rs = rows(i, rb)
        n = u1_ref[rs, :] * sp_ref[3:4, :] + sp_ref[4:5, :]
        ffn = acc_ref[rs, :] + sp_ref[5:6, :]
        y, u, inv = norm_step(n + ffn, sp_ref[6:7, :], sp_ref[7:8, :])
        u_ref[rs, :] = u
        inv_ref[rs, :] = inv
        y_ref[rs, :] = y.astype(bf16)
        rms_ref[2, rs, :] = rms_rows(ffn)
        return 0
    lax.fori_loop(0, M // rb, body, 0)


def norm_bwd(dy_ref, u_ref, inv_ref, gain, dx_ref, low_ref, sm_ref, row, M):
    rb = row_block(M)

    def body(i, carry):
        a, b, c = carry
        rs = rows(i, rb)
        dy = dy_ref[rs, :].astype(f32)
        u = u_ref[rs, :]
        dx = norm_back(dy, u, inv_ref[rs, :], gain)
        dx_ref[rs, :] = dx
        low_ref[rs, :] = dx.astype(bf16)
        return (a + part8(dx), b + part8(dy * u), c + part8(dy))
    z = jnp.zeros((8, D), f32)
    sums = lax.fori_loop(0, M // rb, body, (z, z, z))
    for k in range(3):
        sm_ref[row + k:row + k + 1, :] = jnp.sum(sums[k], axis=0, keepdims=True)


def ffn_bwd_block(df_ref, wu_ref, wd_ref, gp_ref, dz_ref, dx_ref, ub_ref):
    for j in range(FB // 256):
        js = slice(256 * j, 256 * (j + 1))
        dz = (dot(df_ref[...], wd_ref[js, :], NT) * gp_ref[:, js]).astype(bf16)
        dz_ref[:, js] = dz
        ub_ref[:, js] = col_sum(dz.astype(f32))
    dx_ref[...] += dot(dz_ref[...], wu_ref[...], NT)


def attn_bwd_block(da_ref, wa_ref, qkv_ref, a_ref, dc_ref, dqkv_ref, dx_ref, qb_ref, nch, L):
    dc_ref[...] = dot(da_ref[...], wa_ref[:, 3 * HB:4 * HB]).astype(bf16)
    for c in range(nch):
        rs = slice(c * L, (c + 1) * L)
        qkv = qkv_ref[rs, :]
        dc = dc_ref[rs, :]

        def head(t, i):
            return qkv[:, t * HB + i * HS:t * HB + (i + 1) * HS]
        dcs = [dc[:, i * HS:(i + 1) * HS] for i in range(HPB)]
        probs = [a_ref[c, i] for i in range(HPB)]
        drs = [dot(dcs[i], head(2, i), NT) for i in range(HPB)]
        dss = []
        for i in range(HPB):
            af = probs[i].astype(f32)
            t = af * drs[i]
            dss.append(((t - af * jnp.sum(t, axis=-1, keepdims=True)) * (HS ** -0.5)).astype(bf16))
        dqs = [dot(dss[i], head(1, i)) for i in range(HPB)]
        dks = [dot(dss[i], head(0, i), TN) for i in range(HPB)]
        dvs = [dot(probs[i], dcs[i], TN) for i in range(HPB)]
        dqkv_ref[rs, :] = jnp.concatenate(dqs + dks + dvs, axis=1).astype(bf16)
    dx_ref[...] += dot(dqkv_ref[...], wa_ref[:, 0:3 * HB], NT)
    qb_ref[:, 0:3 * HB] = col_sum(dqkv_ref[...].astype(f32))
ZR = 224
XY = D - ZR


def k1_kernel(nch, L,
              wa_in, wu_in, wd_in, sp_in, x_in, kb_ref, live_ref,
              w_out, sp_out, qkv_out, a_out, c_out, u_out, inv_out, g_out, gp_out, y_out, rms_out,
              wv, spv, xb, qkv, a, c, u, inv, g, gp, nlow, acc, rms, rmsv,
              recv, send, sp_recv, sp_send, loc, wsave, ssave, go):
    M = nch * L
    s = lax.axis_index("section")
    t = lax.axis_index("tensor")
    xn = {"tensor": t + 1 - 2 * lax.rem(t, 2)}
    yn = {"tensor": t + 2 - 4 * lax.rem(t // 2, 2)}
    j = lax.axis_index("dp")
    sib = {"section": 1 - s}
    zn = {"dp": j + 1 - 2 * lax.rem(j, 2)}
    diag = {"tensor": 3 - t}
    e = lax.rem(j, 2)
    srcs = (wa_in, wu_in, wd_in)

    def remote(src, dst, ss, rs, dev):
        return pltpu.make_async_remote_copy(src_ref=src, dst_ref=dst, send_sem=ss, recv_sem=rs, device_id=dev, device_id_type=MESH)

    def span(start, n):
        return pl.ds(pl.multiple_of(start, 16), n)
    fetched = span(e * ZR, XY)
    half = [span(e * ZR + i * (XY // 2), XY // 2) for i in range(2)]
    given = span(e * XY, ZR)
    taken = span((1 - e) * XY, ZR)

    def view(ref, p):
        if p == 0:
            return ref.at[0]
        if p in (1, 2):
            return ref.at[p, fetched]
        if p in (3, 4):
            return ref.at[3, half[p - 3]]
        return ref.at[p - 4, taken]

    def part(l, k, p):
        return view(wv.at[l, k], p)

    def wait_part(l, k, p):
        ref = part(l, k, p)
        pltpu.make_async_copy(ref, ref, recv.at[l, k, p]).wait()

    def own_sends(l, k):
        return [remote(srcs[k].at[fetched], wv.at[l, k, 1, fetched], send.at[k, 0], recv.at[l, k, 1], xn),
                remote(srcs[k].at[fetched], wv.at[l, k, 2, fetched], send.at[k, 1], recv.at[l, k, 2], yn)]

    def own_local(l, k):
        return remote(srcs[k], wv.at[l, k, 0], send.at[k, 7], recv.at[l, k, 0], sib)

    def fwd_y(l, k):
        return remote(wv.at[l, k, 1, half[0]], wv.at[l, k, 3, half[0]], send.at[k, 2], recv.at[l, k, 3], yn)

    def fwd_x(l, k):
        return remote(wv.at[l, k, 2, half[1]], wv.at[l, k, 3, half[1]], send.at[k, 3], recv.at[l, k, 4], xn)

    def to_z(l, k, slot):
        ref = wv.at[l, k, slot, given]
        return remote(ref, ref, send.at[k, 3 + slot], recv.at[l, k, 4 + slot], zn)

    def to_sib(l, k, p):
        return remote(part(l, k, p), part(l, k, p), send.at[k, 7 + p], recv.at[l, k, p], sib)

    def save_w(l, k, p):
        return pltpu.make_async_copy(part(l, k, p), view(w_out.at[l, k], p), wsave.at[l, k, p])

    def arrive(l, k, p):
        wait_part(l, k, p)

        @pl.when(s == l)
        def _():
            if p == 1:
                fwd_y(l, k).start()
                to_z(l, k, 1).start()
            if p == 2:
                fwd_x(l, k).start()
                to_z(l, k, 2).start()
                if k == KA:
                    for d in own_sends(l, KD):
                        d.start()
            if p in (3, 4):
                @pl.when(e == p - 3)
                def _():
                    to_z(l, k, 3).start()
            if p > 0:
                to_sib(l, k, p).start()
        save_w(l, k, p).start()

    others = [(q, {"section": sec, "tensor": dev["tensor"]}) for q, dev in ((1, xn), (2, yn), (3, diag)) for sec in (s, 1 - s)] + [(0, sib)]

    def sp_sends(l):
        return [remote(sp_in, spv.at[l, q], sp_send.at[i], sp_recv.at[l, q], dev) for i, (q, dev) in enumerate(others)]

    def sp_wait(l):
        for q in range(4):
            pltpu.make_async_copy(spv.at[l, q], spv.at[l, q], sp_recv.at[l, q]).wait()

    barrier = pltpu.get_barrier_semaphore()
    for dev in [zn] + [dev for q, dev in others]:
        pl.semaphore_signal(barrier, inc=1, device_id=dev, device_id_type=MESH)
    pl.semaphore_wait(barrier, 1 + len(others))

    for l in range(2):
        @pl.when(s == l)
        def _():
            for d in sp_sends(l):
                d.start()
            pltpu.make_async_copy(sp_in, spv.at[l, 0], sp_recv.at[l, 0]).start()
            if l == 0:
                for k in (KA, KU):
                    for d in own_sends(l, k):
                        d.start()
            for k in range(3):
                pltpu.make_async_copy(srcs[k], wv.at[l, k, 0], recv.at[l, k, 0]).start()
                own_local(l, k).start()
    xcopy = pltpu.make_async_copy(x_in, xb, loc.at[0])
    xcopy.start()
    for l in range(2):
        sp_wait(l)
    xcopy.wait()
    spsave = pltpu.make_async_copy(spv, sp_out, loc.at[1])
    spsave.start()

    def saves(l, which):
        pairs = {0: (qkv, qkv_out.at[l]), 1: (a, a_out.at[l]), 2: (c, c_out.at[l]), 3: (u.at[0], u_out.at[l, 0]),
                 4: (inv, inv_out.at[l]), 5: (g, g_out.at[l]), 6: (gp, gp_out.at[l]), 7: (u.at[1], u_out.at[l, 1]), 8: (xb, y_out.at[l])}
        src, dst = pairs[which]
        return pltpu.make_async_copy(src, dst, ssave.at[which])

    def layer(l, _):
        acc[...] = jnp.zeros_like(acc)
        @pl.when(l == 1)
        def _():
            for w in (0, 1, 2):
                saves(0, w).wait()

        def attn_step(r, _):
            @pl.when(r == 0)
            def _():
                arrive(l, KA, 0)
            @pl.when(r == 1)
            def _():
                @pl.when(l == 0)
                def _():
                    arrive(0, KA, 1)
                    arrive(0, KA, 2)
                for k, p in ((KU, 1), (KU, 2), (KA, 5), (KA, 6)):
                    arrive(l, k, p)

            @pl.when(r == 3)
            def _():
                for k, p in ((KA, 3), (KA, 4), (KU, 5), (KU, 6), (KA, 7)):
                    arrive(l, k, p)
            attn_fwd_block(xb, wv.at[l, KA, r], spv.at[l, r], kb_ref, qkv.at[r], a.at[r], c.at[r], acc, nch, L)
            return 0
        lax.fori_loop(0, 4, attn_step, 0)
        arrive(l, KD, 1)
        arrive(l, KD, 2)

        @pl.when((l == 0) & (s == 0))
        def _():
            pl.semaphore_signal(go, inc=1, device_id=sib, device_id_type=MESH)

        @pl.when((l == 0) & (s == 1))
        def _():
            pl.semaphore_wait(go, 1)
            for k in (KA, KU):
                for d in own_sends(1, k):
                    d.start()
        for w in (0, 1, 2):
            saves(l, w).start()
        @pl.when(l == 1)
        def _():
            for w in (3, 4, 5, 6, 7):
                saves(0, w).wait()
        ln1_fwd(xb, acc, spv.at[l, 0], u.at[0], inv.at[0], nlow, rms, M)
        saves(l, 3).start()

        def up_step(r, _):
            @pl.when(r == 0)
            def _():
                arrive(l, KU, 0)

            @pl.when(r == 3)
            def _():
                for k, p in ((KU, 3), (KU, 4), (KD, 5), (KD, 6), (KD, 3), (KD, 4), (KU, 7)):
                    arrive(l, k, p)
            up_block(nlow, wv.at[l, KU, r], spv.at[l, r], g.at[r], gp.at[r])
            return 0
        lax.fori_loop(0, 4, up_step, 0)
        saves(l, 5).start()
        saves(l, 6).start()
        acc[...] = jnp.zeros_like(acc)
        @pl.when(l == 1)
        def _():
            saves(0, 8).wait()

        def down_step(r, _):
            @pl.when(r == 0)
            def _():
                arrive(l, KD, 0)

            @pl.when(r == 3)
            def _():
                arrive(l, KD, 7)

                @pl.when(l == 0)
                def _():
                    arrive(1, KA, 1)
                    arrive(1, KA, 2)
            down_block(g.at[r], wv.at[l, KD, r], acc)
            return 0
        lax.fori_loop(0, 4, down_step, 0)
        ln2_fwd(u.at[0], acc, spv.at[l, 0], u.at[1], inv.at[1], xb, rms, M)
        for w in (4, 7, 8):
            saves(l, w).start()
        for k in range(3):
            for ch in range(nch):
                rs = slice(ch * L, (ch + 1) * L)
                v = jnp.sum(rms[k, rs, :] * live_ref[rs, :], axis=0, keepdims=True)
                rmsv[l, pl.ds(k * nch + ch, 1), :] = jnp.broadcast_to(v, (1, 128))
        return 0
    lax.fori_loop(0, 2, layer, 0)
    for w in range(9):
        saves(1, w).wait()
    rc = pltpu.make_async_copy(rmsv, rms_out, loc.at[0])
    rc.start()
    rc.wait()
    spsave.wait()
    for l in range(2):
        for k in range(3):
            for p in range(8):
                save_w(l, k, p).wait()
        @pl.when(s == l)
        def _():
            for k in range(3):
                for d in own_sends(l, k) + [own_local(l, k), fwd_y(l, k), fwd_x(l, k)] + [to_z(l, k, q) for q in (1, 2, 3)] + [to_sib(l, k, p) for p in range(1, 8)]:
                    d.wait_send()
            for d in sp_sends(l):
                d.wait_send()


def run_k1(nch, L, wa, wu, wd, sp, x, kb, live):
    M = nch * L
    S = jax.ShapeDtypeStruct
    V = pltpu.VMEM
    any_ = pl.BlockSpec(memory_space=pl.ANY)
    vm = pl.BlockSpec(memory_space=pltpu.VMEM)
    outs = (S((2, 3, 4, D, 768), bf16), S((2, 4, 8, D), f32), S((2, 4, M, 3 * HB), bf16), S((2, 4, nch, 3, L, L), bf16), S((2, 4, M, HB), bf16),
            S((2, 2, M, D), f32), S((2, 2, M, 1), f32), S((2, 4, M, FB), bf16), S((2, 4, M, FB), f32), S((2, M, D), bf16), S((2, 16, 128), f32))
    DMA = pltpu.SemaphoreType.DMA
    return pl.pallas_call(
        functools.partial(k1_kernel, nch, L),
        out_shape=outs,
        in_specs=[any_] * 5 + [vm] * 2,
        out_specs=[any_] * len(outs),
        scratch_shapes=[V((2, 3, 4, D, 768), bf16), V((2, 4, 8, D), f32), V((M, D), bf16), V((4, M, 3 * HB), bf16), V((4, nch, 3, L, L), bf16), V((4, M, HB), bf16),
                        V((2, M, D), f32), V((2, M, 1), f32), V((4, M, FB), bf16), V((4, M, FB), f32), V((M, D), bf16), V((M, D), f32), V((3, M, 1), f32), V((2, 16, 128), f32),
                        DMA((2, 3, 8)), DMA((3, 15)), DMA((2, 4)), DMA((7,)), DMA((2,)), DMA((2, 3, 8)), DMA((9,)), pltpu.SemaphoreType.REGULAR],
        compiler_params=pltpu.CompilerParams(collective_id=0, has_side_effects=True, vmem_limit_bytes=62 << 20),
        name="gather_forward",
    )(wa, wu, wd, sp, x, kb, live)

NJ = 4


def k2_kernel(nch, L, n_dp, zin,
              w_in, sp_in, qkv_in, a_in, c_in, u_in, inv_in, g_in, gp_in, y_in, x_in, dy_in, rms_in,
              f_out, sm_out, lo_out, dh_out, rm_out,
              wd, wu, wa, gp, g, qkv, a, c, u, inv, xin, dyv, spv, dx, low, low2, dc, dqkv, xt, xt2,
              pbuf, dbuf, qbuf, xbuf, ybuf, zbuf, fbuf, sm, smr,
              st_g, st_f, st_a, ld, dsend, drecv, xsend, xrecv, ysend, yrecv, zsend, zrecv, fsend, frecv, fl, msend, mrecv, osend, orecv, ol,
              dcred, xcred, ycred):
    M = nch * L
    sub = D // (NJ * 4)
    s = lax.axis_index("section")
    t = lax.axis_index("tensor")
    j = lax.axis_index("dp")
    xn = {"tensor": t + 1 - 2 * lax.rem(t, 2)}
    yn = {"tensor": t + 2 - 4 * lax.rem(t // 2, 2)}
    sib = {"section": 1 - s}
    zn = [{"dp": lax.rem(j + d, n_dp)} for d in range(1, n_dp)] if zin else []

    def remote(src, dst, ss, rs, dev):
        return pltpu.make_async_remote_copy(src_ref=src, dst_ref=dst, send_sem=ss, recv_sem=rs, device_id=dev, device_id_type=MESH)

    def arrived(ref, sem):
        pltpu.make_async_copy(ref, ref, sem).wait()

    def where_of(m):
        li = m // 4
        return 1 - li, 3 - (m - 4 * li), lax.rem(m, 2)

    def g_copies(m):
        l, r, b = where_of(m)
        return [pltpu.make_async_copy(g_in.at[l, r], g.at[b], st_g.at[b])]

    def f_copies(m):
        l, r, b = where_of(m)
        return [pltpu.make_async_copy(w_in.at[l, KD, r], wd.at[b], st_f.at[b, 0]),
                pltpu.make_async_copy(w_in.at[l, KU, r], wu.at[b], st_f.at[b, 1]),
                pltpu.make_async_copy(gp_in.at[l, r], gp.at[b], st_f.at[b, 2])]

    def a_copies(m):
        l, r, b = where_of(m)
        return [pltpu.make_async_copy(w_in.at[l, KA, r], wa.at[b], st_a.at[b, 0]),
                pltpu.make_async_copy(qkv_in.at[l, r], qkv.at[b], st_a.at[b, 1]),
                pltpu.make_async_copy(a_in.at[l, r], a.at[b], st_a.at[b, 2]),
                pltpu.make_async_copy(c_in.at[l, r], c.at[b], st_a.at[b, 3])]

    def begin(copies):
        for d in copies:
            d.start()

    def finish(copies):
        for d in copies:
            d.wait()

    def u_copies(l, i):
        return [pltpu.make_async_copy(u_in.at[l, i], u.at[i], ld.at[2 * i]), pltpu.make_async_copy(inv_in.at[l, i], inv.at[i], ld.at[2 * i + 1])]

    def x_copy(src):
        return [pltpu.make_async_copy(src, xin, ld.at[4])]

    first = [pltpu.make_async_copy(dy_in, dyv, ld.at[5]), pltpu.make_async_copy(sp_in, spv, ld.at[6])]
    begin(first)
    begin(u_copies(1, 1))
    begin(g_copies(0))
    begin(u_copies(1, 0))
    begin(g_copies(1))
    begin(f_copies(0))
    begin(f_copies(1))
    begin(x_copy(y_in.at[0]))
    begin(a_copies(0))
    begin(a_copies(1))

    barrier = pltpu.get_barrier_semaphore()
    for dev in [xn, yn, sib] + zn:
        pl.semaphore_signal(barrier, inc=1, device_id=dev, device_id_type=MESH)
    pl.semaphore_wait(barrier, 3 + len(zn))

    def out_send(src, dst, i):
        return remote(src.at[1 - s], dst.at[s], osend.at[i], orecv.at[i], sib)

    def out_keep(src, dst, i):
        return pltpu.make_async_copy(src.at[s], dst.at[s], ol.at[i])
    for src, dst, i in ((y_in, lo_out, 0), (rms_in, rm_out, 1)):
        out_send(src, dst, i).start()
        out_keep(src, dst, i).start()

    def d_copy(r):
        return remote(pbuf.at[r, 1 - s], dbuf.at[r], dsend.at[r], drecv.at[r], sib)

    def put(n, r, parts):
        @pl.when(n > 0)
        def _():
            d_copy(r).wait_send()
        for k in range(NJ):
            for h in range(2):
                for ab in range(2):
                    lo = ((k * 2 + h) * 2 + ab) * sub
                    pbuf[r, h, ab, k] = parts[lo:lo + sub, :].astype(bf16)

        @pl.when(n > 0)
        def _():
            pl.semaphore_wait(dcred, 1)
        d_copy(r).start()

    def x_copies(n):
        b = lax.rem(n, 3)
        return [remote(qbuf.at[n, 0, 3], xbuf.at[b, 1], xsend.at[n, 1], xrecv.at[n, 1], xn),
                remote(qbuf.at[n, 1, 3], xbuf.at[b, 3], xsend.at[n, 3], xrecv.at[n, 3], yn),
                remote(qbuf.at[n, 1, 2], xbuf.at[b, 2], xsend.at[n, 2], xrecv.at[n, 2], yn),
                remote(qbuf.at[n, 0, 1], xbuf.at[b, 0], xsend.at[n, 0], xrecv.at[n, 0], xn)]

    def d_add(n, r):
        arrived(dbuf.at[r], drecv.at[r])

        def one(ab, _):
            qbuf[n, ab, r] = (pbuf[r, s, ab].astype(f32) + dbuf[r, ab].astype(f32)).astype(bf16)
            return 0
        lax.fori_loop(0, 2, one, 0)

        @pl.when(n < 5)
        def _():
            pl.semaphore_signal(dcred, inc=1, device_id=sib, device_id_type=MESH)
        cs = x_copies(n)

        @pl.when(r == 3)
        def _():
            @pl.when(n >= 3)
            def _():
                pl.semaphore_wait(xcred, 1)
                pl.semaphore_wait(ycred, 1)
            cs[0].start()
            cs[1].start()

        @pl.when(r == 2)
        def _():
            cs[2].start()

        @pl.when(r == 1)
        def _():
            cs[3].start()

    def slots(n, step):
        def body(ri, _):
            step(ri, 3 - ri)

            @pl.when(ri > 0)
            def _():
                d_add(n, 4 - ri)
            return 0
        lax.fori_loop(0, 4, body, 0)
        d_add(n, 0)

    def y_copies(n):
        return [remote(qbuf.at[n, 0, 2], ybuf.at[n, 0], ysend.at[n, 0], yrecv.at[n, 0], yn),
                remote(qbuf.at[n, 1, 1], ybuf.at[n, 1], ysend.at[n, 1], yrecv.at[n, 1], xn)]

    def add_to(n, ab, r, ref):
        qbuf[n, ab, r] = (qbuf[n, ab, r].astype(f32) + ref[...].astype(f32)).astype(bf16)

    def ev_x(n):
        b = lax.rem(n, 3)
        arrived(xbuf.at[b, 1], xrecv.at[n, 1])
        add_to(n, 0, 2, xbuf.at[b, 1])
        cs = y_copies(n)
        cs[0].start()
        arrived(xbuf.at[b, 3], xrecv.at[n, 3])
        add_to(n, 1, 1, xbuf.at[b, 3])
        cs[1].start()
        arrived(xbuf.at[b, 0], xrecv.at[n, 0])
        add_to(n, 0, 0, xbuf.at[b, 0])
        arrived(xbuf.at[b, 2], xrecv.at[n, 2])
        add_to(n, 1, 0, xbuf.at[b, 2])

        @pl.when(n < 3)
        def _():
            pl.semaphore_signal(xcred, inc=1, device_id=xn, device_id_type=MESH)
            pl.semaphore_signal(ycred, inc=1, device_id=yn, device_id_type=MESH)

    def z_copies(n):
        return [remote(qbuf.at[n, :, 0, lax.rem(j + d, n_dp)], zbuf.at[n, d - 1], zsend.at[n, d - 1], zrecv.at[n, d - 1], zn[d - 1]) for d in range(1, n_dp)]

    def q_copy(n):
        li = n // 3
        return pltpu.make_async_copy(qbuf.at[n, :, 0], f_out.at[1 - li, 2 - (n - 3 * li)], fl.at[n])

    def ev_y(n):
        for i in range(2):
            arrived(ybuf.at[n, i], yrecv.at[n, i])
            add_to(n, i, 0, ybuf.at[n, i])
        if zin:
            begin(z_copies(n))
        else:
            q_copy(n).start()

    def f_keep(n):
        return pltpu.make_async_copy(fbuf.at[n], f_out.at[2 - lax.rem(n, 3), s], fl.at[lax.rem(n, 3)])

    def f_send(n):
        return remote(fbuf.at[n], f_out.at[2 - lax.rem(n, 3), s], fsend.at[lax.rem(n, 3)], frecv.at[lax.rem(n, 3)], sib)

    def ev_z(n):
        if not zin:
            return
        tot = qbuf[n, :, 0, j].astype(f32)
        for d in range(n_dp - 1):
            arrived(zbuf.at[n, d], zrecv.at[n, d])
            tot = tot + zbuf[n, d].astype(f32)
        fbuf[n] = tot
        mine = (1 - n // 3) == s

        @pl.when(mine)
        def _():
            f_keep(n).start()

        @pl.when(jnp.logical_not(mine))
        def _():
            f_send(n).start()

    def m_copy(i):
        if i == 0:
            return remote(sm.at[1 - s], smr.at[0], msend.at[0], mrecv.at[0], sib)
        return remote(sm.at[s], smr.at[i], msend.at[i], mrecv.at[i], xn if i == 1 else yn)

    def m_z(d):
        return remote(sm.at[s], smr.at[2 + d], msend.at[2 + d], mrecv.at[2 + d], zn[d - 1])

    def m_add(i, flip):
        arrived(smr.at[i], mrecv.at[i])
        if i in (1, 2):
            m_copy(i).wait_send()
        sm[s, 0:8, :] += smr[i, 0:8, :]
        for r in range(4):
            for base in (8, 12):
                sm[s, base + r:base + r + 1, :] += smr[i, base + (r ^ flip):base + (r ^ flip) + 1, :]

    finish(first)
    sm[...] = jnp.zeros_like(sm)

    def layer(li, _):
        l = 1 - li
        n0 = 3 * li
        spl = spv.at[l, 0]
        sml = sm.at[l]
        finish(u_copies(l, 1))
        norm_bwd(dyv, u.at[1], inv.at[1], spl[6:7, :], dx, low, sml, 3, M)

        @pl.when(li == 0)
        def _():
            begin(u_copies(0, 1))
        xt[...] = low[...].T

        def down_step(ri, r):
            m = 4 * li + ri
            finish(g_copies(m))
            put(n0, r, dot(xt[...], g[lax.rem(m, 2)]))

            @pl.when(m + 2 < 8)
            def _():
                begin(g_copies(m + 2))
        slots(n0, down_step)

        @pl.when(li == 1)
        def _():
            ev_y(1)
        finish(u_copies(l, 0))
        low2[...] = (u[0] * spl[3:4, :] + spl[4:5, :]).astype(bf16)
        xt[...] = low2[...].T

        def up_step(ri, r):
            m = 4 * li + ri
            b = lax.rem(m, 2)
            finish(f_copies(m))
            ffn_bwd_block(low, wu.at[b], wd.at[b], gp.at[b], low2, dx, sml.at[pl.ds(8 + r, 1)])
            put(n0 + 1, r, dot(xt[...], low2[...]))

            @pl.when(m + 2 < 8)
            def _():
                begin(f_copies(m + 2))
        slots(n0 + 1, up_step)

        @pl.when(li == 1)
        def _():
            ev_x(2)
            ev_z(0)
        norm_bwd(dx, u.at[0], inv.at[0], spl[3:4, :], dx, low, sml, 0, M)

        @pl.when(li == 0)
        def _():
            begin(u_copies(0, 0))
        xt2[...] = low[...].T
        finish(x_copy(x_in))
        xt[...] = xin[...].T

        @pl.when(li == 0)
        def _():
            begin(x_copy(x_in))

        def attn_step(ri, r):
            m = 4 * li + ri
            b = lax.rem(m, 2)
            finish(a_copies(m))
            attn_bwd_block(low, wa.at[b], qkv.at[b], a.at[b], dc, dqkv, dx, sml.at[pl.ds(12 + r, 1)], nch, L)
            put(n0 + 2, r, jnp.concatenate([dot(xt[...], dqkv[...]), dot(xt2[...], c[b])], axis=1))

            @pl.when(m + 2 < 8)
            def _():
                begin(a_copies(m + 2))

            @pl.when((li == 0) & (ri == 1))
            def _():
                ev_x(0)

            @pl.when((li == 0) & (ri == 3))
            def _():
                ev_x(1)
                ev_y(0)

            @pl.when((li == 1) & (ri == 3))
            def _():
                ev_x(3)
        slots(n0 + 2, attn_step)
        dyv[...] = dx[...].astype(bf16)
        own = l == s

        @pl.when(own)
        def _():
            dh_keep().start()

        @pl.when(jnp.logical_not(own))
        def _():
            dh_send().start()

        @pl.when(own & (li == 0))
        def _():
            dh_keep().wait()

        @pl.when(jnp.logical_not(own) & (li == 0))
        def _():
            dh_send().wait_send()
        return 0

    def dh_keep():
        return pltpu.make_async_copy(dyv, dh_out.at[s], ol.at[2])

    def dh_send():
        return remote(dyv, dh_out.at[s], osend.at[2], orecv.at[2], sib)

    lax.fori_loop(0, 2, layer, 0)

    m_copy(0).start()
    ev_y(2)
    m_add(0, 0)
    m_copy(1).start()
    ev_z(1)
    ev_x(4)
    m_add(1, 1)
    m_copy(2).start()
    ev_y(3)
    ev_z(2)
    m_add(2, 2)
    if zin:
        for d in range(1, n_dp):
            m_z(d).start()
    ev_x(5)
    ev_y(4)
    ev_z(3)
    ev_y(5)
    ev_z(4)
    if zin:
        for d in range(1, n_dp):
            m_z(d).wait_send()
        for d in range(1, n_dp):
            m_add(2 + d, 0)
    smc = pltpu.make_async_copy(sm.at[s], sm_out, ld.at[5])
    smc.start()
    ev_z(5)

    smc.wait()
    m_copy(0).wait_send()
    for r in range(4):
        d_copy(r).wait_send()
    for n in range(6):
        for d in x_copies(n) + y_copies(n):
            d.wait_send()
        if zin:
            for d in z_copies(n):
                d.wait_send()
        else:
            q_copy(n).wait()
    for src, dst, i in ((y_in, lo_out, 0), (rms_in, rm_out, 1)):
        out_send(src, dst, i).wait()
        out_keep(src, dst, i).wait()
    @pl.when(s == 0)
    def _():
        dh_keep().wait()
    @pl.when(s == 1)
    def _():
        dh_send().wait_send()
    arrived(dh_out.at[1 - s], orecv.at[2])
    if zin:
        for k in range(3):
            arrived(f_out.at[2 - k, 1 - s], frecv.at[k])
            f_keep(k).wait()
            f_send(k).wait_send()


def run_k2(nch, L, n_dp, *ops):
    M = nch * L
    zin = n_dp == 4
    sub = D // (NJ * 4)
    S = jax.ShapeDtypeStruct
    V = pltpu.VMEM
    any_ = pl.BlockSpec(memory_space=pl.ANY)
    outs = (S((3, 2, 2, sub, 768), f32) if zin else S((2, 3, 2, NJ, sub, 768), bf16), S((16, 768), f32), S((2, M, D), bf16), S((2, M, D), bf16), S((2, 16, 128), f32))
    DMA = pltpu.SemaphoreType.DMA
    REG = pltpu.SemaphoreType.REGULAR
    bufs = [V((2, D, 768), bf16), V((2, D, 768), bf16), V((2, D, 768), bf16), V((2, M, FB), f32), V((2, M, FB), bf16), V((2, M, 3 * HB), bf16), V((2, nch, HPB, L, L), bf16), V((2, M, HB), bf16),
            V((2, M, D), f32), V((2, M, 1), f32), V((M, D), bf16), V((M, D), bf16), V((2, 4, 8, D), f32), V((M, D), f32), V((M, D), bf16), V((M, D), bf16), V((M, HB), bf16), V((M, 3 * HB), bf16), V((D, M), bf16), V((D, M), bf16),
            V((4, 2, 2, NJ, sub, 768), bf16), V((4, 2, NJ, sub, 768), bf16), V((6, 2, 4, NJ, sub, 768), bf16), V((3, 4, NJ, sub, 768), bf16), V((6, 2, NJ, sub, 768), bf16),
            V((6, 3, 2, sub, 768) if zin else (8, 128), bf16), V((6, 2, sub, 768) if zin else (8, 128), f32), V((2, 16, 768), f32), V((6, 16, 768), f32)]
    sems = [DMA((2,)), DMA((2, 3)), DMA((2, 4)), DMA((7,)), DMA((4,)), DMA((4,)), DMA((6, 4)), DMA((6, 4)), DMA((6, 2)), DMA((6, 2)), DMA((6, 3)), DMA((6, 3)), DMA((3,)), DMA((3,)), DMA((6,)), DMA((6,)), DMA((6,)),
            DMA((3,)), DMA((3,)), DMA((3,)), REG, REG, REG]
    return pl.pallas_call(
        functools.partial(k2_kernel, nch, L, n_dp, zin),
        out_shape=outs,
        in_specs=[any_] * 13,
        out_specs=[any_] * len(outs),
        scratch_shapes=bufs + sems,
        compiler_params=pltpu.CompilerParams(collective_id=1, has_side_effects=True, vmem_limit_bytes=63 << 20),
        name="backward_reduce",
    )(*ops)

def on_device(inputs, lengths, cotangent, w_qkv, qv_bias, w_out, out_bias, ln1_gain, ln1_bias, w_up, up_bias, w_down, down_bias, ln2_gain, ln2_bias):
    s = lax.axis_index("section")
    t = lax.axis_index("tensor")
    j = lax.axis_index("dp")
    n_dp = lax.axis_size("dp")
    chains, L, _ = inputs.shape
    nch = chains // 2
    M = nch * L
    wa = jnp.concatenate([w_qkv[0, 0], w_qkv[0, 1], w_qkv[0, 2], w_out[0].T], axis=1)
    z = jnp.zeros((HB,), f32)
    sp = jnp.stack([up_bias[0].reshape(-1), jnp.concatenate([qv_bias[0, 0].reshape(-1), z, qv_bias[0, 1].reshape(-1), z]),
                    out_bias[0], ln1_gain[0], ln1_bias[0], down_bias[0], ln2_gain[0], ln2_bias[0]])
    x = lax.dynamic_slice_in_dim(inputs, s * nch, nch, 0).reshape(M, D)
    dy = lax.dynamic_slice_in_dim(cotangent, s * nch, nch, 0).reshape(M, D)
    own_len = lax.dynamic_slice_in_dim(lengths, t * chains, chains, 0)
    my_len = lax.dynamic_slice_in_dim(own_len, s * nch, nch, 0)
    alive = jnp.arange(L)[None] < my_len[:, None]
    kb = jnp.where(alive, 0.0, MASK_FILL).astype(f32)
    live = alive.astype(f32).reshape(M, 1)
    w_all, sp_all, qkv, a, c, u, inv, g, gp, y, rms = run_k1(nch, L, wa, w_up[0], w_down[0], sp, x, kb, live)
    grads, sm, lo, dh, rm = run_k2(nch, L, n_dp, w_all, sp_all, qkv, a, c, u, inv, g, gp, y, x, dy, rms)
    if n_dp == 4:
        grads = grads.reshape(3, D // n_dp, 768)
    else:
        mine = grads[s].astype(f32)
        got = lax.ppermute(grads[1 - s], "section", [(0, 1), (1, 0)]).astype(f32)
        both = jnp.stack([jnp.where(s == 0, mine, got), jnp.where(s == 0, got, mine)])
        both = both.transpose(1, 3, 0, 2, 4, 5).reshape(3, D, 768)
        grads = lax.psum_scatter(both, "dp", scatter_dimension=1, tiled=True)
        sm = lax.psum(sm, "dp")
    ga, gu, gd = grads[0], grads[1], grads[2]
    dd = D // n_dp
    part = HS // n_dp
    share = D // (n_dp * 4)
    vec = lax.dynamic_slice_in_dim(sm[:6], (j * 4 + t) * share, share, 1)
    ub = lax.dynamic_slice_in_dim(sm[8].reshape(FB // HS, HS), j * part, part, 1)
    qb = lax.dynamic_slice_in_dim(sm[12, :3 * HB].reshape(3, HPB, HS), j * part, part, 2)[0::2]
    sums = rm[:, :3 * nch, 0].reshape(2, 3, nch).transpose(1, 0, 2).reshape(3, chains) / own_len.astype(f32)
    gq = ga[:, :3 * HB].reshape(dd, 3, HB).transpose(1, 0, 2)
    return (lo.reshape(1, chains, L, D), dh.reshape(1, chains, L, D), gq[None], qb[None], ga[:, 3 * HB:].T[None], gu[None], ub[None], gd.T[None], vec[None], sums[None])


def solution(mesh):
    in_specs = (
        P(("dp", "tensor"), None, None),
        P("dp"),
        P(("dp", "tensor"), None, None),
        P("section", None, None, "tensor"),
        P("section", None, "tensor", None),
        P("section", "tensor", None),
        P("section", None),
        P("section", None),
        P("section", None),
        P("section", None, "tensor"),
        P("section", "tensor", None),
        P("section", "tensor", None),
        P("section", None),
        P("section", None),
        P("section", None),
    )
    out_specs = (
        P("section", ("dp", "tensor"), None, None),
        P("section", ("dp", "tensor"), None, None),
        P("section", None, "dp", "tensor"),
        P("section", None, "tensor", "dp"),
        P("section", "tensor", "dp"),
        P("section", "dp", "tensor"),
        P("section", "tensor", "dp"),
        P("section", "tensor", "dp"),
        P("section", None, ("dp", "tensor")),
        P("section", None, ("dp", "tensor")),
    )
    return jax.shard_map(on_device, mesh=mesh, in_specs=in_specs, out_specs=out_specs, check_vma=False)
```

```python
import functools

import jax
import jax.numpy as jnp
from jax import lax
from jax.experimental import pallas as pl
from jax.experimental.pallas import tpu as pltpu
from jax.sharding import PartitionSpec as P


f32, bf16 = jnp.float32, jnp.bfloat16
D, FB, HB, HS = 768, 768, 192, 64
NT = (((1,), (1,)), ((), ()))
NN = (((1,), (0,)), ((), ()))
TN = (((0,), (0,)), ((), ()))
EPS_NORM, EPS_ROOT = 1e-12, 1e-6
MASK_FILL = -1e9
ROOT_HALF, INV_ROOT_TWO_PI = 0.7071067811865476, 0.3989422804014327
MESH = pl.DeviceIdType.MESH
KA, KU, KD = 0, 1, 2
HPB = HB // HS


def dot(a, b, dims=NN):
    return lax.dot_general(a, b, dims, preferred_element_type=f32)


def rows(i, n):
    return pl.ds(pl.multiple_of(i * n, n), n)


def mean_last(v):
    return jnp.mean(v, axis=-1, keepdims=True)


def rms_rows(v):
    return jnp.sqrt(mean_last(v * v) + EPS_ROOT)


def norm_step(x, gain, bias):
    c = x - mean_last(x)
    inv = lax.rsqrt(mean_last(c * c) + EPS_NORM)
    u = c * inv
    return u * gain + bias, u, inv


def norm_back(dn, u, inv, gain):
    du = dn * gain
    return inv * (du - mean_last(du) - u * mean_last(du * u))


def part8(v):
    t = v[0:8]
    for i in range(1, v.shape[0] // 8):
        t = t + v[8 * i:8 * (i + 1)]
    return t


def col_sum(v):
    return jnp.sum(part8(v), axis=0, keepdims=True)


def row_block(M):
    for n in (96, 80, 64, 48, 32, 16):
        if M % n == 0:
            return n
    return M


def attn_fwd_block(x_ref, wa_ref, sp_ref, kb_ref, qkv_ref, a_ref, c_ref, acc_ref, nch, L):
    qkv_ref[...] = (dot(x_ref[...], wa_ref[0:3 * HB, :], NT) + sp_ref[1:2, 0:3 * HB]).astype(bf16)
    for c in range(nch):
        rs = slice(c * L, (c + 1) * L)
        qkv = qkv_ref[rs, :]
        kb = kb_ref[c:c + 1, :]

        def head(t, i):
            return qkv[:, t * HB + i * HS:t * HB + (i + 1) * HS]
        scores = [dot(head(0, i), head(1, i), NT) * (HS ** -0.5) + kb for i in range(HPB)]
        probs = []
        for i in range(HPB):
            e = jnp.exp(scores[i] - jnp.max(scores[i], axis=-1, keepdims=True))
            a = (e / jnp.sum(e, axis=-1, keepdims=True)).astype(bf16)
            a_ref[c, i] = a
            probs.append(a)
        c_ref[rs, :] = jnp.concatenate([dot(probs[i], head(2, i)).astype(bf16) for i in range(HPB)], axis=1)
    acc_ref[...] += dot(c_ref[...], wa_ref[3 * HB:4 * HB, :])


def ln1_fwd(x_ref, acc_ref, sp_ref, u_ref, inv_ref, nlow_ref, rms_ref, M):
    rb = M // 3 if M % 48 == 0 else M

    def body(i, _):
        rs = rows(i, rb)
        h = x_ref[rs, :].astype(f32)
        att = acc_ref[rs, :] + sp_ref[2:3, :]
        n, u, inv = norm_step(h + att, sp_ref[3:4, :], sp_ref[4:5, :])
        u_ref[rs, :] = u
        inv_ref[rs, :] = inv
        nlow_ref[rs, :] = n.astype(bf16)
        rms_ref[0, rs, :] = rms_rows(h)
        rms_ref[1, rs, :] = rms_rows(att)
        return 0
    lax.fori_loop(0, M // rb, body, 0)


def up_block(nlow_ref, wu_ref, sp_ref, g_ref, gp_ref):
    for j in range(FB // 256):
        js = slice(256 * j, 256 * (j + 1))
        z = dot(nlow_ref[...], wu_ref[:, js]) + sp_ref[0:1, js]
        cdf = 0.5 * (1.0 + lax.erf(z * ROOT_HALF))
        g_ref[:, js] = (z * cdf).astype(bf16)
        gp_ref[:, js] = cdf + z * (INV_ROOT_TWO_PI * jnp.exp(-0.5 * z * z))


def down_block(g_ref, wd_ref, acc_ref):
    acc_ref[...] += dot(g_ref[...], wd_ref[...])


def ln2_fwd(u1_ref, acc_ref, sp_ref, u_ref, inv_ref, y_ref, rms_ref, M):
    rb = M // 3 if M % 48 == 0 else M

    def body(i, _):
        rs = rows(i, rb)
        n = u1_ref[rs, :] * sp_ref[3:4, :] + sp_ref[4:5, :]
        ffn = acc_ref[rs, :] + sp_ref[5:6, :]
        y, u, inv = norm_step(n + ffn, sp_ref[6:7, :], sp_ref[7:8, :])
        u_ref[rs, :] = u
        inv_ref[rs, :] = inv
        y_ref[rs, :] = y.astype(bf16)
        rms_ref[2, rs, :] = rms_rows(ffn)
        return 0
    lax.fori_loop(0, M // rb, body, 0)


def norm_bwd(dy_ref, u_ref, inv_ref, gain, dx_ref, low_ref, sm_ref, row, M):
    rb = row_block(M)

    def body(i, carry):
        a, b, c = carry
        rs = rows(i, rb)
        dy = dy_ref[rs, :].astype(f32)
        u = u_ref[rs, :]
        dx = norm_back(dy, u, inv_ref[rs, :], gain)
        dx_ref[rs, :] = dx
        low_ref[rs, :] = dx.astype(bf16)
        return (a + part8(dx), b + part8(dy * u), c + part8(dy))
    z = jnp.zeros((8, D), f32)
    sums = lax.fori_loop(0, M // rb, body, (z, z, z))
    for k in range(3):
        sm_ref[row + k:row + k + 1, :] = jnp.sum(sums[k], axis=0, keepdims=True)


def ffn_bwd_block(df_ref, wu_ref, wd_ref, gp_ref, dz_ref, dx_ref, ub_ref):
    for j in range(FB // 256):
        js = slice(256 * j, 256 * (j + 1))
        dz = (dot(df_ref[...], wd_ref[js, :], NT) * gp_ref[:, js]).astype(bf16)
        dz_ref[:, js] = dz
        ub_ref[:, js] = col_sum(dz.astype(f32))
    dx_ref[...] += dot(dz_ref[...], wu_ref[...], NT)


def attn_bwd_block(da_ref, wa_ref, qkv_ref, a_ref, dc_ref, dqkv_ref, dx_ref, qb_ref, nch, L):
    dc_ref[...] = dot(da_ref[...], wa_ref[3 * HB:4 * HB, :], NT).astype(bf16)
    for c in range(nch):
        rs = slice(c * L, (c + 1) * L)
        qkv = qkv_ref[rs, :]
        dc = dc_ref[rs, :]

        def head(t, i):
            return qkv[:, t * HB + i * HS:t * HB + (i + 1) * HS]
        dcs = [dc[:, i * HS:(i + 1) * HS] for i in range(HPB)]
        probs = [a_ref[c, i] for i in range(HPB)]
        drs = [dot(dcs[i], head(2, i), NT) for i in range(HPB)]
        dss = []
        for i in range(HPB):
            af = probs[i].astype(f32)
            t = af * drs[i]
            dss.append(((t - af * jnp.sum(t, axis=-1, keepdims=True)) * (HS ** -0.5)).astype(bf16))
        dqs = [dot(dss[i], head(1, i)) for i in range(HPB)]
        dks = [dot(dss[i], head(0, i), TN) for i in range(HPB)]
        dvs = [dot(probs[i], dcs[i], TN) for i in range(HPB)]
        dqkv_ref[rs, :] = jnp.concatenate(dqs + dks + dvs, axis=1).astype(bf16)
    dx_ref[...] += dot(dqkv_ref[...], wa_ref[0:3 * HB, :])
    qb_ref[:, 0:3 * HB] = col_sum(dqkv_ref[...].astype(f32))
ZR = 224
XY = D - ZR


def k1_kernel(nch, L,
              len_ref, x_in, wq_in, wo_in, wu_in, wd_in, qv_in, ub_in, v0_in, v1_in, v2_in, v3_in, v4_in, v5_in,
              w_out, sp_out, qkv_out, a_out, c_out, u_out, inv_out, g_out, gp_out, y_out, rms_out,
              wv, spv, xb, qkv, a, c, u, inv, g, gp, nlow, acc, rms, rmsv, wa_in, sp_in, qv, ub, vecs, kb_ref,
              recv, send, sp_recv, sp_send, loc, wsave, ssave, pre, go):
    M = nch * L
    s = lax.axis_index("section")
    t = lax.axis_index("tensor")
    xn = {"tensor": t + 1 - 2 * lax.rem(t, 2)}
    yn = {"tensor": t + 2 - 4 * lax.rem(t // 2, 2)}
    j = lax.axis_index("dp")
    sib = {"section": 1 - s}
    zn = {"dp": j + 1 - 2 * lax.rem(j, 2)}
    diag = {"tensor": 3 - t}
    e = lax.rem(j, 2)
    srcs = (wa_in, wu_in, wd_in)

    def remote(src, dst, ss, rs, dev):
        return pltpu.make_async_remote_copy(src_ref=src, dst_ref=dst, send_sem=ss, recv_sem=rs, device_id=dev, device_id_type=MESH)

    def span(start, n):
        return pl.ds(pl.multiple_of(start, 16), n)
    fetched = span(e * ZR, XY)
    half = [span(e * ZR + i * (XY // 2), XY // 2) for i in range(2)]
    given = span(e * XY, ZR)
    taken = span((1 - e) * XY, ZR)

    def view(ref, p):
        if p == 0:
            return ref.at[0]
        if p in (1, 2):
            return ref.at[p, fetched]
        if p in (3, 4):
            return ref.at[3, half[p - 3]]
        return ref.at[p - 4, taken]

    def part(l, k, p):
        return view(wv.at[l, k], p)

    def wait_part(l, k, p):
        ref = part(l, k, p)
        pltpu.make_async_copy(ref, ref, recv.at[l, k, p]).wait()

    def own_sends(l, k):
        return [remote(srcs[k].at[fetched], wv.at[l, k, 1, fetched], send.at[k, 0], recv.at[l, k, 1], xn),
                remote(srcs[k].at[fetched], wv.at[l, k, 2, fetched], send.at[k, 1], recv.at[l, k, 2], yn)]

    def own_local(l, k):
        return remote(srcs[k], wv.at[l, k, 0], send.at[k, 7], recv.at[l, k, 0], sib)

    def fwd_y(l, k):
        return remote(wv.at[l, k, 1, half[0]], wv.at[l, k, 3, half[0]], send.at[k, 2], recv.at[l, k, 3], yn)

    def fwd_x(l, k):
        return remote(wv.at[l, k, 2, half[1]], wv.at[l, k, 3, half[1]], send.at[k, 3], recv.at[l, k, 4], xn)

    def to_z(l, k, slot):
        ref = wv.at[l, k, slot, given]
        return remote(ref, ref, send.at[k, 3 + slot], recv.at[l, k, 4 + slot], zn)

    def to_sib(l, k, p):
        return remote(part(l, k, p), part(l, k, p), send.at[k, 7 + p], recv.at[l, k, p], sib)

    def save_w(l, k, p):
        return pltpu.make_async_copy(part(l, k, p), view(w_out.at[l, k], p), wsave.at[l, k, p])

    def arrive(l, k, p):
        wait_part(l, k, p)

        @pl.when(s == l)
        def _():
            if p == 1:
                fwd_y(l, k).start()
                to_z(l, k, 1).start()
            if p == 2:
                fwd_x(l, k).start()
                to_z(l, k, 2).start()
                if k == KA:
                    for d in own_sends(l, KD):
                        d.start()
            if p in (3, 4):
                @pl.when(e == p - 3)
                def _():
                    to_z(l, k, 3).start()
            if p > 0:
                to_sib(l, k, p).start()
        save_w(l, k, p).start()

    others = [(q, {"section": sec, "tensor": dev["tensor"]}) for q, dev in ((1, xn), (2, yn), (3, diag)) for sec in (s, 1 - s)] + [(0, sib)]

    def sp_sends(l):
        return [remote(sp_in, spv.at[l, q], sp_send.at[i], sp_recv.at[l, q], dev) for i, (q, dev) in enumerate(others)]

    def sp_wait(l):
        for q in range(4):
            pltpu.make_async_copy(spv.at[l, q], spv.at[l, q], sp_recv.at[l, q]).wait()

    loads = [pltpu.make_async_copy(src, dst, pre.at[i]) for i, (src, dst) in enumerate(
        [(wq_in.at[i], wa_in.at[pl.ds(i * HB, HB)]) for i in range(3)] + [(wo_in, wa_in.at[pl.ds(3 * HB, HB)]), (qv_in, qv), (ub_in, ub)] + [(v, vecs.at[i]) for i, v in enumerate((v0_in, v1_in, v2_in, v3_in, v4_in, v5_in))])]
    xcopy = pltpu.make_async_copy(x_in.at[s], xb, loc.at[0])
    for d in loads:
        d.start()
    xcopy.start()
    barrier = pltpu.get_barrier_semaphore()
    for dev in [zn] + [dev for q, dev in others]:
        pl.semaphore_signal(barrier, inc=1, device_id=dev, device_id_type=MESH)
    for d in loads:
        d.wait()
    zeros = jnp.zeros((1, HB), f32)
    sp_in[0:1, :] = jnp.concatenate([ub[i] for i in range(FB // HS)], axis=1)
    sp_in[1:2, :] = jnp.concatenate([qv[i, 0:1, :] for i in range(HPB)] + [zeros] + [qv[i, 1:2, :] for i in range(HPB)] + [zeros], axis=1)
    for i in range(6):
        sp_in[2 + i:3 + i, :] = vecs[i]
    first = (t * 2 + s) * nch
    place = lax.broadcasted_iota(jnp.int32, (1, L), 1)
    for i in range(nch):
        kb_ref[i:i + 1, :] = jnp.where(place < len_ref[first + i], 0.0, MASK_FILL)
    pl.semaphore_wait(barrier, 1 + len(others))

    for l in range(2):
        @pl.when(s == l)
        def _():
            for d in sp_sends(l):
                d.start()
            pltpu.make_async_copy(sp_in, spv.at[l, 0], sp_recv.at[l, 0]).start()
            if l == 0:
                for k in (KA, KU):
                    for d in own_sends(l, k):
                        d.start()
            for k in range(3):
                pltpu.make_async_copy(srcs[k], wv.at[l, k, 0], recv.at[l, k, 0]).start()
                own_local(l, k).start()
    for l in range(2):
        sp_wait(l)
    xcopy.wait()
    spsave = pltpu.make_async_copy(spv, sp_out, loc.at[1])
    spsave.start()

    def saves(l, which):
        pairs = {0: (qkv, qkv_out.at[l]), 1: (a, a_out.at[l]), 2: (c, c_out.at[l]), 3: (u.at[0], u_out.at[l, 0]),
                 4: (inv, inv_out.at[l]), 5: (g, g_out.at[l]), 6: (gp, gp_out.at[l]), 7: (u.at[1], u_out.at[l, 1]), 8: (xb, y_out.at[l])}
        src, dst = pairs[which]
        return pltpu.make_async_copy(src, dst, ssave.at[which])

    def layer(l, _):
        acc[...] = jnp.zeros_like(acc)
        @pl.when(l == 1)
        def _():
            for w in (0, 1, 2):
                saves(0, w).wait()

        def attn_step(r, _):
            @pl.when(r == 0)
            def _():
                arrive(l, KA, 0)
            @pl.when(r == 1)
            def _():
                @pl.when(l == 0)
                def _():
                    arrive(0, KA, 1)
                    arrive(0, KA, 2)
                for k, p in ((KU, 1), (KU, 2), (KA, 5), (KA, 6)):
                    arrive(l, k, p)

            @pl.when(r == 3)
            def _():
                for k, p in ((KA, 3), (KA, 4), (KU, 5), (KU, 6), (KA, 7)):
                    arrive(l, k, p)
            attn_fwd_block(xb, wv.at[l, KA, r], spv.at[l, r], kb_ref, qkv.at[r], a.at[r], c.at[r], acc, nch, L)
            return 0
        lax.fori_loop(0, 4, attn_step, 0)
        arrive(l, KD, 1)
        arrive(l, KD, 2)

        @pl.when((l == 0) & (s == 0))
        def _():
            pl.semaphore_signal(go, inc=1, device_id=sib, device_id_type=MESH)

        @pl.when((l == 0) & (s == 1))
        def _():
            pl.semaphore_wait(go, 1)
            for k in (KA, KU):
                for d in own_sends(1, k):
                    d.start()
        for w in (0, 1, 2):
            saves(l, w).start()
        @pl.when(l == 1)
        def _():
            for w in (3, 4, 5, 6, 7):
                saves(0, w).wait()
        ln1_fwd(xb, acc, spv.at[l, 0], u.at[0], inv.at[0], nlow, rms, M)
        saves(l, 3).start()

        def up_step(r, _):
            @pl.when(r == 0)
            def _():
                arrive(l, KU, 0)

            @pl.when(r == 3)
            def _():
                for k, p in ((KU, 3), (KU, 4), (KD, 5), (KD, 6), (KD, 3), (KD, 4), (KU, 7)):
                    arrive(l, k, p)
            up_block(nlow, wv.at[l, KU, r], spv.at[l, r], g.at[r], gp.at[r])
            return 0
        lax.fori_loop(0, 4, up_step, 0)
        saves(l, 5).start()
        saves(l, 6).start()
        acc[...] = jnp.zeros_like(acc)
        @pl.when(l == 1)
        def _():
            saves(0, 8).wait()

        def down_step(r, _):
            @pl.when(r == 0)
            def _():
                arrive(l, KD, 0)

            @pl.when(r == 3)
            def _():
                arrive(l, KD, 7)

                @pl.when(l == 0)
                def _():
                    arrive(1, KA, 1)
                    arrive(1, KA, 2)
            down_block(g.at[r], wv.at[l, KD, r], acc)
            return 0
        lax.fori_loop(0, 4, down_step, 0)
        ln2_fwd(u.at[0], acc, spv.at[l, 0], u.at[1], inv.at[1], xb, rms, M)
        for w in (4, 7, 8):
            saves(l, w).start()
        for k in range(3):
            for ch in range(nch):
                rs = slice(ch * L, (ch + 1) * L)
                live = lax.broadcasted_iota(jnp.int32, (L, 1), 0) < len_ref[first + ch]
                v = jnp.sum(jnp.where(live, rms[k, rs, :], 0.0), axis=0, keepdims=True)
                rmsv[l, pl.ds(k * nch + ch, 1), :] = jnp.broadcast_to(v, (1, 128))
        return 0
    lax.fori_loop(0, 2, layer, 0)
    for w in range(9):
        saves(1, w).wait()
    rc = pltpu.make_async_copy(rmsv, rms_out, loc.at[0])
    rc.start()
    rc.wait()
    spsave.wait()
    for l in range(2):
        for k in range(3):
            for p in range(8):
                save_w(l, k, p).wait()
        @pl.when(s == l)
        def _():
            for k in range(3):
                for d in own_sends(l, k) + [own_local(l, k), fwd_y(l, k), fwd_x(l, k)] + [to_z(l, k, q) for q in (1, 2, 3)] + [to_sib(l, k, p) for p in range(1, 8)]:
                    d.wait_send()
            for d in sp_sends(l):
                d.wait_send()


def run_k1(nch, L, lengths, x, *ops):
    M = nch * L
    S = jax.ShapeDtypeStruct
    V = pltpu.VMEM
    any_ = pl.BlockSpec(memory_space=pl.ANY)
    outs = (S((2, 3, 4, D, 768), bf16), S((2, 4, 8, D), f32), S((2, 4, M, 3 * HB), bf16), S((2, 4, nch, 3, L, L), bf16), S((2, 4, M, HB), bf16),
            S((2, 2, M, D), f32), S((2, 2, M, 1), f32), S((2, 4, M, FB), bf16), S((2, 4, M, FB), f32), S((2, M, D), bf16), S((2, 16, 128), f32))
    DMA = pltpu.SemaphoreType.DMA
    return pl.pallas_call(
        functools.partial(k1_kernel, nch, L),
        out_shape=outs,
        in_specs=[pl.BlockSpec(memory_space=pltpu.SMEM)] + [any_] * (1 + len(ops)),
        out_specs=[any_] * len(outs),
        scratch_shapes=[V((2, 3, 4, D, 768), bf16), V((2, 4, 8, D), f32), V((M, D), bf16), V((4, M, 3 * HB), bf16), V((4, nch, 3, L, L), bf16), V((4, M, HB), bf16),
                        V((2, M, D), f32), V((2, M, 1), f32), V((4, M, FB), bf16), V((4, M, FB), f32), V((M, D), bf16), V((M, D), f32), V((3, M, 1), f32), V((2, 16, 128), f32),
                        V((D, 768), bf16), V((8, D), f32), V((HPB, 2, HS), f32), V((FB // HS, 1, HS), f32), V((6, 1, D), f32), V((nch, L), f32),
                        DMA((2, 3, 8)), DMA((3, 15)), DMA((2, 4)), DMA((7,)), DMA((2,)), DMA((2, 3, 8)), DMA((9,)), DMA((12,)), pltpu.SemaphoreType.REGULAR],
        compiler_params=pltpu.CompilerParams(collective_id=0, has_side_effects=True, vmem_limit_bytes=62 << 20),
        name="gather_forward",
    )(lengths, x, *ops)

NJ = 4


def k2_kernel(nch, L, n_dp, zin,
              w_in, sp_in, qkv_in, a_in, c_in, u_in, inv_in, g_in, gp_in, y_in, x_in, dy_in, rms_in,
              f_out, sm_out, lo_out, dh_out, rm_out,
              wd, wu, wa, gp, g, qkv, a, c, u, inv, xin, dyv, spv, dx, low, low2, dc, dqkv, xt, xt2,
              pbuf, dbuf, qbuf, xbuf, ybuf, zbuf, fbuf, sm, smr,
              st_g, st_f, st_a, ld, dsend, drecv, xsend, xrecv, ysend, yrecv, zsend, zrecv, fsend, frecv, fl, msend, mrecv, osend, orecv, ol,
              dcred, xcred, ycred):
    M = nch * L
    sub = D // (NJ * 4)
    s = lax.axis_index("section")
    t = lax.axis_index("tensor")
    j = lax.axis_index("dp")
    xn = {"tensor": t + 1 - 2 * lax.rem(t, 2)}
    yn = {"tensor": t + 2 - 4 * lax.rem(t // 2, 2)}
    sib = {"section": 1 - s}
    zn = [{"dp": lax.rem(j + d, n_dp)} for d in range(1, n_dp)] if zin else []

    def remote(src, dst, ss, rs, dev):
        return pltpu.make_async_remote_copy(src_ref=src, dst_ref=dst, send_sem=ss, recv_sem=rs, device_id=dev, device_id_type=MESH)

    def arrived(ref, sem):
        pltpu.make_async_copy(ref, ref, sem).wait()

    def where_of(m):
        li = m // 4
        return 1 - li, 3 - (m - 4 * li), lax.rem(m, 2)

    def g_copies(m):
        l, r, b = where_of(m)
        return [pltpu.make_async_copy(g_in.at[l, r], g.at[b], st_g.at[b])]

    def f_copies(m):
        l, r, b = where_of(m)
        return [pltpu.make_async_copy(w_in.at[l, KD, r], wd.at[b], st_f.at[b, 0]),
                pltpu.make_async_copy(w_in.at[l, KU, r], wu.at[b], st_f.at[b, 1]),
                pltpu.make_async_copy(gp_in.at[l, r], gp.at[b], st_f.at[b, 2])]

    def a_copies(m):
        l, r, b = where_of(m)
        return [pltpu.make_async_copy(w_in.at[l, KA, r], wa.at[b], st_a.at[b, 0]),
                pltpu.make_async_copy(qkv_in.at[l, r], qkv.at[b], st_a.at[b, 1]),
                pltpu.make_async_copy(a_in.at[l, r], a.at[b], st_a.at[b, 2]),
                pltpu.make_async_copy(c_in.at[l, r], c.at[b], st_a.at[b, 3])]

    def begin(copies):
        for d in copies:
            d.start()

    def finish(copies):
        for d in copies:
            d.wait()

    def u_copies(l, i):
        return [pltpu.make_async_copy(u_in.at[l, i], u.at[i], ld.at[2 * i]), pltpu.make_async_copy(inv_in.at[l, i], inv.at[i], ld.at[2 * i + 1])]

    def x_copy(src):
        return [pltpu.make_async_copy(src, xin, ld.at[4])]

    first = [pltpu.make_async_copy(dy_in.at[s], dyv, ld.at[5]), pltpu.make_async_copy(sp_in, spv, ld.at[6])]
    begin(first)
    begin(u_copies(1, 1))
    begin(g_copies(0))
    begin(u_copies(1, 0))
    begin(g_copies(1))
    begin(f_copies(0))
    begin(f_copies(1))
    begin(x_copy(y_in.at[0]))
    begin(a_copies(0))
    begin(a_copies(1))

    barrier = pltpu.get_barrier_semaphore()
    for dev in [xn, yn, sib] + zn:
        pl.semaphore_signal(barrier, inc=1, device_id=dev, device_id_type=MESH)
    pl.semaphore_wait(barrier, 3 + len(zn))

    def out_send(src, dst, i):
        return remote(src.at[1 - s], dst.at[s], osend.at[i], orecv.at[i], sib)

    def out_keep(src, dst, i):
        return pltpu.make_async_copy(src.at[s], dst.at[s], ol.at[i])
    for src, dst, i in ((y_in, lo_out, 0), (rms_in, rm_out, 1)):
        out_send(src, dst, i).start()
        out_keep(src, dst, i).start()

    def d_copy(r):
        return remote(pbuf.at[r, 1 - s], dbuf.at[r], dsend.at[r], drecv.at[r], sib)

    def put(n, r, parts):
        @pl.when(n > 0)
        def _():
            d_copy(r).wait_send()
        for k in range(NJ):
            for h in range(2):
                for ab in range(2):
                    lo = ((k * 2 + h) * 2 + ab) * sub
                    pbuf[r, h, ab, k] = parts[lo:lo + sub, :].astype(bf16)

        @pl.when(n > 0)
        def _():
            pl.semaphore_wait(dcred, 1)
        d_copy(r).start()

    def x_copies(n):
        b = lax.rem(n, 3)
        return [remote(qbuf.at[n, 0, 3], xbuf.at[b, 1], xsend.at[n, 1], xrecv.at[n, 1], xn),
                remote(qbuf.at[n, 1, 3], xbuf.at[b, 3], xsend.at[n, 3], xrecv.at[n, 3], yn),
                remote(qbuf.at[n, 1, 2], xbuf.at[b, 2], xsend.at[n, 2], xrecv.at[n, 2], yn),
                remote(qbuf.at[n, 0, 1], xbuf.at[b, 0], xsend.at[n, 0], xrecv.at[n, 0], xn)]

    def d_add(n, r):
        arrived(dbuf.at[r], drecv.at[r])

        def one(ab, _):
            qbuf[n, ab, r] = (pbuf[r, s, ab].astype(f32) + dbuf[r, ab].astype(f32)).astype(bf16)
            return 0
        lax.fori_loop(0, 2, one, 0)

        @pl.when(n < 5)
        def _():
            pl.semaphore_signal(dcred, inc=1, device_id=sib, device_id_type=MESH)
        cs = x_copies(n)

        @pl.when(r == 3)
        def _():
            @pl.when(n >= 3)
            def _():
                pl.semaphore_wait(xcred, 1)
                pl.semaphore_wait(ycred, 1)
            cs[0].start()
            cs[1].start()

        @pl.when(r == 2)
        def _():
            cs[2].start()

        @pl.when(r == 1)
        def _():
            cs[3].start()

    def slots(n, step):
        def body(ri, _):
            step(ri, 3 - ri)

            @pl.when(ri > 0)
            def _():
                d_add(n, 4 - ri)
            return 0
        lax.fori_loop(0, 4, body, 0)
        d_add(n, 0)

    def y_copies(n):
        return [remote(qbuf.at[n, 0, 2], ybuf.at[n, 0], ysend.at[n, 0], yrecv.at[n, 0], yn),
                remote(qbuf.at[n, 1, 1], ybuf.at[n, 1], ysend.at[n, 1], yrecv.at[n, 1], xn)]

    def add_to(n, ab, r, ref):
        qbuf[n, ab, r] = (qbuf[n, ab, r].astype(f32) + ref[...].astype(f32)).astype(bf16)

    def ev_x(n):
        b = lax.rem(n, 3)
        arrived(xbuf.at[b, 1], xrecv.at[n, 1])
        add_to(n, 0, 2, xbuf.at[b, 1])
        cs = y_copies(n)
        cs[0].start()
        arrived(xbuf.at[b, 3], xrecv.at[n, 3])
        add_to(n, 1, 1, xbuf.at[b, 3])
        cs[1].start()
        arrived(xbuf.at[b, 0], xrecv.at[n, 0])
        add_to(n, 0, 0, xbuf.at[b, 0])
        arrived(xbuf.at[b, 2], xrecv.at[n, 2])
        add_to(n, 1, 0, xbuf.at[b, 2])

        @pl.when(n < 3)
        def _():
            pl.semaphore_signal(xcred, inc=1, device_id=xn, device_id_type=MESH)
            pl.semaphore_signal(ycred, inc=1, device_id=yn, device_id_type=MESH)

    def z_copies(n):
        return [remote(qbuf.at[n, :, 0, lax.rem(j + d, n_dp)], zbuf.at[n, d - 1], zsend.at[n, d - 1], zrecv.at[n, d - 1], zn[d - 1]) for d in range(1, n_dp)]

    def q_copy(n):
        li = n // 3
        return pltpu.make_async_copy(qbuf.at[n, :, 0], f_out.at[1 - li, 2 - (n - 3 * li)], fl.at[n])

    def ev_y(n):
        for i in range(2):
            arrived(ybuf.at[n, i], yrecv.at[n, i])
            add_to(n, i, 0, ybuf.at[n, i])
        if zin:
            begin(z_copies(n))
        else:
            q_copy(n).start()

    def f_keep(n):
        return pltpu.make_async_copy(fbuf.at[n], f_out.at[2 - lax.rem(n, 3), s], fl.at[lax.rem(n, 3)])

    def f_send(n):
        return remote(fbuf.at[n], f_out.at[2 - lax.rem(n, 3), s], fsend.at[lax.rem(n, 3)], frecv.at[lax.rem(n, 3)], sib)

    def ev_z(n):
        if not zin:
            return
        tot = qbuf[n, :, 0, j].astype(f32)
        for d in range(n_dp - 1):
            arrived(zbuf.at[n, d], zrecv.at[n, d])
            tot = tot + zbuf[n, d].astype(f32)
        fbuf[n] = tot
        mine = (1 - n // 3) == s

        @pl.when(mine)
        def _():
            f_keep(n).start()

        @pl.when(jnp.logical_not(mine))
        def _():
            f_send(n).start()

    def m_copy(i):
        if i == 0:
            return remote(sm.at[1 - s], smr.at[0], msend.at[0], mrecv.at[0], sib)
        return remote(sm.at[s], smr.at[i], msend.at[i], mrecv.at[i], xn if i == 1 else yn)

    def m_z(d):
        return remote(sm.at[s], smr.at[2 + d], msend.at[2 + d], mrecv.at[2 + d], zn[d - 1])

    def m_add(i, flip):
        arrived(smr.at[i], mrecv.at[i])
        if i in (1, 2):
            m_copy(i).wait_send()
        sm[s, 0:8, :] += smr[i, 0:8, :]
        for r in range(4):
            for base in (8, 12):
                sm[s, base + r:base + r + 1, :] += smr[i, base + (r ^ flip):base + (r ^ flip) + 1, :]

    finish(first)
    sm[...] = jnp.zeros_like(sm)

    def layer(li, _):
        l = 1 - li
        n0 = 3 * li
        spl = spv.at[l, 0]
        sml = sm.at[l]
        finish(u_copies(l, 1))
        norm_bwd(dyv, u.at[1], inv.at[1], spl[6:7, :], dx, low, sml, 3, M)

        @pl.when(li == 0)
        def _():
            begin(u_copies(0, 1))
        xt[...] = low[...].T

        def down_step(ri, r):
            m = 4 * li + ri
            finish(g_copies(m))
            put(n0, r, dot(xt[...], g[lax.rem(m, 2)]))

            @pl.when(m + 2 < 8)
            def _():
                begin(g_copies(m + 2))
        slots(n0, down_step)

        @pl.when(li == 1)
        def _():
            ev_y(1)
        finish(u_copies(l, 0))
        low2[...] = (u[0] * spl[3:4, :] + spl[4:5, :]).astype(bf16)
        xt[...] = low2[...].T

        def up_step(ri, r):
            m = 4 * li + ri
            b = lax.rem(m, 2)
            finish(f_copies(m))
            ffn_bwd_block(low, wu.at[b], wd.at[b], gp.at[b], low2, dx, sml.at[pl.ds(8 + r, 1)])
            put(n0 + 1, r, dot(xt[...], low2[...]))

            @pl.when(m + 2 < 8)
            def _():
                begin(f_copies(m + 2))
        slots(n0 + 1, up_step)

        @pl.when(li == 1)
        def _():
            ev_x(2)
            ev_z(0)
        norm_bwd(dx, u.at[0], inv.at[0], spl[3:4, :], dx, low, sml, 0, M)

        @pl.when(li == 0)
        def _():
            begin(u_copies(0, 0))
        xt2[...] = low[...].T
        finish(x_copy(x_in.at[s]))
        xt[...] = xin[...].T

        @pl.when(li == 0)
        def _():
            begin(x_copy(x_in.at[s]))

        def attn_step(ri, r):
            m = 4 * li + ri
            b = lax.rem(m, 2)
            finish(a_copies(m))
            attn_bwd_block(low, wa.at[b], qkv.at[b], a.at[b], dc, dqkv, dx, sml.at[pl.ds(12 + r, 1)], nch, L)
            put(n0 + 2, r, jnp.concatenate([dot(xt[...], dqkv[...]), dot(xt2[...], c[b])], axis=1))

            @pl.when(m + 2 < 8)
            def _():
                begin(a_copies(m + 2))

            @pl.when((li == 0) & (ri == 1))
            def _():
                ev_x(0)

            @pl.when((li == 0) & (ri == 3))
            def _():
                ev_x(1)
                ev_y(0)

            @pl.when((li == 1) & (ri == 3))
            def _():
                ev_x(3)
        slots(n0 + 2, attn_step)
        dyv[...] = dx[...].astype(bf16)
        own = l == s

        @pl.when(own)
        def _():
            dh_keep().start()

        @pl.when(jnp.logical_not(own))
        def _():
            dh_send().start()

        @pl.when(own & (li == 0))
        def _():
            dh_keep().wait()

        @pl.when(jnp.logical_not(own) & (li == 0))
        def _():
            dh_send().wait_send()
        return 0

    def dh_keep():
        return pltpu.make_async_copy(dyv, dh_out.at[s], ol.at[2])

    def dh_send():
        return remote(dyv, dh_out.at[s], osend.at[2], orecv.at[2], sib)

    lax.fori_loop(0, 2, layer, 0)

    m_copy(0).start()
    ev_y(2)
    m_add(0, 0)
    m_copy(1).start()
    ev_z(1)
    ev_x(4)
    m_add(1, 1)
    m_copy(2).start()
    ev_y(3)
    ev_z(2)
    m_add(2, 2)
    if zin:
        for d in range(1, n_dp):
            m_z(d).start()
    ev_x(5)
    ev_y(4)
    ev_z(3)
    ev_y(5)
    ev_z(4)
    if zin:
        for d in range(1, n_dp):
            m_z(d).wait_send()
        for d in range(1, n_dp):
            m_add(2 + d, 0)
    smc = pltpu.make_async_copy(sm.at[s], sm_out, ld.at[5])
    smc.start()
    ev_z(5)

    smc.wait()
    m_copy(0).wait_send()
    for r in range(4):
        d_copy(r).wait_send()
    for n in range(6):
        for d in x_copies(n) + y_copies(n):
            d.wait_send()
        if zin:
            for d in z_copies(n):
                d.wait_send()
        else:
            q_copy(n).wait()
    for src, dst, i in ((y_in, lo_out, 0), (rms_in, rm_out, 1)):
        out_send(src, dst, i).wait()
        out_keep(src, dst, i).wait()
    @pl.when(s == 0)
    def _():
        dh_keep().wait()
    @pl.when(s == 1)
    def _():
        dh_send().wait_send()
    arrived(dh_out.at[1 - s], orecv.at[2])
    if zin:
        for k in range(3):
            arrived(f_out.at[2 - k, 1 - s], frecv.at[k])
            f_keep(k).wait()
            f_send(k).wait_send()


def run_k2(nch, L, n_dp, *ops):
    M = nch * L
    zin = n_dp == 4
    sub = D // (NJ * 4)
    S = jax.ShapeDtypeStruct
    V = pltpu.VMEM
    any_ = pl.BlockSpec(memory_space=pl.ANY)
    outs = (S((3, 2, 2, sub, 768), f32) if zin else S((2, 3, 2, NJ, sub, 768), bf16), S((16, 768), f32), S((2, M, D), bf16), S((2, M, D), bf16), S((2, 16, 128), f32))
    DMA = pltpu.SemaphoreType.DMA
    REG = pltpu.SemaphoreType.REGULAR
    bufs = [V((2, D, 768), bf16), V((2, D, 768), bf16), V((2, D, 768), bf16), V((2, M, FB), f32), V((2, M, FB), bf16), V((2, M, 3 * HB), bf16), V((2, nch, HPB, L, L), bf16), V((2, M, HB), bf16),
            V((2, M, D), f32), V((2, M, 1), f32), V((M, D), bf16), V((M, D), bf16), V((2, 4, 8, D), f32), V((M, D), f32), V((M, D), bf16), V((M, D), bf16), V((M, HB), bf16), V((M, 3 * HB), bf16), V((D, M), bf16), V((D, M), bf16),
            V((4, 2, 2, NJ, sub, 768), bf16), V((4, 2, NJ, sub, 768), bf16), V((6, 2, 4, NJ, sub, 768), bf16), V((3, 4, NJ, sub, 768), bf16), V((6, 2, NJ, sub, 768), bf16),
            V((6, 3, 2, sub, 768) if zin else (8, 128), bf16), V((6, 2, sub, 768) if zin else (8, 128), f32), V((2, 16, 768), f32), V((6, 16, 768), f32)]
    sems = [DMA((2,)), DMA((2, 3)), DMA((2, 4)), DMA((7,)), DMA((4,)), DMA((4,)), DMA((6, 4)), DMA((6, 4)), DMA((6, 2)), DMA((6, 2)), DMA((6, 3)), DMA((6, 3)), DMA((3,)), DMA((3,)), DMA((6,)), DMA((6,)), DMA((6,)),
            DMA((3,)), DMA((3,)), DMA((3,)), REG, REG, REG]
    return pl.pallas_call(
        functools.partial(k2_kernel, nch, L, n_dp, zin),
        out_shape=outs,
        in_specs=[any_] * 13,
        out_specs=[any_] * len(outs),
        scratch_shapes=bufs + sems,
        compiler_params=pltpu.CompilerParams(collective_id=1, has_side_effects=True, vmem_limit_bytes=63 << 20),
        name="backward_reduce",
    )(*ops)

def finish_kernel(n_dp, nch, len_ref, f_in, sm_in, rm_in, lo_in, dh_in, lo_out, dh_out, gu, gd, gq, qb, go, ub, vec, sums, f_ref, sm_ref, rm_ref, lo_ref, dh_ref, sem):
    t = lax.axis_index("tensor")
    j = lax.axis_index("dp")
    loads = [pltpu.make_async_copy(src, dst, sem.at[i]) for i, (src, dst) in enumerate(((f_in, f_ref), (sm_in, sm_ref), (rm_in, rm_ref), (lo_in, lo_ref), (dh_in, dh_ref)))]
    stores = [pltpu.make_async_copy(src, dst, sem.at[5 + i]) for i, (src, dst) in enumerate(((f_ref.at[1], gu), (f_ref.at[2], gd), (lo_ref, lo_out), (dh_ref, dh_out)))]
    for d in loads:
        d.start()
    for d in loads:
        d.wait()
    for d in stores:
        d.start()
    ga = f_ref[0]
    for i in range(3):
        gq[i] = ga[:, i * HB:(i + 1) * HB]
    go[...] = ga[:, 3 * HB:4 * HB].T
    part = HS // n_dp
    share = D // (4 * n_dp)
    off = (j * 4 + t) * share
    rolled = pltpu.roll(sm_ref[0:8, :], lax.rem(D - off, D), 1)
    for i in range(6):
        vec[i] = rolled[i:i + 1, 0:share]
    slots = pltpu.roll(sm_ref[8:16, :], lax.rem(D - j * part, D), 1)
    for i in range(FB // HS):
        ub[i] = slots[0:1, i * HS:i * HS + part]
    for i in range(HPB):
        for b in range(2):
            lo = 2 * b * HB + i * HS
            qb[i, b:b + 1, :] = slots[4:5, lo:lo + part]
    for h in range(2):
        for c in range(nch):
            at = h * nch + c
            size = len_ref[t * 2 * nch + at].astype(f32)
            for k in range(3):
                sums[k, 0:1, at:at + 1] = rm_ref[h, k * nch + c:k * nch + c + 1, 0:1] / size
    for d in stores:
        d.wait()


def run_finish(n_dp, nch, M, lengths, f, sm, rm, lo, dh):
    S = jax.ShapeDtypeStruct
    V = pltpu.VMEM
    dd = D // n_dp
    part = HS // n_dp
    vm = pl.BlockSpec(memory_space=pltpu.VMEM)
    any_ = pl.BlockSpec(memory_space=pl.ANY)
    return pl.pallas_call(
        functools.partial(finish_kernel, n_dp, nch),
        out_shape=(S((2, M, D), bf16), S((2, M, D), bf16), S((dd, FB), f32), S((dd, FB), f32), S((3, dd, HB), f32), S((HPB, 2, part), f32), S((HB, dd), f32),
                   S((FB // HS, 1, part), f32), S((6, 1, D // (4 * n_dp)), f32), S((3, 1, 2 * nch), f32)),
        in_specs=[pl.BlockSpec(memory_space=pltpu.SMEM)] + [any_] * 5,
        out_specs=[any_] * 4 + [vm] * 6,
        scratch_shapes=[V((3, dd, FB), f32), V((16, D), f32), V((2, 16, 128), f32), V((2, M, D), bf16), V((2, M, D), bf16), pltpu.SemaphoreType.DMA((9,))],
        compiler_params=pltpu.CompilerParams(vmem_limit_bytes=60 << 20),
        name="finish",
    )(lengths, f, sm, rm, lo, dh)


def on_device(inputs, lengths, cotangent, w_qkv, qv_bias, w_out, out_bias, ln1_gain, ln1_bias, w_up, up_bias, w_down, down_bias, ln2_gain, ln2_bias):
    s = lax.axis_index("section")
    n_dp = lax.axis_size("dp")
    chains, L, _ = inputs.shape
    nch = chains // 2
    M = nch * L
    x = inputs.reshape(2, M, D)
    dy = cotangent.reshape(2, M, D)
    w_all, sp_all, qkv, a, c, u, inv, g, gp, y, rms = run_k1(
        nch, L, lengths, x, jnp.swapaxes(w_qkv[0], 1, 2), w_out[0], w_up[0], w_down[0], qv_bias[0].transpose(1, 0, 2), up_bias.transpose(1, 0, 2), out_bias, ln1_gain, ln1_bias, down_bias, ln2_gain, ln2_bias)
    grads, sm, lo, dh, rm = run_k2(nch, L, n_dp, w_all, sp_all, qkv, a, c, u, inv, g, gp, y, x, dy, rms)
    if n_dp == 4:
        grads = grads.reshape(3, D // n_dp, 768)
    else:
        mine = grads[s].astype(f32)
        got = lax.ppermute(grads[1 - s], "section", [(0, 1), (1, 0)]).astype(f32)
        both = jnp.stack([jnp.where(s == 0, mine, got), jnp.where(s == 0, got, mine)])
        both = both.transpose(1, 3, 0, 2, 4, 5).reshape(3, D, 768)
        grads = lax.psum_scatter(both, "dp", scatter_dimension=1, tiled=True)
        sm = lax.psum(sm, "dp")
    lo, dh, gu, gd, gq, qb, go, ub, vec, sums = run_finish(n_dp, nch, M, lengths, grads, sm, rm, lo, dh)
    return (lo.reshape(1, chains, L, D), dh.reshape(1, chains, L, D), gq[None], qb.transpose(1, 0, 2)[None], go[None], gu[None],
            ub.transpose(1, 0, 2), gd.T[None], vec.transpose(1, 0, 2), sums.transpose(1, 0, 2))


def solution(mesh):
    in_specs = (
        P(("dp", "tensor"), None, None),
        P("dp"),
        P(("dp", "tensor"), None, None),
        P("section", None, None, "tensor"),
        P("section", None, "tensor", None),
        P("section", "tensor", None),
        P("section", None),
        P("section", None),
        P("section", None),
        P("section", None, "tensor"),
        P("section", "tensor", None),
        P("section", "tensor", None),
        P("section", None),
        P("section", None),
        P("section", None),
    )
    out_specs = (
        P("section", ("dp", "tensor"), None, None),
        P("section", ("dp", "tensor"), None, None),
        P("section", None, "dp", "tensor"),
        P("section", None, "tensor", "dp"),
        P("section", "tensor", "dp"),
        P("section", "dp", "tensor"),
        P("section", "tensor", "dp"),
        P("section", "tensor", "dp"),
        P("section", None, ("dp", "tensor")),
        P("section", None, ("dp", "tensor")),
    )
    return jax.shard_map(on_device, mesh=mesh, in_specs=in_specs, out_specs=out_specs, check_vma=False)
```

```python
import functools

import jax
import jax.numpy as jnp
from jax import lax
from jax.experimental import pallas as pl
from jax.experimental.pallas import tpu as pltpu
from jax.sharding import PartitionSpec as P


f32, bf16 = jnp.float32, jnp.bfloat16
D, FB, HB, HS = 768, 768, 192, 64
NT = (((1,), (1,)), ((), ()))
NN = (((1,), (0,)), ((), ()))
TN = (((0,), (0,)), ((), ()))
EPS_NORM, EPS_ROOT = 1e-12, 1e-6
MASK_FILL = -1e9
ROOT_HALF, INV_ROOT_TWO_PI = 0.7071067811865476, 0.3989422804014327
MESH = pl.DeviceIdType.MESH
KA, KU, KD = 0, 1, 2
HPB = HB // HS


def dot(a, b, dims=NN):
    return lax.dot_general(a, b, dims, preferred_element_type=f32)


def rows(i, n):
    return pl.ds(pl.multiple_of(i * n, n), n)


def mean_last(v):
    return jnp.mean(v, axis=-1, keepdims=True)


def rms_rows(v):
    return jnp.sqrt(mean_last(v * v) + EPS_ROOT)


def norm_step(x, gain, bias):
    c = x - mean_last(x)
    inv = lax.rsqrt(mean_last(c * c) + EPS_NORM)
    u = c * inv
    return u * gain + bias, u, inv


def norm_back(dn, u, inv, gain):
    du = dn * gain
    return inv * (du - mean_last(du) - u * mean_last(du * u))


def part8(v):
    t = v[0:8]
    for i in range(1, v.shape[0] // 8):
        t = t + v[8 * i:8 * (i + 1)]
    return t


def col_sum(v):
    return jnp.sum(part8(v), axis=0, keepdims=True)


def row_block(M):
    for n in (96, 80, 64, 48, 32, 16):
        if M % n == 0:
            return n
    return M


def attn_fwd_block(x_ref, wa_ref, sp_ref, kb_ref, qkv_ref, a_ref, c_ref, acc_ref, nch, L):
    qkv_ref[...] = (dot(x_ref[...], wa_ref[0:3 * HB, :], NT) + sp_ref[1:2, 0:3 * HB]).astype(bf16)
    for c in range(nch):
        rs = slice(c * L, (c + 1) * L)
        qkv = qkv_ref[rs, :]
        kb = kb_ref[c:c + 1, :]

        def head(t, i):
            return qkv[:, t * HB + i * HS:t * HB + (i + 1) * HS]
        scores = [dot(head(0, i), head(1, i), NT) * (HS ** -0.5) + kb for i in range(HPB)]
        probs = []
        for i in range(HPB):
            e = jnp.exp(scores[i] - jnp.max(scores[i], axis=-1, keepdims=True))
            a = (e / jnp.sum(e, axis=-1, keepdims=True)).astype(bf16)
            a_ref[c, i] = a
            probs.append(a)
        c_ref[rs, :] = jnp.concatenate([dot(probs[i], head(2, i)).astype(bf16) for i in range(HPB)], axis=1)
    acc_ref[...] += dot(c_ref[...], wa_ref[3 * HB:4 * HB, :])


def ln1_fwd(x_ref, acc_ref, sp_ref, u_ref, inv_ref, nlow_ref, rms_ref, M):
    rb = M // 3 if M % 48 == 0 else M

    def body(i, _):
        rs = rows(i, rb)
        h = x_ref[rs, :].astype(f32)
        att = acc_ref[rs, :] + sp_ref[2:3, :]
        n, u, inv = norm_step(h + att, sp_ref[3:4, :], sp_ref[4:5, :])
        u_ref[rs, :] = u
        inv_ref[rs, :] = inv
        nlow_ref[rs, :] = n.astype(bf16)
        rms_ref[0, rs, :] = rms_rows(h)
        rms_ref[1, rs, :] = rms_rows(att)
        return 0
    lax.fori_loop(0, M // rb, body, 0)


def up_block(nlow_ref, wu_ref, sp_ref, g_ref, gp_ref):
    for j in range(FB // 256):
        js = slice(256 * j, 256 * (j + 1))
        z = dot(nlow_ref[...], wu_ref[:, js]) + sp_ref[0:1, js]
        cdf = 0.5 * (1.0 + lax.erf(z * ROOT_HALF))
        g_ref[:, js] = (z * cdf).astype(bf16)
        gp_ref[:, js] = cdf + z * (INV_ROOT_TWO_PI * jnp.exp(-0.5 * z * z))


def down_block(g_ref, wd_ref, acc_ref):
    acc_ref[...] += dot(g_ref[...], wd_ref[...])


def ln2_fwd(u1_ref, acc_ref, sp_ref, u_ref, inv_ref, y_ref, rms_ref, M):
    rb = M // 3 if M % 48 == 0 else M

    def body(i, _):
        rs = rows(i, rb)
        n = u1_ref[rs, :] * sp_ref[3:4, :] + sp_ref[4:5, :]
        ffn = acc_ref[rs, :] + sp_ref[5:6, :]
        y, u, inv = norm_step(n + ffn, sp_ref[6:7, :], sp_ref[7:8, :])
        u_ref[rs, :] = u
        inv_ref[rs, :] = inv
        y_ref[rs, :] = y.astype(bf16)
        rms_ref[2, rs, :] = rms_rows(ffn)
        return 0
    lax.fori_loop(0, M // rb, body, 0)


def norm_bwd(dy_ref, u_ref, inv_ref, gain, dx_ref, low_ref, sm_ref, row, M):
    rb = row_block(M)

    def body(i, carry):
        a, b, c = carry
        rs = rows(i, rb)
        dy = dy_ref[rs, :].astype(f32)
        u = u_ref[rs, :]
        dx = norm_back(dy, u, inv_ref[rs, :], gain)
        dx_ref[rs, :] = dx
        low_ref[rs, :] = dx.astype(bf16)
        return (a + part8(dx), b + part8(dy * u), c + part8(dy))
    z = jnp.zeros((8, D), f32)
    sums = lax.fori_loop(0, M // rb, body, (z, z, z))
    for k in range(3):
        sm_ref[row + k:row + k + 1, :] = jnp.sum(sums[k], axis=0, keepdims=True)


def ffn_bwd_block(df_ref, wu_ref, wd_ref, gp_ref, dz_ref, dx_ref, ub_ref):
    for j in range(FB // 256):
        js = slice(256 * j, 256 * (j + 1))
        dz = (dot(df_ref[...], wd_ref[js, :], NT) * gp_ref[:, js]).astype(bf16)
        dz_ref[:, js] = dz
        ub_ref[:, js] = col_sum(dz.astype(f32))
    dx_ref[...] += dot(dz_ref[...], wu_ref[...], NT)


def attn_bwd_block(da_ref, wa_ref, qkv_ref, a_ref, dc_ref, dqkv_ref, dx_ref, qb_ref, nch, L):
    dc_ref[...] = dot(da_ref[...], wa_ref[3 * HB:4 * HB, :], NT).astype(bf16)
    for c in range(nch):
        rs = slice(c * L, (c + 1) * L)
        qkv = qkv_ref[rs, :]
        dc = dc_ref[rs, :]

        def head(t, i):
            return qkv[:, t * HB + i * HS:t * HB + (i + 1) * HS]
        dcs = [dc[:, i * HS:(i + 1) * HS] for i in range(HPB)]
        probs = [a_ref[c, i] for i in range(HPB)]
        drs = [dot(dcs[i], head(2, i), NT) for i in range(HPB)]
        dss = []
        for i in range(HPB):
            af = probs[i].astype(f32)
            t = af * drs[i]
            dss.append(((t - af * jnp.sum(t, axis=-1, keepdims=True)) * (HS ** -0.5)).astype(bf16))
        dqs = [dot(dss[i], head(1, i)) for i in range(HPB)]
        dks = [dot(dss[i], head(0, i), TN) for i in range(HPB)]
        dvs = [dot(probs[i], dcs[i], TN) for i in range(HPB)]
        dqkv_ref[rs, :] = jnp.concatenate(dqs + dks + dvs, axis=1).astype(bf16)
    dx_ref[...] += dot(dqkv_ref[...], wa_ref[0:3 * HB, :])
    qb_ref[:, 0:3 * HB] = col_sum(dqkv_ref[...].astype(f32))
ZR = 192
XY = D - ZR


def k1_kernel(nch, L,
              len_ref, x_in, wq_in, wo_in, wu_in, wd_in, qv_in, ub_in, v0_in, v1_in, v2_in, v3_in, v4_in, v5_in,
              w_out, sp_out, qkv_out, a_out, c_out, u_out, inv_out, g_out, gp_out, y_out, rms_out,
              wv, spv, xb, qkv, a, c, u, inv, g, gp, nlow, acc, rms, rmsv, wa_in, sp_in, qv, ub, vecs, kb_ref,
              recv, send, sp_recv, sp_send, loc, wsave, ssave, pre, go):
    M = nch * L
    s = lax.axis_index("section")
    t = lax.axis_index("tensor")
    xn = {"tensor": t + 1 - 2 * lax.rem(t, 2)}
    yn = {"tensor": t + 2 - 4 * lax.rem(t // 2, 2)}
    j = lax.axis_index("dp")
    sib = {"section": 1 - s}
    zn = {"dp": j + 1 - 2 * lax.rem(j, 2)}
    diag = {"tensor": 3 - t}
    e = lax.rem(j, 2)
    srcs = (wa_in, wu_in, wd_in)

    def remote(src, dst, ss, rs, dev):
        return pltpu.make_async_remote_copy(src_ref=src, dst_ref=dst, send_sem=ss, recv_sem=rs, device_id=dev, device_id_type=MESH)

    def span(start, n):
        return pl.ds(pl.multiple_of(start, 16), n)
    fetched = span(e * ZR, XY)
    half = [span(e * ZR + i * (XY // 2), XY // 2) for i in range(2)]
    given = span(e * XY, ZR)
    taken = span((1 - e) * XY, ZR)

    def view(ref, p):
        if p == 0:
            return ref.at[0]
        if p in (1, 2):
            return ref.at[p, fetched]
        if p in (3, 4):
            return ref.at[3, half[p - 3]]
        return ref.at[p - 4, taken]

    def part(l, k, p):
        return view(wv.at[l, k], p)

    def wait_part(l, k, p):
        ref = part(l, k, p)
        pltpu.make_async_copy(ref, ref, recv.at[l, k, p]).wait()

    def own_sends(l, k):
        return [remote(srcs[k].at[fetched], wv.at[l, k, 1, fetched], send.at[k, 0], recv.at[l, k, 1], xn),
                remote(srcs[k].at[fetched], wv.at[l, k, 2, fetched], send.at[k, 1], recv.at[l, k, 2], yn)]

    def own_local(l, k):
        return remote(srcs[k], wv.at[l, k, 0], send.at[k, 7], recv.at[l, k, 0], sib)

    def fwd_y(l, k):
        return remote(wv.at[l, k, 1, half[0]], wv.at[l, k, 3, half[0]], send.at[k, 2], recv.at[l, k, 3], yn)

    def fwd_x(l, k):
        return remote(wv.at[l, k, 2, half[1]], wv.at[l, k, 3, half[1]], send.at[k, 3], recv.at[l, k, 4], xn)

    def to_z(l, k, slot):
        ref = wv.at[l, k, slot, given]
        return remote(ref, ref, send.at[k, 3 + slot], recv.at[l, k, 4 + slot], zn)

    def to_sib(l, k, p):
        return remote(part(l, k, p), part(l, k, p), send.at[k, 7 + p], recv.at[l, k, p], sib)

    def save_w(l, k, p):
        return pltpu.make_async_copy(part(l, k, p), view(w_out.at[l, k], p), wsave.at[l, k, p])

    def arrive(l, k, p):
        wait_part(l, k, p)

        @pl.when(s == l)
        def _():
            if p == 1:
                fwd_y(l, k).start()
                to_z(l, k, 1).start()
            if p == 2:
                fwd_x(l, k).start()
                to_z(l, k, 2).start()
                if k == KA:
                    for d in own_sends(l, KD):
                        d.start()

                    @pl.when(l == 0)
                    def _():
                        own_local(0, KU).start()
                        own_local(0, KD).start()
            if p in (3, 4):
                @pl.when(e == p - 3)
                def _():
                    to_z(l, k, 3).start()
            if p > 0:
                to_sib(l, k, p).start()
        save_w(l, k, p).start()

    others = [(q, {"section": sec, "tensor": dev["tensor"]}) for q, dev in ((1, xn), (2, yn), (3, diag)) for sec in (s, 1 - s)] + [(0, sib)]

    def sp_sends(l):
        return [remote(sp_in, spv.at[l, q], sp_send.at[i], sp_recv.at[l, q], dev) for i, (q, dev) in enumerate(others)]

    def sp_wait(l):
        for q in range(4):
            pltpu.make_async_copy(spv.at[l, q], spv.at[l, q], sp_recv.at[l, q]).wait()

    loads = [pltpu.make_async_copy(src, dst, pre.at[i]) for i, (src, dst) in enumerate(
        [(wq_in.at[i], wa_in.at[pl.ds(i * HB, HB)]) for i in range(3)] + [(wo_in, wa_in.at[pl.ds(3 * HB, HB)]), (qv_in, qv), (ub_in, ub)] + [(v, vecs.at[i]) for i, v in enumerate((v0_in, v1_in, v2_in, v3_in, v4_in, v5_in))])]
    xcopy = pltpu.make_async_copy(x_in.at[s], xb, loc.at[0])
    for d in loads:
        d.start()
    xcopy.start()
    barrier = pltpu.get_barrier_semaphore()
    for dev in [zn] + [dev for q, dev in others]:
        pl.semaphore_signal(barrier, inc=1, device_id=dev, device_id_type=MESH)
    for d in loads:
        d.wait()
    zeros = jnp.zeros((1, HB), f32)
    sp_in[0:1, :] = jnp.concatenate([ub[i] for i in range(FB // HS)], axis=1)
    sp_in[1:2, :] = jnp.concatenate([qv[i, 0:1, :] for i in range(HPB)] + [zeros] + [qv[i, 1:2, :] for i in range(HPB)] + [zeros], axis=1)
    for i in range(6):
        sp_in[2 + i:3 + i, :] = vecs[i]
    first = (t * 2 + s) * nch
    place = lax.broadcasted_iota(jnp.int32, (1, L), 1)
    for i in range(nch):
        kb_ref[i:i + 1, :] = jnp.where(place < len_ref[first + i], 0.0, MASK_FILL)
    pl.semaphore_wait(barrier, 1 + len(others))

    for l in range(2):
        @pl.when(s == l)
        def _():
            for d in sp_sends(l):
                d.start()
            pltpu.make_async_copy(sp_in, spv.at[l, 0], sp_recv.at[l, 0]).start()
            if l == 0:
                for k in (KA, KU):
                    for d in own_sends(l, k):
                        d.start()
            for k in range(3):
                pltpu.make_async_copy(srcs[k], wv.at[l, k, 0], recv.at[l, k, 0]).start()
                if l == 1 or k == KA:
                    own_local(l, k).start()
    for l in range(2):
        sp_wait(l)
    xcopy.wait()
    spsave = pltpu.make_async_copy(spv, sp_out, loc.at[1])
    spsave.start()

    def saves(l, which):
        pairs = {0: (qkv, qkv_out.at[l]), 1: (a, a_out.at[l]), 2: (c, c_out.at[l]), 3: (u.at[0], u_out.at[l, 0]),
                 4: (inv, inv_out.at[l]), 5: (g, g_out.at[l]), 6: (gp, gp_out.at[l]), 7: (u.at[1], u_out.at[l, 1]), 8: (xb, y_out.at[l])}
        src, dst = pairs[which]
        return pltpu.make_async_copy(src, dst, ssave.at[which])

    def layer(l, _):
        acc[...] = jnp.zeros_like(acc)
        @pl.when(l == 1)
        def _():
            for w in (0, 1, 2):
                saves(0, w).wait()

        def attn_step(r, _):
            @pl.when(r == 0)
            def _():
                arrive(l, KA, 0)
            @pl.when(r == 1)
            def _():
                @pl.when(l == 0)
                def _():
                    arrive(0, KA, 1)
                    arrive(0, KA, 2)
                for k, p in ((KU, 1), (KU, 2), (KA, 5), (KA, 6)):
                    arrive(l, k, p)

            @pl.when(r == 3)
            def _():
                for k, p in ((KA, 3), (KA, 4), (KU, 5), (KU, 6), (KA, 7)):
                    arrive(l, k, p)
            attn_fwd_block(xb, wv.at[l, KA, r], spv.at[l, r], kb_ref, qkv.at[r], a.at[r], c.at[r], acc, nch, L)
            return 0
        lax.fori_loop(0, 4, attn_step, 0)
        arrive(l, KD, 1)
        arrive(l, KD, 2)

        @pl.when((l == 0) & (s == 0))
        def _():
            pl.semaphore_signal(go, inc=1, device_id=sib, device_id_type=MESH)

        @pl.when((l == 0) & (s == 1))
        def _():
            pl.semaphore_wait(go, 1)
            for k in (KA, KU):
                for d in own_sends(1, k):
                    d.start()
        for w in (0, 1, 2):
            saves(l, w).start()
        @pl.when(l == 1)
        def _():
            for w in (3, 4, 5, 6, 7):
                saves(0, w).wait()
        ln1_fwd(xb, acc, spv.at[l, 0], u.at[0], inv.at[0], nlow, rms, M)
        saves(l, 3).start()

        def up_step(r, _):
            @pl.when(r == 0)
            def _():
                arrive(l, KU, 0)

            @pl.when(r == 3)
            def _():
                for k, p in ((KU, 3), (KU, 4), (KD, 5), (KD, 6), (KD, 3), (KD, 4), (KU, 7)):
                    arrive(l, k, p)
            up_block(nlow, wv.at[l, KU, r], spv.at[l, r], g.at[r], gp.at[r])
            return 0
        lax.fori_loop(0, 4, up_step, 0)
        saves(l, 5).start()
        saves(l, 6).start()
        acc[...] = jnp.zeros_like(acc)
        @pl.when(l == 1)
        def _():
            saves(0, 8).wait()

        def down_step(r, _):
            @pl.when(r == 0)
            def _():
                arrive(l, KD, 0)

            @pl.when(r == 3)
            def _():
                arrive(l, KD, 7)

                @pl.when(l == 0)
                def _():
                    arrive(1, KA, 1)
                    arrive(1, KA, 2)
            down_block(g.at[r], wv.at[l, KD, r], acc)
            return 0
        lax.fori_loop(0, 4, down_step, 0)
        ln2_fwd(u.at[0], acc, spv.at[l, 0], u.at[1], inv.at[1], xb, rms, M)
        for w in (4, 7, 8):
            saves(l, w).start()
        for k in range(3):
            for ch in range(nch):
                rs = slice(ch * L, (ch + 1) * L)
                live = lax.broadcasted_iota(jnp.int32, (L, 1), 0) < len_ref[first + ch]
                v = jnp.sum(jnp.where(live, rms[k, rs, :], 0.0), axis=0, keepdims=True)
                rmsv[l, pl.ds(k * nch + ch, 1), :] = jnp.broadcast_to(v, (1, 128))
        return 0
    lax.fori_loop(0, 2, layer, 0)
    for w in range(9):
        saves(1, w).wait()
    rc = pltpu.make_async_copy(rmsv, rms_out, loc.at[0])
    rc.start()
    rc.wait()
    spsave.wait()
    for l in range(2):
        for k in range(3):
            for p in range(8):
                save_w(l, k, p).wait()
        @pl.when(s == l)
        def _():
            for k in range(3):
                for d in own_sends(l, k) + [own_local(l, k), fwd_y(l, k), fwd_x(l, k)] + [to_z(l, k, q) for q in (1, 2, 3)] + [to_sib(l, k, p) for p in range(1, 8)]:
                    d.wait_send()
            for d in sp_sends(l):
                d.wait_send()


def run_k1(nch, L, lengths, x, *ops):
    M = nch * L
    S = jax.ShapeDtypeStruct
    V = pltpu.VMEM
    any_ = pl.BlockSpec(memory_space=pl.ANY)
    outs = (S((2, 3, 4, D, 768), bf16), S((2, 4, 8, D), f32), S((2, 4, M, 3 * HB), bf16), S((2, 4, nch, 3, L, L), bf16), S((2, 4, M, HB), bf16),
            S((2, 2, M, D), f32), S((2, 2, M, 1), f32), S((2, 4, M, FB), bf16), S((2, 4, M, FB), f32), S((2, M, D), bf16), S((2, 16, 128), f32))
    DMA = pltpu.SemaphoreType.DMA
    return pl.pallas_call(
        functools.partial(k1_kernel, nch, L),
        out_shape=outs,
        in_specs=[pl.BlockSpec(memory_space=pltpu.SMEM)] + [any_] * (1 + len(ops)),
        out_specs=[any_] * len(outs),
        scratch_shapes=[V((2, 3, 4, D, 768), bf16), V((2, 4, 8, D), f32), V((M, D), bf16), V((4, M, 3 * HB), bf16), V((4, nch, 3, L, L), bf16), V((4, M, HB), bf16),
                        V((2, M, D), f32), V((2, M, 1), f32), V((4, M, FB), bf16), V((4, M, FB), f32), V((M, D), bf16), V((M, D), f32), V((3, M, 1), f32), V((2, 16, 128), f32),
                        V((D, 768), bf16), V((8, D), f32), V((HPB, 2, HS), f32), V((FB // HS, 1, HS), f32), V((6, 1, D), f32), V((nch, L), f32),
                        DMA((2, 3, 8)), DMA((3, 15)), DMA((2, 4)), DMA((7,)), DMA((2,)), DMA((2, 3, 8)), DMA((9,)), DMA((12,)), pltpu.SemaphoreType.REGULAR],
        compiler_params=pltpu.CompilerParams(collective_id=0, has_side_effects=True, vmem_limit_bytes=62 << 20),
        name="gather_forward",
    )(lengths, x, *ops)

NJ = 4
NC = 2
CW = 768 // NC


def k2_kernel(nch, L, n_dp, zin,
              w_in, sp_in, qkv_in, a_in, c_in, u_in, inv_in, g_in, gp_in, y_in, x_in, dy_in, rms_in,
              f_out, sm_out, lo_out, dh_out, rm_out,
              wd, wu, wa, gp, g, qkv, a, c, u, inv, xin, dyv, spv, dx, low, low2, dc, dqkv, xt, xt2,
              pbuf, dbuf, qbuf, xbuf, ybuf, zbuf, fbuf, sm, smr, z0, x0, y0, z0send, z0recv,
              st_g, st_f, st_a, ld, dsend, drecv, xsend, xrecv, ysend, yrecv, zsend, zrecv, fsend, frecv, fl, msend, mrecv, osend, orecv, ol,
              dcred, xcred, ycred):
    M = nch * L
    sub = D // (NJ * 4)
    s = lax.axis_index("section")
    t = lax.axis_index("tensor")
    j = lax.axis_index("dp")
    xn = {"tensor": t + 1 - 2 * lax.rem(t, 2)}
    yn = {"tensor": t + 2 - 4 * lax.rem(t // 2, 2)}
    sib = {"section": 1 - s}
    zn = [{"dp": lax.rem(j + d, n_dp)} for d in range(1, n_dp)] if zin else []

    def remote(src, dst, ss, rs, dev):
        return pltpu.make_async_remote_copy(src_ref=src, dst_ref=dst, send_sem=ss, recv_sem=rs, device_id=dev, device_id_type=MESH)

    def arrived(ref, sem):
        pltpu.make_async_copy(ref, ref, sem).wait()

    def where_of(m):
        li = m // 4
        return 1 - li, 3 - (m - 4 * li), lax.rem(m, 2)

    def g_copies(m):
        l, r, b = where_of(m)
        return [pltpu.make_async_copy(g_in.at[l, r], g.at[b], st_g.at[b])]

    def f_copies(m):
        l, r, b = where_of(m)
        return [pltpu.make_async_copy(w_in.at[l, KD, r], wd.at[b], st_f.at[b, 0]),
                pltpu.make_async_copy(w_in.at[l, KU, r], wu.at[b], st_f.at[b, 1]),
                pltpu.make_async_copy(gp_in.at[l, r], gp.at[b], st_f.at[b, 2])]

    def a_copies(m):
        l, r, b = where_of(m)
        return [pltpu.make_async_copy(w_in.at[l, KA, r], wa.at[b], st_a.at[b, 0]),
                pltpu.make_async_copy(qkv_in.at[l, r], qkv.at[b], st_a.at[b, 1]),
                pltpu.make_async_copy(a_in.at[l, r], a.at[b], st_a.at[b, 2]),
                pltpu.make_async_copy(c_in.at[l, r], c.at[b], st_a.at[b, 3])]

    def begin(copies):
        for d in copies:
            d.start()

    def finish(copies):
        for d in copies:
            d.wait()

    def u_copies(l, i):
        return [pltpu.make_async_copy(u_in.at[l, i], u.at[i], ld.at[2 * i]), pltpu.make_async_copy(inv_in.at[l, i], inv.at[i], ld.at[2 * i + 1])]

    def x_copy(src):
        return [pltpu.make_async_copy(src, xin, ld.at[4])]

    first = [pltpu.make_async_copy(dy_in.at[s], dyv, ld.at[5]), pltpu.make_async_copy(sp_in, spv, ld.at[6])]
    begin(first)
    begin(u_copies(1, 1))
    begin(g_copies(0))
    begin(u_copies(1, 0))
    begin(g_copies(1))
    begin(f_copies(0))
    begin(f_copies(1))
    begin(x_copy(y_in.at[0]))
    begin(a_copies(0))
    begin(a_copies(1))

    barrier = pltpu.get_barrier_semaphore()
    for dev in [xn, yn, sib] + zn:
        pl.semaphore_signal(barrier, inc=1, device_id=dev, device_id_type=MESH)

    def out_send(src, dst, i):
        return remote(src.at[1 - s], dst.at[s], osend.at[i], orecv.at[i], sib)

    def out_keep(src, dst, i):
        return pltpu.make_async_copy(src.at[s], dst.at[s], ol.at[i])
    def d_copy(r):
        return remote(pbuf.at[r, 1 - s], dbuf.at[r], dsend.at[r], drecv.at[r], sib)

    def put(n, r, parts):
        @pl.when(n > 0)
        def _():
            d_copy(r).wait_send()
        for k in range(NJ):
            for h in range(2):
                for ab in range(2):
                    lo = ((k * 2 + h) * 2 + ab) * sub
                    pbuf[r, h, ab, k] = parts[lo:lo + sub, :].astype(bf16)

        @pl.when(n > 0)
        def _():
            pl.semaphore_wait(dcred, 1)
        d_copy(r).start()

    def x_copy_of(n, h, i):
        ab, r, dev = ((0, 1, xn), (0, 3, xn), (1, 2, yn), (1, 3, yn))[i]
        return remote(qbuf.at[n, h, ab, r], xbuf.at[lax.rem(n, 3), h, i], xsend.at[n, h, i], xrecv.at[n, h, i], dev)

    def cols(h):
        return slice(h * CW, (h + 1) * CW)

    def d_add(n, r):
        arrived(dbuf.at[r], drecv.at[r])

        def one(ab, _):
            for h in range(NC):
                qbuf[n, h, ab, r] = (pbuf[r, s, ab, :, :, cols(h)].astype(f32) + dbuf[r, ab, :, :, cols(h)].astype(f32)).astype(bf16)
            return 0
        lax.fori_loop(0, 2, one, 0)

        @pl.when(n < 5)
        def _():
            pl.semaphore_signal(dcred, inc=1, device_id=sib, device_id_type=MESH)

        x_sends(n, r)

    def x_sends(n, r):
        go = n >= (1 if zin else 0)

        @pl.when(go & (r == 3))
        def _():
            @pl.when(n >= (4 if zin else 3))
            def _():
                pl.semaphore_wait(xcred, 1)
                pl.semaphore_wait(ycred, 1)
            for h in range(NC):
                x_copy_of(n, h, 1).start()
                x_copy_of(n, h, 3).start()

        @pl.when(go & (r == 2))
        def _():
            for h in range(NC):
                x_copy_of(n, h, 2).start()

        @pl.when(go & (r == 1))
        def _():
            for h in range(NC):
                x_copy_of(n, h, 0).start()

    def slots(n, step):
        def body(ri, _):
            step(ri, 3 - ri)

            @pl.when(ri > 0)
            def _():
                d_add(n, 4 - ri)
            return 0
        lax.fori_loop(0, 4, body, 0)
        d_add(n, 0)

    def y_copies(n, h):
        return [remote(qbuf.at[n, h, 0, 2], ybuf.at[n, h, 0], ysend.at[n, h, 0], yrecv.at[n, h, 0], yn),
                remote(qbuf.at[n, h, 1, 1], ybuf.at[n, h, 1], ysend.at[n, h, 1], yrecv.at[n, h, 1], xn)]

    def add_to(n, h, ab, r, ref):
        qbuf[n, h, ab, r] = (qbuf[n, h, ab, r].astype(f32) + ref[...].astype(f32)).astype(bf16)

    def ev_x(n, h):
        b = lax.rem(n, 3)
        cs = y_copies(n, h)
        for i, ab, r in ((1, 0, 2), (3, 1, 1), (0, 0, 0), (2, 1, 0)):
            arrived(xbuf.at[b, h, i], xrecv.at[n, h, i])
            add_to(n, h, ab, r, xbuf.at[b, h, i])
            if i in (1, 3):
                cs[i // 2].start()
        if h == NC - 1:
            @pl.when((n < 3) & (n > 0) if zin else n < 3)
            def _():
                pl.semaphore_signal(xcred, inc=1, device_id=xn, device_id_type=MESH)
                pl.semaphore_signal(ycred, inc=1, device_id=yn, device_id_type=MESH)

    def z_copies(n, h):
        return [remote(qbuf.at[n, h, :, 0, lax.rem(j + d, n_dp)], zbuf.at[n, h, d - 1], zsend.at[n, h, d - 1], zrecv.at[n, h, d - 1], zn[d - 1]) for d in range(1, n_dp)]

    def q_copy(n, h):
        li = n // 3
        return pltpu.make_async_copy(qbuf.at[n, h, :, 0], f_out.at[1 - li, 2 - (n - 3 * li), h], fl.at[n, h])

    def ev_y(n, h):
        for i in range(2):
            arrived(ybuf.at[n, h, i], yrecv.at[n, h, i])
            add_to(n, h, i, 0, ybuf.at[n, h, i])
        if zin:
            begin(z_copies(n, h))
        else:
            q_copy(n, h).start()

    def f_keep(n):
        return pltpu.make_async_copy(fbuf.at[n], f_out.at[2 - lax.rem(n, 3), s], fl.at[lax.rem(n, 3), 0])

    def f_send(n):
        return remote(fbuf.at[n], f_out.at[2 - lax.rem(n, 3), s], fsend.at[lax.rem(n, 3)], frecv.at[lax.rem(n, 3)], sib)

    def ship(n):
        mine = (1 - n // 3) == s

        @pl.when(mine)
        def _():
            f_keep(n).start()

        @pl.when(jnp.logical_not(mine))
        def _():
            f_send(n).start()

    def ev_z(n, h):
        if not zin:
            return
        tot = qbuf[n, h, :, 0, j].astype(f32)
        for d in range(n_dp - 1):
            arrived(zbuf.at[n, h, d], zrecv.at[n, h, d])
            tot = tot + zbuf[n, h, d].astype(f32)
        fbuf[n, :, :, cols(h)] = tot
        if h < NC - 1:
            return
        ship(n)

    def first_z(h):
        return [remote(qbuf.at[0, h, :, :, lax.rem(j + d, n_dp)], z0.at[h, d - 1], z0send.at[h, d - 1], z0recv.at[h, d - 1], zn[d - 1]) for d in range(1, n_dp)]

    def first_x(h, i):
        ab, r, dev = ((0, 1, xn), (0, 3, xn), (1, 2, yn), (1, 3, yn))[i]
        return remote(qbuf.at[0, h, ab, r, j], x0.at[h, i], xsend.at[0, h, i], xrecv.at[0, h, i], dev)

    def first_y(h):
        return [remote(qbuf.at[0, h, 0, 2, j], y0.at[h, 0], ysend.at[0, h, 0], yrecv.at[0, h, 0], yn),
                remote(qbuf.at[0, h, 1, 1, j], y0.at[h, 1], ysend.at[0, h, 1], yrecv.at[0, h, 1], xn)]

    def add_first(h, ab, r, ref):
        qbuf[0, h, ab, r, j] = (qbuf[0, h, ab, r, j].astype(f32) + ref[...].astype(f32)).astype(bf16)

    def ev_first_z():
        for h in range(NC):
            for d in range(n_dp - 1):
                arrived(z0.at[h, d], z0recv.at[h, d])
            for ab in range(2):
                for r in range(4):
                    tot = qbuf[0, h, ab, r, j].astype(f32)
                    for d in range(n_dp - 1):
                        tot = tot + z0[h, d, ab, r].astype(f32)
                    qbuf[0, h, ab, r, j] = tot.astype(bf16)
            for i in range(4):
                first_x(h, i).start()

    def ev_first_x():
        for h in range(NC):
            for i, ab, r in ((1, 0, 2), (3, 1, 1), (0, 0, 0), (2, 1, 0)):
                arrived(x0.at[h, i], xrecv.at[0, h, i])
                add_first(h, ab, r, x0.at[h, i])
            begin(first_y(h))

    def ev_first_y():
        for h in range(NC):
            for i in range(2):
                arrived(y0.at[h, i], yrecv.at[0, h, i])
                fbuf[0, i, :, cols(h)] = qbuf[0, h, i, 0, j].astype(f32) + y0[h, i].astype(f32)
        ship(0)

    def both(ev, n):
        for h in range(NC):
            ev(n, h)

    def m_copy(i):
        if i == 0:
            return remote(sm.at[1 - s], smr.at[0], msend.at[0], mrecv.at[0], sib)
        return remote(sm.at[s], smr.at[i], msend.at[i], mrecv.at[i], xn if i == 1 else yn)

    def m_z(d):
        return remote(sm.at[s], smr.at[2 + d], msend.at[2 + d], mrecv.at[2 + d], zn[d - 1])

    def m_add(i, flip):
        arrived(smr.at[i], mrecv.at[i])
        if i in (1, 2):
            m_copy(i).wait_send()
        sm[s, 0:8, :] += smr[i, 0:8, :]
        for r in range(4):
            for base in (8, 12):
                sm[s, base + r:base + r + 1, :] += smr[i, base + (r ^ flip):base + (r ^ flip) + 1, :]

    def start_layer(l):
        finish(u_copies(l, 1))
        norm_bwd(dyv, u.at[1], inv.at[1], spv[l, 0, 6:7, :], dx, low, sm.at[l], 3, M)
        xt[...] = low[...].T

    finish(first)
    sm[...] = jnp.zeros_like(sm)
    start_layer(1)
    begin(u_copies(0, 1))
    pl.semaphore_wait(barrier, 3 + len(zn))
    for src, dst, i in ((y_in, lo_out, 0), (rms_in, rm_out, 1)):
        out_send(src, dst, i).start()
        out_keep(src, dst, i).start()

    def layer(li, _):
        l = 1 - li
        n0 = 3 * li
        spl = spv.at[l, 0]
        sml = sm.at[l]
        def down_step(ri, r):
            m = 4 * li + ri
            finish(g_copies(m))
            put(n0, r, dot(xt[...], g[lax.rem(m, 2)]))

            @pl.when(m + 2 < 8)
            def _():
                begin(g_copies(m + 2))
        slots(n0, down_step)

        @pl.when(li == 0)
        def _():
            if zin:
                for h in range(NC):
                    begin(first_z(h))

        @pl.when(li == 1)
        def _():
            both(ev_y, 1)
        finish(u_copies(l, 0))
        low2[...] = (u[0] * spl[3:4, :] + spl[4:5, :]).astype(bf16)
        xt[...] = low2[...].T

        def up_step(ri, r):
            m = 4 * li + ri
            b = lax.rem(m, 2)
            finish(f_copies(m))
            ffn_bwd_block(low, wu.at[b], wd.at[b], gp.at[b], low2, dx, sml.at[pl.ds(8 + r, 1)])
            put(n0 + 1, r, dot(xt[...], low2[...]))

            @pl.when(m + 2 < 8)
            def _():
                begin(f_copies(m + 2))

            @pl.when((li == 1) & (ri == 1))
            def _():
                both(ev_x, 2)
        slots(n0 + 1, up_step)

        @pl.when(li == 0)
        def _():
            if not zin:
                both(ev_x, 0)

        norm_bwd(dx, u.at[0], inv.at[0], spl[3:4, :], dx, low, sml, 0, M)

        @pl.when(li == 0)
        def _():
            begin(u_copies(0, 0))
        xt2[...] = low[...].T
        finish(x_copy(x_in.at[s]))
        xt[...] = xin[...].T

        @pl.when(li == 0)
        def _():
            begin(x_copy(x_in.at[s]))

        def attn_step(ri, r):
            m = 4 * li + ri
            b = lax.rem(m, 2)
            finish(a_copies(m))
            attn_bwd_block(low, wa.at[b], qkv.at[b], a.at[b], dc, dqkv, dx, sml.at[pl.ds(12 + r, 1)], nch, L)
            put(n0 + 2, r, jnp.concatenate([dot(xt[...], dqkv[...]), dot(xt2[...], c[b])], axis=1))

            @pl.when(m + 2 < 8)
            def _():
                begin(a_copies(m + 2))

            @pl.when((li == 0) & (ri == 1))
            def _():
                both(ev_x, 1)

            if not zin:
                @pl.when((li == 0) & (ri == 2))
                def _():
                    both(ev_y, 0)

            @pl.when((li == 1) & (ri == 0))
            def _():
                both(ev_x, 3)

            @pl.when((li == 1) & (ri == 1))
            def _():
                both(ev_y, 2)
                if zin:
                    ev_first_z()

            @pl.when((li == 1) & (ri == 2))
            def _():
                both(ev_x, 4)

            @pl.when((li == 1) & (ri == 3))
            def _():
                both(ev_y, 3)
                if zin:
                    ev_first_x()
        slots(n0 + 2, attn_step)
        dyv[...] = dx[...].astype(bf16)
        own = l == s

        @pl.when(own)
        def _():
            dh_keep().start()

        @pl.when(jnp.logical_not(own))
        def _():
            dh_send().start()

        @pl.when(own & (li == 0))
        def _():
            dh_keep().wait()

        @pl.when(jnp.logical_not(own) & (li == 0))
        def _():
            dh_send().wait_send()

        @pl.when(li == 0)
        def _():
            start_layer(0)
        return 0

    def dh_keep():
        return pltpu.make_async_copy(dyv, dh_out.at[s], ol.at[2])

    def dh_send():
        return remote(dyv, dh_out.at[s], osend.at[2], orecv.at[2], sib)

    lax.fori_loop(0, 2, layer, 0)

    m_copy(0).start()
    both(ev_y, 4)
    m_add(0, 0)
    m_copy(1).start()
    both(ev_x, 5)
    if zin:
        ev_first_y()
    both(ev_z, 1)
    both(ev_z, 2)
    m_add(1, 1)
    m_copy(2).start()
    both(ev_y, 5)
    both(ev_z, 3)
    m_add(2, 2)
    if zin:
        for d in range(1, n_dp):
            m_z(d).start()
    both(ev_z, 4)
    if zin:
        for d in range(1, n_dp):
            m_z(d).wait_send()
        for d in range(1, n_dp):
            m_add(2 + d, 0)
    smc = pltpu.make_async_copy(sm.at[s], sm_out, ld.at[5])
    smc.start()
    both(ev_z, 5)

    smc.wait()
    m_copy(0).wait_send()
    for r in range(4):
        d_copy(r).wait_send()
    for n in range(6):
        for h in range(NC):
            if zin and n == 0:
                for d in first_z(h) + [first_x(h, i) for i in range(4)] + first_y(h):
                    d.wait_send()
                continue
            for d in [x_copy_of(n, h, i) for i in range(4)] + y_copies(n, h):
                d.wait_send()
            if zin:
                for d in z_copies(n, h):
                    d.wait_send()
            else:
                q_copy(n, h).wait()
    for src, dst, i in ((y_in, lo_out, 0), (rms_in, rm_out, 1)):
        out_send(src, dst, i).wait()
        out_keep(src, dst, i).wait()
    @pl.when(s == 0)
    def _():
        dh_keep().wait()
    @pl.when(s == 1)
    def _():
        dh_send().wait_send()
    arrived(dh_out.at[1 - s], orecv.at[2])
    if zin:
        for k in range(3):
            arrived(f_out.at[2 - k, 1 - s], frecv.at[k])
            f_keep(k).wait()
            f_send(k).wait_send()


def run_k2(nch, L, n_dp, *ops):
    M = nch * L
    zin = n_dp == 4
    sub = D // (NJ * 4)
    S = jax.ShapeDtypeStruct
    V = pltpu.VMEM
    any_ = pl.BlockSpec(memory_space=pl.ANY)
    outs = (S((3, 2, 2, sub, 768), f32) if zin else S((2, 3, NC, 2, NJ, sub, CW), bf16), S((16, 768), f32), S((2, M, D), bf16), S((2, M, D), bf16), S((2, 16, 128), f32))
    DMA = pltpu.SemaphoreType.DMA
    REG = pltpu.SemaphoreType.REGULAR
    bufs = [V((2, D, 768), bf16), V((2, D, 768), bf16), V((2, D, 768), bf16), V((2, M, FB), f32), V((2, M, FB), bf16), V((2, M, 3 * HB), bf16), V((2, nch, HPB, L, L), bf16), V((2, M, HB), bf16),
            V((2, M, D), f32), V((2, M, 1), f32), V((M, D), bf16), V((M, D), bf16), V((2, 4, 8, D), f32), V((M, D), f32), V((M, D), bf16), V((M, D), bf16), V((M, HB), bf16), V((M, 3 * HB), bf16), V((D, M), bf16), V((D, M), bf16),
            V((4, 2, 2, NJ, sub, 768), bf16), V((4, 2, NJ, sub, 768), bf16), V((6, NC, 2, 4, NJ, sub, CW), bf16), V((3, NC, 4, NJ, sub, CW), bf16), V((6, NC, 2, NJ, sub, CW), bf16),
            V((6, NC, 3, 2, sub, CW) if zin else (8, 128), bf16), V((6, 2, sub, 768) if zin else (8, 128), f32), V((2, 16, 768), f32), V((6, 16, 768), f32),
            V((NC, 3, 2, 4, sub, CW) if zin else (8, 128), bf16), V((NC, 4, sub, CW), bf16), V((NC, 2, sub, CW), bf16), pltpu.SemaphoreType.DMA((NC, 3)), pltpu.SemaphoreType.DMA((NC, 3))]
    sems = [DMA((2,)), DMA((2, 3)), DMA((2, 4)), DMA((7,)), DMA((4,)), DMA((4,)), DMA((6, NC, 4)), DMA((6, NC, 4)), DMA((6, NC, 2)), DMA((6, NC, 2)), DMA((6, NC, 3)), DMA((6, NC, 3)), DMA((3,)), DMA((3,)), DMA((6, NC)), DMA((6,)), DMA((6,)),
            DMA((3,)), DMA((3,)), DMA((3,)), REG, REG, REG]
    return pl.pallas_call(
        functools.partial(k2_kernel, nch, L, n_dp, zin),
        out_shape=outs,
        in_specs=[any_] * 13,
        out_specs=[any_] * len(outs),
        scratch_shapes=bufs + sems,
        compiler_params=pltpu.CompilerParams(collective_id=1, has_side_effects=True, vmem_limit_bytes=63 << 20),
        name="backward_reduce",
    )(*ops)

def finish_kernel(n_dp, nch, len_ref, f_in, sm_in, rm_in, lo_in, dh_in, lo_out, dh_out, gu, gd, gq, qb, go, ub, vec, sums, f_ref, sm_ref, rm_ref, lo_ref, dh_ref, sem):
    t = lax.axis_index("tensor")
    j = lax.axis_index("dp")
    loads = [pltpu.make_async_copy(src, dst, sem.at[i]) for i, (src, dst) in enumerate(((f_in, f_ref), (sm_in, sm_ref), (rm_in, rm_ref), (lo_in, lo_ref), (dh_in, dh_ref)))]
    stores = [pltpu.make_async_copy(src, dst, sem.at[5 + i]) for i, (src, dst) in enumerate(((f_ref.at[1], gu), (f_ref.at[2], gd), (lo_ref, lo_out), (dh_ref, dh_out)))]
    for d in loads:
        d.start()
    for d in loads:
        d.wait()
    for d in stores:
        d.start()
    ga = f_ref[0]
    for i in range(3):
        gq[i] = ga[:, i * HB:(i + 1) * HB]
    go[...] = ga[:, 3 * HB:4 * HB].T
    part = HS // n_dp
    share = D // (4 * n_dp)
    off = (j * 4 + t) * share
    rolled = pltpu.roll(sm_ref[0:8, :], lax.rem(D - off, D), 1)
    for i in range(6):
        vec[i] = rolled[i:i + 1, 0:share]
    slots = pltpu.roll(sm_ref[8:16, :], lax.rem(D - j * part, D), 1)
    for i in range(FB // HS):
        ub[i] = slots[0:1, i * HS:i * HS + part]
    for i in range(HPB):
        for b in range(2):
            lo = 2 * b * HB + i * HS
            qb[i, b:b + 1, :] = slots[4:5, lo:lo + part]
    for h in range(2):
        for c in range(nch):
            at = h * nch + c
            size = len_ref[t * 2 * nch + at].astype(f32)
            for k in range(3):
                sums[k, 0:1, at:at + 1] = rm_ref[h, k * nch + c:k * nch + c + 1, 0:1] / size
    for d in stores:
        d.wait()


def run_finish(n_dp, nch, M, lengths, f, sm, rm, lo, dh):
    S = jax.ShapeDtypeStruct
    V = pltpu.VMEM
    dd = D // n_dp
    part = HS // n_dp
    vm = pl.BlockSpec(memory_space=pltpu.VMEM)
    any_ = pl.BlockSpec(memory_space=pl.ANY)
    return pl.pallas_call(
        functools.partial(finish_kernel, n_dp, nch),
        out_shape=(S((2, M, D), bf16), S((2, M, D), bf16), S((dd, FB), f32), S((dd, FB), f32), S((3, dd, HB), f32), S((HPB, 2, part), f32), S((HB, dd), f32),
                   S((FB // HS, 1, part), f32), S((6, 1, D // (4 * n_dp)), f32), S((3, 1, 2 * nch), f32)),
        in_specs=[pl.BlockSpec(memory_space=pltpu.SMEM)] + [any_] * 5,
        out_specs=[any_] * 4 + [vm] * 6,
        scratch_shapes=[V((3, dd, FB), f32), V((16, D), f32), V((2, 16, 128), f32), V((2, M, D), bf16), V((2, M, D), bf16), pltpu.SemaphoreType.DMA((9,))],
        compiler_params=pltpu.CompilerParams(vmem_limit_bytes=60 << 20),
        name="finish",
    )(lengths, f, sm, rm, lo, dh)


def on_device(inputs, lengths, cotangent, w_qkv, qv_bias, w_out, out_bias, ln1_gain, ln1_bias, w_up, up_bias, w_down, down_bias, ln2_gain, ln2_bias):
    s = lax.axis_index("section")
    n_dp = lax.axis_size("dp")
    chains, L, _ = inputs.shape
    nch = chains // 2
    M = nch * L
    x = inputs.reshape(2, M, D)
    dy = cotangent.reshape(2, M, D)
    w_all, sp_all, qkv, a, c, u, inv, g, gp, y, rms = run_k1(
        nch, L, lengths, x, jnp.swapaxes(w_qkv[0], 1, 2), w_out[0], w_up[0], w_down[0], qv_bias[0].transpose(1, 0, 2), up_bias.transpose(1, 0, 2), out_bias, ln1_gain, ln1_bias, down_bias, ln2_gain, ln2_bias)
    grads, sm, lo, dh, rm = run_k2(nch, L, n_dp, w_all, sp_all, qkv, a, c, u, inv, g, gp, y, x, dy, rms)
    if n_dp == 4:
        grads = grads.reshape(3, D // n_dp, 768)
    else:
        mine = grads[s].astype(f32)
        got = lax.ppermute(grads[1 - s], "section", [(0, 1), (1, 0)]).astype(f32)
        both = jnp.stack([jnp.where(s == 0, mine, got), jnp.where(s == 0, got, mine)])
        both = both.transpose(1, 4, 0, 3, 5, 2, 6).reshape(3, D, 768)
        grads = lax.psum_scatter(both, "dp", scatter_dimension=1, tiled=True)
        sm = lax.psum(sm, "dp")
    lo, dh, gu, gd, gq, qb, go, ub, vec, sums = run_finish(n_dp, nch, M, lengths, grads, sm, rm, lo, dh)
    return (lo.reshape(1, chains, L, D), dh.reshape(1, chains, L, D), gq[None], qb.transpose(1, 0, 2)[None], go[None], gu[None],
            ub.transpose(1, 0, 2), gd.T[None], vec.transpose(1, 0, 2), sums.transpose(1, 0, 2))


def solution(mesh):
    in_specs = (
        P(("dp", "tensor"), None, None),
        P("dp"),
        P(("dp", "tensor"), None, None),
        P("section", None, None, "tensor"),
        P("section", None, "tensor", None),
        P("section", "tensor", None),
        P("section", None),
        P("section", None),
        P("section", None),
        P("section", None, "tensor"),
        P("section", "tensor", None),
        P("section", "tensor", None),
        P("section", None),
        P("section", None),
        P("section", None),
    )
    out_specs = (
        P("section", ("dp", "tensor"), None, None),
        P("section", ("dp", "tensor"), None, None),
        P("section", None, "dp", "tensor"),
        P("section", None, "tensor", "dp"),
        P("section", "tensor", "dp"),
        P("section", "dp", "tensor"),
        P("section", "tensor", "dp"),
        P("section", "tensor", "dp"),
        P("section", None, ("dp", "tensor")),
        P("section", None, ("dp", "tensor")),
    )
    return jax.shard_map(on_device, mesh=mesh, in_specs=in_specs, out_specs=out_specs, check_vma=False)
```

```python
import functools

import jax
import jax.numpy as jnp
from jax import lax
from jax.experimental import pallas as pl
from jax.experimental.pallas import tpu as pltpu
from jax.sharding import PartitionSpec as P


f32, bf16 = jnp.float32, jnp.bfloat16
D, FB, HB, HS = 768, 768, 192, 64
NT = (((1,), (1,)), ((), ()))
NN = (((1,), (0,)), ((), ()))
TN = (((0,), (0,)), ((), ()))
EPS_NORM, EPS_ROOT = 1e-12, 1e-6
MASK_FILL = -1e9
ROOT_HALF, INV_ROOT_TWO_PI = 0.7071067811865476, 0.3989422804014327
MESH = pl.DeviceIdType.MESH
KA, KU, KD = 0, 1, 2
HPB = HB // HS


def dot(a, b, dims=NN):
    return lax.dot_general(a, b, dims, preferred_element_type=f32)


def rows(i, n):
    return pl.ds(pl.multiple_of(i * n, n), n)


def mean_last(v):
    return jnp.mean(v, axis=-1, keepdims=True)


def rms_rows(v):
    return jnp.sqrt(mean_last(v * v) + EPS_ROOT)


def norm_step(x, gain, bias):
    c = x - mean_last(x)
    inv = lax.rsqrt(mean_last(c * c) + EPS_NORM)
    u = c * inv
    return u * gain + bias, u, inv


def norm_back(dn, u, inv, gain):
    du = dn * gain
    return inv * (du - mean_last(du) - u * mean_last(du * u))


def part8(v):
    t = v[0:8]
    for i in range(1, v.shape[0] // 8):
        t = t + v[8 * i:8 * (i + 1)]
    return t


def col_sum(v):
    return jnp.sum(part8(v), axis=0, keepdims=True)


def row_block(M):
    for n in (96, 80, 64, 48, 32, 16):
        if M % n == 0:
            return n
    return M


def attn_fwd_block(x_ref, wa_ref, sp_ref, kb_ref, qkv_ref, a_ref, c_ref, acc_ref, nch, L):
    qkv_ref[...] = (dot(x_ref[...], wa_ref[0:3 * HB, :], NT) + sp_ref[1:2, 0:3 * HB]).astype(bf16)
    for c in range(nch):
        rs = slice(c * L, (c + 1) * L)
        qkv = qkv_ref[rs, :]
        kb = kb_ref[c:c + 1, :]

        def head(t, i):
            return qkv[:, t * HB + i * HS:t * HB + (i + 1) * HS]
        scores = [dot(head(0, i), head(1, i), NT) * (HS ** -0.5) + kb for i in range(HPB)]
        probs = []
        for i in range(HPB):
            e = jnp.exp(scores[i] - jnp.max(scores[i], axis=-1, keepdims=True))
            a = (e / jnp.sum(e, axis=-1, keepdims=True)).astype(bf16)
            a_ref[c, i] = a
            probs.append(a)
        c_ref[rs, :] = jnp.concatenate([dot(probs[i], head(2, i)).astype(bf16) for i in range(HPB)], axis=1)
    acc_ref[...] += dot(c_ref[...], wa_ref[3 * HB:4 * HB, :])


def ln1_fwd(x_ref, acc_ref, sp_ref, u_ref, inv_ref, nlow_ref, rms_ref, M):
    rb = M // 3 if M % 48 == 0 else M

    def body(i, _):
        rs = rows(i, rb)
        h = x_ref[rs, :].astype(f32)
        att = acc_ref[rs, :] + sp_ref[2:3, :]
        n, u, inv = norm_step(h + att, sp_ref[3:4, :], sp_ref[4:5, :])
        u_ref[rs, :] = u
        inv_ref[rs, :] = inv
        nlow_ref[rs, :] = n.astype(bf16)
        rms_ref[0, rs, :] = rms_rows(h)
        rms_ref[1, rs, :] = rms_rows(att)
        return 0
    lax.fori_loop(0, M // rb, body, 0)


def up_block(nlow_ref, wu_ref, sp_ref, g_ref, gp_ref):
    for j in range(FB // 256):
        js = slice(256 * j, 256 * (j + 1))
        z = dot(nlow_ref[...], wu_ref[:, js]) + sp_ref[0:1, js]
        cdf = 0.5 * (1.0 + lax.erf(z * ROOT_HALF))
        g_ref[:, js] = (z * cdf).astype(bf16)
        gp_ref[:, js] = cdf + z * (INV_ROOT_TWO_PI * jnp.exp(-0.5 * z * z))


def down_block(g_ref, wd_ref, acc_ref):
    acc_ref[...] += dot(g_ref[...], wd_ref[...])


def ln2_fwd(u1_ref, acc_ref, sp_ref, u_ref, inv_ref, y_ref, rms_ref, M):
    rb = M // 3 if M % 48 == 0 else M

    def body(i, _):
        rs = rows(i, rb)
        n = u1_ref[rs, :] * sp_ref[3:4, :] + sp_ref[4:5, :]
        ffn = acc_ref[rs, :] + sp_ref[5:6, :]
        y, u, inv = norm_step(n + ffn, sp_ref[6:7, :], sp_ref[7:8, :])
        u_ref[rs, :] = u
        inv_ref[rs, :] = inv
        y_ref[rs, :] = y.astype(bf16)
        rms_ref[2, rs, :] = rms_rows(ffn)
        return 0
    lax.fori_loop(0, M // rb, body, 0)


def norm_bwd(dy_ref, u_ref, inv_ref, gain, dx_ref, low_ref, sm_ref, row, M):
    rb = row_block(M)

    def body(i, carry):
        a, b, c = carry
        rs = rows(i, rb)
        dy = dy_ref[rs, :].astype(f32)
        u = u_ref[rs, :]
        dx = norm_back(dy, u, inv_ref[rs, :], gain)
        dx_ref[rs, :] = dx
        low_ref[rs, :] = dx.astype(bf16)
        return (a + part8(dx), b + part8(dy * u), c + part8(dy))
    z = jnp.zeros((8, D), f32)
    sums = lax.fori_loop(0, M // rb, body, (z, z, z))
    for k in range(3):
        sm_ref[row + k:row + k + 1, :] = jnp.sum(sums[k], axis=0, keepdims=True)


def ffn_bwd_block(df_ref, wu_ref, wd_ref, gp_ref, dz_ref, dx_ref, ub_ref):
    for j in range(FB // 256):
        js = slice(256 * j, 256 * (j + 1))
        dz = (dot(df_ref[...], wd_ref[js, :], NT) * gp_ref[:, js]).astype(bf16)
        dz_ref[:, js] = dz
        ub_ref[:, js] = col_sum(dz.astype(f32))
    dx_ref[...] += dot(dz_ref[...], wu_ref[...], NT)


def attn_bwd_block(da_ref, wa_ref, qkv_ref, a_ref, dc_ref, dqkv_ref, dx_ref, qb_ref, nch, L):
    dc_ref[...] = dot(da_ref[...], wa_ref[3 * HB:4 * HB, :], NT).astype(bf16)
    for c in range(nch):
        rs = slice(c * L, (c + 1) * L)
        qkv = qkv_ref[rs, :]
        dc = dc_ref[rs, :]

        def head(t, i):
            return qkv[:, t * HB + i * HS:t * HB + (i + 1) * HS]
        dcs = [dc[:, i * HS:(i + 1) * HS] for i in range(HPB)]
        probs = [a_ref[c, i] for i in range(HPB)]
        drs = [dot(dcs[i], head(2, i), NT) for i in range(HPB)]
        dss = []
        for i in range(HPB):
            af = probs[i].astype(f32)
            t = af * drs[i]
            dss.append(((t - af * jnp.sum(t, axis=-1, keepdims=True)) * (HS ** -0.5)).astype(bf16))
        dqs = [dot(dss[i], head(1, i)) for i in range(HPB)]
        dks = [dot(dss[i], head(0, i), TN) for i in range(HPB)]
        dvs = [dot(probs[i], dcs[i], TN) for i in range(HPB)]
        dqkv_ref[rs, :] = jnp.concatenate(dqs + dks + dvs, axis=1).astype(bf16)
    dx_ref[...] += dot(dqkv_ref[...], wa_ref[0:3 * HB, :])
    qb_ref[:, 0:3 * HB] = col_sum(dqkv_ref[...].astype(f32))
ZR = 192
XY = D - ZR


def k1_kernel(nch, L,
              len_ref, x_in, wq_in, wo_in, wu_in, wd_in, qv_in, ub_in, v0_in, v1_in, v2_in, v3_in, v4_in, v5_in,
              w_out, sp_out, qkv_out, a_out, c_out, u_out, inv_out, g_out, gp_out, y_out, rms_out,
              wv, spv, xb, qkv, a, c, u, inv, g, gp, nlow, acc, rms, rmsv, wa_in, sp_in, qv, ub, vecs, kb_ref,
              recv, send, sp_recv, sp_send, loc, wsave, ssave, pre, go):
    M = nch * L
    s = lax.axis_index("section")
    t = lax.axis_index("tensor")
    xn = {"tensor": t + 1 - 2 * lax.rem(t, 2)}
    yn = {"tensor": t + 2 - 4 * lax.rem(t // 2, 2)}
    j = lax.axis_index("dp")
    sib = {"section": 1 - s}
    zn = {"dp": j + 1 - 2 * lax.rem(j, 2)}
    diag = {"tensor": 3 - t}
    e = lax.rem(j, 2)
    srcs = (wa_in, wu_in, wd_in)

    def remote(src, dst, ss, rs, dev):
        return pltpu.make_async_remote_copy(src_ref=src, dst_ref=dst, send_sem=ss, recv_sem=rs, device_id=dev, device_id_type=MESH)

    def span(start, n):
        return pl.ds(pl.multiple_of(start, 16), n)
    fetched = span(e * ZR, XY)
    half = [span(e * ZR + i * (XY // 2), XY // 2) for i in range(2)]
    given = span(e * XY, ZR)
    taken = span((1 - e) * XY, ZR)

    def view(ref, p):
        if p == 0:
            return ref.at[0]
        if p in (1, 2):
            return ref.at[p, fetched]
        if p in (3, 4):
            return ref.at[3, half[p - 3]]
        return ref.at[p - 4, taken]

    def part(l, k, p):
        return view(wv.at[l, k], p)

    def wait_part(l, k, p):
        ref = part(l, k, p)
        pltpu.make_async_copy(ref, ref, recv.at[l, k, p]).wait()

    def own_sends(l, k):
        return [remote(srcs[k].at[fetched], wv.at[l, k, 1, fetched], send.at[k, 0], recv.at[l, k, 1], xn),
                remote(srcs[k].at[fetched], wv.at[l, k, 2, fetched], send.at[k, 1], recv.at[l, k, 2], yn)]

    def own_local(l, k):
        return remote(srcs[k], wv.at[l, k, 0], send.at[k, 7], recv.at[l, k, 0], sib)

    def fwd_y(l, k):
        return remote(wv.at[l, k, 1, half[0]], wv.at[l, k, 3, half[0]], send.at[k, 2], recv.at[l, k, 3], yn)

    def fwd_x(l, k):
        return remote(wv.at[l, k, 2, half[1]], wv.at[l, k, 3, half[1]], send.at[k, 3], recv.at[l, k, 4], xn)

    def to_z(l, k, slot):
        ref = wv.at[l, k, slot, given]
        return remote(ref, ref, send.at[k, 3 + slot], recv.at[l, k, 4 + slot], zn)

    def to_sib(l, k, p):
        return remote(part(l, k, p), part(l, k, p), send.at[k, 7 + p], recv.at[l, k, p], sib)

    def save_w(l, k, p):
        return pltpu.make_async_copy(part(l, k, p), view(w_out.at[l, k], p), wsave.at[l, k, p])

    def arrive(l, k, p):
        wait_part(l, k, p)

        @pl.when(s == l)
        def _():
            if p == 1:
                fwd_y(l, k).start()
                to_z(l, k, 1).start()
            if p == 2:
                fwd_x(l, k).start()
                to_z(l, k, 2).start()
                if k == KA:
                    for d in own_sends(l, KD):
                        d.start()

                    @pl.when(l == 0)
                    def _():
                        own_local(0, KU).start()
                        own_local(0, KD).start()
            if p in (3, 4):
                @pl.when(e == p - 3)
                def _():
                    to_z(l, k, 3).start()
            if p > 0:
                to_sib(l, k, p).start()
        save_w(l, k, p).start()

    others = [(q, {"section": sec, "tensor": dev["tensor"]}) for q, dev in ((1, xn), (2, yn), (3, diag)) for sec in (s, 1 - s)] + [(0, sib)]

    def sp_sends(l):
        return [remote(sp_in, spv.at[l, q], sp_send.at[i], sp_recv.at[l, q], dev) for i, (q, dev) in enumerate(others)]

    def sp_wait(l):
        for q in range(4):
            pltpu.make_async_copy(spv.at[l, q], spv.at[l, q], sp_recv.at[l, q]).wait()

    loads = [pltpu.make_async_copy(src, dst, pre.at[i]) for i, (src, dst) in enumerate(
        [(wq_in.at[i], wa_in.at[pl.ds(i * HB, HB)]) for i in range(3)] + [(wo_in, wa_in.at[pl.ds(3 * HB, HB)]), (qv_in, qv), (ub_in, ub)] + [(v, vecs.at[i]) for i, v in enumerate((v0_in, v1_in, v2_in, v3_in, v4_in, v5_in))])]
    xcopy = pltpu.make_async_copy(x_in.at[s], xb, loc.at[0])
    for d in loads:
        d.start()
    xcopy.start()
    barrier = pltpu.get_barrier_semaphore()
    for dev in [zn] + [dev for q, dev in others]:
        pl.semaphore_signal(barrier, inc=1, device_id=dev, device_id_type=MESH)
    for d in loads:
        d.wait()
    zeros = jnp.zeros((1, HB), f32)
    sp_in[0:1, :] = jnp.concatenate([ub[i] for i in range(FB // HS)], axis=1)
    sp_in[1:2, :] = jnp.concatenate([qv[i, 0:1, :] for i in range(HPB)] + [zeros] + [qv[i, 1:2, :] for i in range(HPB)] + [zeros], axis=1)
    for i in range(6):
        sp_in[2 + i:3 + i, :] = vecs[i]
    first = (t * 2 + s) * nch
    place = lax.broadcasted_iota(jnp.int32, (1, L), 1)
    for i in range(nch):
        kb_ref[i:i + 1, :] = jnp.where(place < len_ref[first + i], 0.0, MASK_FILL)
    pl.semaphore_wait(barrier, 1 + len(others))

    for l in range(2):
        @pl.when(s == l)
        def _():
            for d in sp_sends(l):
                d.start()
            pltpu.make_async_copy(sp_in, spv.at[l, 0], sp_recv.at[l, 0]).start()
            if l == 0:
                for k in (KA, KU):
                    for d in own_sends(l, k):
                        d.start()
            for k in range(3):
                pltpu.make_async_copy(srcs[k], wv.at[l, k, 0], recv.at[l, k, 0]).start()
                if l == 1 or k == KA:
                    own_local(l, k).start()
    for l in range(2):
        sp_wait(l)
    xcopy.wait()
    spsave = pltpu.make_async_copy(spv, sp_out, loc.at[1])
    spsave.start()

    def saves(l, which):
        pairs = {0: (qkv, qkv_out.at[l]), 1: (a, a_out.at[l]), 2: (c, c_out.at[l]), 3: (u.at[0], u_out.at[l, 0]),
                 4: (inv, inv_out.at[l]), 5: (g, g_out.at[l]), 6: (gp, gp_out.at[l]), 7: (u.at[1], u_out.at[l, 1]), 8: (xb, y_out.at[l])}
        src, dst = pairs[which]
        return pltpu.make_async_copy(src, dst, ssave.at[which])

    def layer(l, _):
        acc[...] = jnp.zeros_like(acc)
        @pl.when(l == 1)
        def _():
            for w in (0, 1, 2):
                saves(0, w).wait()

        def attn_step(r, _):
            @pl.when(r == 0)
            def _():
                arrive(l, KA, 0)
            @pl.when(r == 1)
            def _():
                @pl.when(l == 0)
                def _():
                    arrive(0, KA, 1)
                    arrive(0, KA, 2)
                for k, p in ((KU, 1), (KU, 2), (KA, 5), (KA, 6)):
                    arrive(l, k, p)

            @pl.when(r == 3)
            def _():
                for k, p in ((KA, 3), (KA, 4), (KU, 5), (KU, 6), (KA, 7)):
                    arrive(l, k, p)
            attn_fwd_block(xb, wv.at[l, KA, r], spv.at[l, r], kb_ref, qkv.at[r], a.at[r], c.at[r], acc, nch, L)
            return 0
        lax.fori_loop(0, 4, attn_step, 0)
        arrive(l, KD, 1)
        arrive(l, KD, 2)

        @pl.when((l == 0) & (s == 0))
        def _():
            pl.semaphore_signal(go, inc=1, device_id=sib, device_id_type=MESH)

        @pl.when((l == 0) & (s == 1))
        def _():
            pl.semaphore_wait(go, 1)
            for k in (KA, KU):
                for d in own_sends(1, k):
                    d.start()
        for w in (0, 1, 2):
            saves(l, w).start()
        @pl.when(l == 1)
        def _():
            for w in (3, 4, 5, 6, 7):
                saves(0, w).wait()
        ln1_fwd(xb, acc, spv.at[l, 0], u.at[0], inv.at[0], nlow, rms, M)
        saves(l, 3).start()

        def up_step(r, _):
            @pl.when(r == 0)
            def _():
                arrive(l, KU, 0)

            @pl.when(r == 3)
            def _():
                for k, p in ((KU, 3), (KU, 4), (KD, 5), (KD, 6), (KD, 3), (KD, 4), (KU, 7)):
                    arrive(l, k, p)
            up_block(nlow, wv.at[l, KU, r], spv.at[l, r], g.at[r], gp.at[r])
            return 0
        lax.fori_loop(0, 4, up_step, 0)
        saves(l, 5).start()
        saves(l, 6).start()
        acc[...] = jnp.zeros_like(acc)
        @pl.when(l == 1)
        def _():
            saves(0, 8).wait()

        def down_step(r, _):
            @pl.when(r == 0)
            def _():
                arrive(l, KD, 0)

            @pl.when(r == 3)
            def _():
                arrive(l, KD, 7)

                @pl.when(l == 0)
                def _():
                    arrive(1, KA, 1)
                    arrive(1, KA, 2)
            down_block(g.at[r], wv.at[l, KD, r], acc)
            return 0
        lax.fori_loop(0, 4, down_step, 0)
        ln2_fwd(u.at[0], acc, spv.at[l, 0], u.at[1], inv.at[1], xb, rms, M)
        for w in (4, 7, 8):
            saves(l, w).start()
        for k in range(3):
            for ch in range(nch):
                rs = slice(ch * L, (ch + 1) * L)
                live = lax.broadcasted_iota(jnp.int32, (L, 1), 0) < len_ref[first + ch]
                v = jnp.sum(jnp.where(live, rms[k, rs, :], 0.0), axis=0, keepdims=True)
                rmsv[l, pl.ds(k * nch + ch, 1), :] = jnp.broadcast_to(v, (1, 128))
        return 0
    lax.fori_loop(0, 2, layer, 0)
    for w in range(9):
        saves(1, w).wait()
    rc = pltpu.make_async_copy(rmsv, rms_out, loc.at[0])
    rc.start()
    rc.wait()
    spsave.wait()
    for l in range(2):
        for k in range(3):
            for p in range(8):
                save_w(l, k, p).wait()
        @pl.when(s == l)
        def _():
            for k in range(3):
                for d in own_sends(l, k) + [own_local(l, k), fwd_y(l, k), fwd_x(l, k)] + [to_z(l, k, q) for q in (1, 2, 3)] + [to_sib(l, k, p) for p in range(1, 8)]:
                    d.wait_send()
            for d in sp_sends(l):
                d.wait_send()


def run_k1(nch, L, lengths, x, *ops):
    M = nch * L
    S = jax.ShapeDtypeStruct
    V = pltpu.VMEM
    any_ = pl.BlockSpec(memory_space=pl.ANY)
    outs = (S((2, 3, 4, D, 768), bf16), S((2, 4, 8, D), f32), S((2, 4, M, 3 * HB), bf16), S((2, 4, nch, 3, L, L), bf16), S((2, 4, M, HB), bf16),
            S((2, 2, M, D), f32), S((2, 2, M, 1), f32), S((2, 4, M, FB), bf16), S((2, 4, M, FB), f32), S((2, M, D), bf16), S((2, 16, 128), f32))
    DMA = pltpu.SemaphoreType.DMA
    return pl.pallas_call(
        functools.partial(k1_kernel, nch, L),
        out_shape=outs,
        in_specs=[pl.BlockSpec(memory_space=pltpu.SMEM)] + [any_] * (1 + len(ops)),
        out_specs=[any_] * len(outs),
        scratch_shapes=[V((2, 3, 4, D, 768), bf16), V((2, 4, 8, D), f32), V((M, D), bf16), V((4, M, 3 * HB), bf16), V((4, nch, 3, L, L), bf16), V((4, M, HB), bf16),
                        V((2, M, D), f32), V((2, M, 1), f32), V((4, M, FB), bf16), V((4, M, FB), f32), V((M, D), bf16), V((M, D), f32), V((3, M, 1), f32), V((2, 16, 128), f32),
                        V((D, 768), bf16), V((8, D), f32), V((HPB, 2, HS), f32), V((FB // HS, 1, HS), f32), V((6, 1, D), f32), V((nch, L), f32),
                        DMA((2, 3, 8)), DMA((3, 15)), DMA((2, 4)), DMA((7,)), DMA((2,)), DMA((2, 3, 8)), DMA((9,)), DMA((12,)), pltpu.SemaphoreType.REGULAR],
        compiler_params=pltpu.CompilerParams(collective_id=0, has_side_effects=True, vmem_limit_bytes=62 << 20),
        name="gather_forward",
    )(lengths, x, *ops)

NJ = 4
NC = 2
ZF, HZ = 1, 1
CW = 768 // NC


def k2_kernel(nch, L, n_dp, zin,
              w_in, sp_in, qkv_in, a_in, c_in, u_in, inv_in, g_in, gp_in, y_in, x_in, dy_in, rms_in,
              f_out, sm_out, lo_out, dh_out, rm_out,
              wd, wu, wa, gp, g, qkv, a, c, u, inv, xin, dyv, spv, dx, low, low2, dc, dqkv, xt, xt2,
              pbuf, dbuf, qbuf, xbuf, ybuf, zbuf, fbuf, sm, smr, z0, x0, y0, z0send, z0recv,
              st_g, st_f, st_a, ld, dsend, drecv, xsend, xrecv, ysend, yrecv, zsend, zrecv, fsend, frecv, fl, msend, mrecv, osend, orecv, ol,
              dcred, xcred, ycred):
    M = nch * L
    sub = D // (NJ * 4)
    s = lax.axis_index("section")
    t = lax.axis_index("tensor")
    j = lax.axis_index("dp")
    xn = {"tensor": t + 1 - 2 * lax.rem(t, 2)}
    yn = {"tensor": t + 2 - 4 * lax.rem(t // 2, 2)}
    sib = {"section": 1 - s}
    diag = {"tensor": 3 - t}
    zn = [{"dp": lax.rem(j + d, n_dp)} for d in range(1, n_dp)] if zin else []

    def remote(src, dst, ss, rs, dev):
        return pltpu.make_async_remote_copy(src_ref=src, dst_ref=dst, send_sem=ss, recv_sem=rs, device_id=dev, device_id_type=MESH)

    def arrived(ref, sem):
        pltpu.make_async_copy(ref, ref, sem).wait()

    def where_of(m):
        li = m // 4
        return 1 - li, 3 - (m - 4 * li), lax.rem(m, 2)

    def g_copies(m):
        l, r, b = where_of(m)
        return [pltpu.make_async_copy(g_in.at[l, r], g.at[b], st_g.at[b])]

    def f_copies(m):
        l, r, b = where_of(m)
        return [pltpu.make_async_copy(w_in.at[l, KD, r], wd.at[b], st_f.at[b, 0]),
                pltpu.make_async_copy(w_in.at[l, KU, r], wu.at[b], st_f.at[b, 1]),
                pltpu.make_async_copy(gp_in.at[l, r], gp.at[b], st_f.at[b, 2])]

    def a_copies(m):
        l, r, b = where_of(m)
        return [pltpu.make_async_copy(w_in.at[l, KA, r], wa.at[b], st_a.at[b, 0]),
                pltpu.make_async_copy(qkv_in.at[l, r], qkv.at[b], st_a.at[b, 1]),
                pltpu.make_async_copy(a_in.at[l, r], a.at[b], st_a.at[b, 2]),
                pltpu.make_async_copy(c_in.at[l, r], c.at[b], st_a.at[b, 3])]

    def begin(copies):
        for d in copies:
            d.start()

    def finish(copies):
        for d in copies:
            d.wait()

    def u_copies(l, i):
        return [pltpu.make_async_copy(u_in.at[l, i], u.at[i], ld.at[2 * i]), pltpu.make_async_copy(inv_in.at[l, i], inv.at[i], ld.at[2 * i + 1])]

    def x_copy(src):
        return [pltpu.make_async_copy(src, xin, ld.at[4])]

    first = [pltpu.make_async_copy(dy_in.at[s], dyv, ld.at[5]), pltpu.make_async_copy(sp_in, spv, ld.at[6])]
    begin(first)
    begin(u_copies(1, 1))
    begin(u_copies(1, 0))
    begin(f_copies(0))
    begin(f_copies(1))
    begin(g_copies(0))
    begin(g_copies(1))
    begin(x_copy(y_in.at[0]))
    begin(a_copies(0))
    begin(a_copies(1))

    barrier = pltpu.get_barrier_semaphore()
    for dev in [xn, yn, diag, sib] + zn:
        pl.semaphore_signal(barrier, inc=1, device_id=dev, device_id_type=MESH)

    def out_send(src, dst, i):
        return remote(src.at[1 - s], dst.at[s], osend.at[i], orecv.at[i], sib)

    def out_keep(src, dst, i):
        return pltpu.make_async_copy(src.at[s], dst.at[s], ol.at[i])
    def d_copy(r):
        return remote(pbuf.at[r, 1 - s], dbuf.at[r], dsend.at[r], drecv.at[r], sib)

    def put(n, r, parts):
        @pl.when(n > 0)
        def _():
            d_copy(r).wait_send()
        for k in range(NJ):
            for h in range(2):
                for ab in range(2):
                    lo = ((k * 2 + h) * 2 + ab) * sub
                    pbuf[r, h, ab, k] = parts[lo:lo + sub, :].astype(bf16)

        @pl.when(n > 0)
        def _():
            pl.semaphore_wait(dcred, 1)
        d_copy(r).start()

    def x_copy_of(n, h, i):
        ab, r, dev = ((0, 1, xn), (0, 3, xn), (1, 2, yn), (1, 3, yn))[i]
        return remote(qbuf.at[n, h, ab, r], xbuf.at[lax.rem(n, 3), h, i], xsend.at[n, h, i], xrecv.at[n, h, i], dev)

    def cols(h):
        return slice(h * CW, (h + 1) * CW)

    def d_add(n, r):
        arrived(dbuf.at[r], drecv.at[r])

        def one(ab, _):
            for h in range(NC):
                qbuf[n, h, ab, r] = (pbuf[r, s, ab, :, :, cols(h)].astype(f32) + dbuf[r, ab, :, :, cols(h)].astype(f32)).astype(bf16)
            return 0
        lax.fori_loop(0, 2, one, 0)

        @pl.when(n < 5)
        def _():
            pl.semaphore_signal(dcred, inc=1, device_id=sib, device_id_type=MESH)

        x_sends(n, r)

    def x_sends(n, r):
        if zin:
            go = (n < 5) | (r < 3)
        else:
            go = n >= 0
        send_x(n, r, go)

    def send_x(n, r, go):
        def begin_x(*which):
            for h in range(NC):
                def start_them():
                    for i in which:
                        x_copy_of(n, h, i).start()
                if zin and h < HZ:
                    pl.when(n != ZF)(start_them)
                else:
                    start_them()

        @pl.when(go & (r == 3))
        def _():
            @pl.when(n >= 3)
            def _():
                pl.semaphore_wait(xcred, 1)
                pl.semaphore_wait(ycred, 1)
            begin_x(1, 3)

        @pl.when(go & (r == 2))
        def _():
            begin_x(2)

        @pl.when(go & (r == 1))
        def _():
            begin_x(0)

    def slots(n, step):
        def body(ri, _):
            step(ri, 3 - ri)

            @pl.when(ri > 0)
            def _():
                d_add(n, 4 - ri)
            return 0
        lax.fori_loop(0, 4, body, 0)
        d_add(n, 0)

    def y_copies(n, h):
        return [remote(qbuf.at[n, h, 0, 2], ybuf.at[n, h, 0], ysend.at[n, h, 0], yrecv.at[n, h, 0], yn),
                remote(qbuf.at[n, h, 1, 1], ybuf.at[n, h, 1], ysend.at[n, h, 1], yrecv.at[n, h, 1], xn)]

    def add_to(n, h, ab, r, ref):
        qbuf[n, h, ab, r] = (qbuf[n, h, ab, r].astype(f32) + ref[...].astype(f32)).astype(bf16)

    def ev_x(n, h):
        b = lax.rem(n, 3)
        cs = y_copies(n, h)
        for i, ab, r in ((1, 0, 2), (3, 1, 1), (0, 0, 0), (2, 1, 0)):
            arrived(xbuf.at[b, h, i], xrecv.at[n, h, i])
            add_to(n, h, ab, r, xbuf.at[b, h, i])
            if i in (1, 3):
                cs[i // 2].start()
        if h == NC - 1:
            @pl.when(n < 3)
            def _():
                pl.semaphore_signal(xcred, inc=1, device_id=xn, device_id_type=MESH)
                pl.semaphore_signal(ycred, inc=1, device_id=yn, device_id_type=MESH)

    def z_copies(n, h):
        return [remote(qbuf.at[n, h, :, 0, lax.rem(j + d, n_dp)], zbuf.at[n, h, d - 1], zsend.at[n, h, d - 1], zrecv.at[n, h, d - 1], zn[d - 1]) for d in range(1, n_dp)]

    def q_copy(n, h):
        li = n // 3
        return pltpu.make_async_copy(qbuf.at[n, h, :, 0], f_out.at[1 - li, lax.rem(n + 1, 3), h], fl.at[n, h])

    def ev_y(n, h):
        for i in range(2):
            arrived(ybuf.at[n, h, i], yrecv.at[n, h, i])
            add_to(n, h, i, 0, ybuf.at[n, h, i])
        if zin:
            begin(z_copies(n, h))
        else:
            q_copy(n, h).start()

    def f_keep(n):
        return pltpu.make_async_copy(fbuf.at[n], f_out.at[lax.rem(n + 1, 3), s], fl.at[lax.rem(n, 3), 0])

    def f_send(n):
        return remote(fbuf.at[n], f_out.at[lax.rem(n + 1, 3), s], fsend.at[lax.rem(n, 3)], frecv.at[lax.rem(n, 3)], sib)

    def ship(n):
        mine = (1 - n // 3) == s

        @pl.when(mine)
        def _():
            f_keep(n).start()

        @pl.when(jnp.logical_not(mine))
        def _():
            f_send(n).start()

    def ev_z(n, h):
        if not zin:
            return
        tot = qbuf[n, h, :, 0, j].astype(f32)
        for d in range(n_dp - 1):
            arrived(zbuf.at[n, h, d], zrecv.at[n, h, d])
            tot = tot + zbuf[n, h, d].astype(f32)
        fbuf[n, :, :, cols(h)] = tot
        if h < NC - 1:
            return
        ship(n)

    def first_z(h):
        return [remote(qbuf.at[ZF, h, :, :, lax.rem(j + d, n_dp)], z0.at[h, d - 1], z0send.at[h, d - 1], z0recv.at[h, d - 1], zn[d - 1]) for d in range(1, n_dp)]

    def first_x(h, i):
        ab, r, dev = ((0, 1, xn), (0, 3, xn), (1, 2, yn), (1, 3, yn))[i]
        return remote(qbuf.at[ZF, h, ab, r, j], x0.at[h, i], xsend.at[ZF, h, i], xrecv.at[ZF, h, i], dev)

    def first_y(h):
        return [remote(qbuf.at[ZF, h, 0, 2, j], y0.at[h, 0], ysend.at[ZF, h, 0], yrecv.at[ZF, h, 0], yn),
                remote(qbuf.at[ZF, h, 1, 1, j], y0.at[h, 1], ysend.at[ZF, h, 1], yrecv.at[ZF, h, 1], xn)]

    def add_first(h, ab, r, ref):
        qbuf[ZF, h, ab, r, j] = (qbuf[ZF, h, ab, r, j].astype(f32) + ref[...].astype(f32)).astype(bf16)

    def ev_first_z():
        for h in range(HZ):
            for d in range(n_dp - 1):
                arrived(z0.at[h, d], z0recv.at[h, d])
            for ab in range(2):
                for r in range(4):
                    tot = qbuf[ZF, h, ab, r, j].astype(f32)
                    for d in range(n_dp - 1):
                        tot = tot + z0[h, d, ab, r].astype(f32)
                    qbuf[ZF, h, ab, r, j] = tot.astype(bf16)
            for i in range(4):
                first_x(h, i).start()

    def ev_first_x():
        for h in range(HZ):
            for i, ab, r in ((1, 0, 2), (3, 1, 1), (0, 0, 0), (2, 1, 0)):
                arrived(x0.at[h, i], xrecv.at[ZF, h, i])
                add_first(h, ab, r, x0.at[h, i])
            begin(first_y(h))

    def ev_first_y():
        for h in range(HZ):
            for i in range(2):
                arrived(y0.at[h, i], yrecv.at[ZF, h, i])
                fbuf[ZF, i, :, cols(h)] = qbuf[ZF, h, i, 0, j].astype(f32) + y0[h, i].astype(f32)

    def both(ev, n):
        for h in range(NC):
            ev(n, h)

    def m_copy(i):
        if i == 0:
            return remote(sm.at[1 - s], smr.at[0], msend.at[0], mrecv.at[0], sib)
        return remote(sm.at[s], smr.at[i], msend.at[i], mrecv.at[i], (xn, yn, diag)[i - 1])

    def m_z(d):
        return remote(sm.at[s], smr.at[3 + d], msend.at[3 + d], mrecv.at[3 + d], zn[d - 1])

    def m_add(i, flip):
        arrived(smr.at[i], mrecv.at[i])
        sm[s, 0:8, :] += smr[i, 0:8, :]
        for r in range(4):
            for base in (8, 12):
                sm[s, base + r:base + r + 1, :] += smr[i, base + (r ^ flip):base + (r ^ flip) + 1, :]

    def rest(ev, n):
        for h in range(HZ if zin else 0, NC):
            ev(n, h)

    def start_layer(l):
        finish(u_copies(l, 1))
        norm_bwd(dyv, u.at[1], inv.at[1], spv[l, 0, 6:7, :], dx, low, sm.at[l], 3, M)
        xt2[...] = low[...].T

    finish(first)
    sm[...] = jnp.zeros_like(sm)
    start_layer(1)
    begin(u_copies(0, 1))
    pl.semaphore_wait(barrier, 4 + len(zn))
    for src, dst, i in ((y_in, lo_out, 0), (rms_in, rm_out, 1)):
        out_send(src, dst, i).start()
        out_keep(src, dst, i).start()

    def layer(li, _):
        l = 1 - li
        n0 = 3 * li
        spl = spv.at[l, 0]
        sml = sm.at[l]
        finish(u_copies(l, 0))
        low2[...] = (u[0] * spl[3:4, :] + spl[4:5, :]).astype(bf16)
        xt[...] = low2[...].T

        def up_step(ri, r):
            m = 4 * li + ri
            b = lax.rem(m, 2)
            finish(f_copies(m))
            ffn_bwd_block(low, wu.at[b], wd.at[b], gp.at[b], low2, dx, sml.at[pl.ds(8 + r, 1)])
            put(n0, r, dot(xt[...], low2[...]))

            @pl.when(m + 2 < 8)
            def _():
                begin(f_copies(m + 2))
        slots(n0, up_step)

        @pl.when(li == 1)
        def _():
            both(ev_x, 2)

        def down_step(ri, r):
            m = 4 * li + ri
            finish(g_copies(m))
            put(n0 + 1, r, dot(xt2[...], g[lax.rem(m, 2)]))

            @pl.when(m + 2 < 8)
            def _():
                begin(g_copies(m + 2))
        slots(n0 + 1, down_step)

        if zin:
            @pl.when(li == 1)
            def _():
                ev_first_z()

        if zin:
            @pl.when(li == 0)
            def _():
                for h in range(HZ):
                    begin(first_z(h))
        norm_bwd(dx, u.at[0], inv.at[0], spl[3:4, :], dx, low, sml, 0, M)

        @pl.when(li == 0)
        def _():
            begin(u_copies(0, 0))
        xt2[...] = low[...].T
        finish(x_copy(x_in.at[s]))
        xt[...] = xin[...].T

        @pl.when(li == 0)
        def _():
            begin(x_copy(x_in.at[s]))

        def attn_step(ri, r):
            m = 4 * li + ri
            b = lax.rem(m, 2)
            finish(a_copies(m))
            attn_bwd_block(low, wa.at[b], qkv.at[b], a.at[b], dc, dqkv, dx, sml.at[pl.ds(12 + r, 1)], nch, L)
            put(n0 + 2, r, jnp.concatenate([dot(xt[...], dqkv[...]), dot(xt2[...], c[b])], axis=1))

            @pl.when(m + 2 < 8)
            def _():
                begin(a_copies(m + 2))

            @pl.when((li == 0) & (ri == 0))
            def _():
                both(ev_x, 0)

            @pl.when((li == 0) & (ri == 1))
            def _():
                rest(ev_x, 1)

            @pl.when((li == 0) & (ri == 2))
            def _():
                both(ev_y, 0)

            @pl.when((li == 0) & (ri == 3))
            def _():
                rest(ev_y, 1)

            @pl.when((li == 1) & (ri == 0))
            def _():
                both(ev_x, 3)

            @pl.when((li == 1) & (ri == 1))
            def _():
                both(ev_y, 2)

            @pl.when((li == 1) & (ri == 2))
            def _():
                both(ev_x, 4)
                if zin:
                    send_x(5, 3, True)

            @pl.when((li == 1) & (ri == 3))
            def _():
                both(ev_y, 3)
                if zin:
                    ev_first_x()
        slots(n0 + 2, attn_step)
        dyv[...] = dx[...].astype(bf16)
        own = l == s

        @pl.when(own)
        def _():
            dh_keep().start()

        @pl.when(jnp.logical_not(own))
        def _():
            dh_send().start()

        @pl.when(own & (li == 0))
        def _():
            dh_keep().wait()

        @pl.when(jnp.logical_not(own) & (li == 0))
        def _():
            dh_send().wait_send()

        @pl.when(li == 0)
        def _():
            start_layer(0)
        return 0

    def dh_keep():
        return pltpu.make_async_copy(dyv, dh_out.at[s], ol.at[2])

    def dh_send():
        return remote(dyv, dh_out.at[s], osend.at[2], orecv.at[2], sib)

    lax.fori_loop(0, 2, layer, 0)

    m_copy(0).start()
    both(ev_y, 4)
    m_add(0, 0)
    for i in (1, 2, 3):
        m_copy(i).start()
    both(ev_x, 5)
    if zin:
        ev_first_y()
    both(ev_z, 0)
    rest(ev_z, 1)
    both(ev_z, 2)
    for i in (1, 2, 3):
        m_copy(i).wait_send()
    for i in (1, 2, 3):
        m_add(i, i)
    if zin:
        for d in range(1, n_dp):
            m_z(d).start()
    both(ev_y, 5)
    both(ev_z, 3)
    both(ev_z, 4)
    if zin:
        for d in range(1, n_dp):
            m_z(d).wait_send()
        for d in range(1, n_dp):
            m_add(3 + d, 0)
    smc = pltpu.make_async_copy(sm.at[s], sm_out, ld.at[5])
    smc.start()
    both(ev_z, 5)

    smc.wait()
    m_copy(0).wait_send()
    for r in range(4):
        d_copy(r).wait_send()
    for n in range(6):
        for h in range(NC):
            if zin and n == ZF and h < HZ:
                for d in first_z(h) + [first_x(h, i) for i in range(4)] + first_y(h):
                    d.wait_send()
                continue
            for d in [x_copy_of(n, h, i) for i in range(4)] + y_copies(n, h):
                d.wait_send()
            if zin:
                for d in z_copies(n, h):
                    d.wait_send()
            else:
                q_copy(n, h).wait()
    for src, dst, i in ((y_in, lo_out, 0), (rms_in, rm_out, 1)):
        out_send(src, dst, i).wait()
        out_keep(src, dst, i).wait()
    @pl.when(s == 0)
    def _():
        dh_keep().wait()
    @pl.when(s == 1)
    def _():
        dh_send().wait_send()
    arrived(dh_out.at[1 - s], orecv.at[2])
    if zin:
        for k in range(3):
            arrived(f_out.at[(k + 1) % 3, 1 - s], frecv.at[k])
            f_keep(k).wait()
            f_send(k).wait_send()


def run_k2(nch, L, n_dp, *ops):
    M = nch * L
    zin = n_dp == 4
    sub = D // (NJ * 4)
    S = jax.ShapeDtypeStruct
    V = pltpu.VMEM
    any_ = pl.BlockSpec(memory_space=pl.ANY)
    outs = (S((3, 2, 2, sub, 768), f32) if zin else S((2, 3, NC, 2, NJ, sub, CW), bf16), S((16, 768), f32), S((2, M, D), bf16), S((2, M, D), bf16), S((2, 16, 128), f32))
    DMA = pltpu.SemaphoreType.DMA
    REG = pltpu.SemaphoreType.REGULAR
    bufs = [V((2, D, 768), bf16), V((2, D, 768), bf16), V((2, D, 768), bf16), V((2, M, FB), f32), V((2, M, FB), bf16), V((2, M, 3 * HB), bf16), V((2, nch, HPB, L, L), bf16), V((2, M, HB), bf16),
            V((2, M, D), f32), V((2, M, 1), f32), V((M, D), bf16), V((M, D), bf16), V((2, 4, 8, D), f32), V((M, D), f32), V((M, D), bf16), V((M, D), bf16), V((M, HB), bf16), V((M, 3 * HB), bf16), V((D, M), bf16), V((D, M), bf16),
            V((4, 2, 2, NJ, sub, 768), bf16), V((4, 2, NJ, sub, 768), bf16), V((6, NC, 2, 4, NJ, sub, CW), bf16), V((3, NC, 4, NJ, sub, CW), bf16), V((6, NC, 2, NJ, sub, CW), bf16),
            V((6, NC, 3, 2, sub, CW) if zin else (8, 128), bf16), V((6, 2, sub, 768) if zin else (8, 128), f32), V((2, 16, 768), f32), V((7, 16, 768), f32),
            V((HZ, 3, 2, 4, sub, CW) if zin else (8, 128), bf16), V((NC, 4, sub, CW), bf16), V((NC, 2, sub, CW), bf16), pltpu.SemaphoreType.DMA((NC, 3)), pltpu.SemaphoreType.DMA((NC, 3))]
    sems = [DMA((2,)), DMA((2, 3)), DMA((2, 4)), DMA((7,)), DMA((4,)), DMA((4,)), DMA((6, NC, 4)), DMA((6, NC, 4)), DMA((6, NC, 2)), DMA((6, NC, 2)), DMA((6, NC, 3)), DMA((6, NC, 3)), DMA((3,)), DMA((3,)), DMA((6, NC)), DMA((7,)), DMA((7,)),
            DMA((3,)), DMA((3,)), DMA((3,)), REG, REG, REG]
    return pl.pallas_call(
        functools.partial(k2_kernel, nch, L, n_dp, zin),
        out_shape=outs,
        in_specs=[any_] * 13,
        out_specs=[any_] * len(outs),
        scratch_shapes=bufs + sems,
        compiler_params=pltpu.CompilerParams(collective_id=1, has_side_effects=True, vmem_limit_bytes=63 << 20),
        name="backward_reduce",
    )(*ops)

def finish_kernel(n_dp, nch, len_ref, f_in, sm_in, rm_in, lo_in, dh_in, lo_out, dh_out, gu, gd, gq, qb, go, ub, vec, sums, f_ref, sm_ref, rm_ref, lo_ref, dh_ref, sem):
    t = lax.axis_index("tensor")
    j = lax.axis_index("dp")
    loads = [pltpu.make_async_copy(src, dst, sem.at[i]) for i, (src, dst) in enumerate(((f_in, f_ref), (sm_in, sm_ref), (rm_in, rm_ref), (lo_in, lo_ref), (dh_in, dh_ref)))]
    stores = [pltpu.make_async_copy(src, dst, sem.at[5 + i]) for i, (src, dst) in enumerate(((f_ref.at[1], gu), (f_ref.at[2], gd), (lo_ref, lo_out), (dh_ref, dh_out)))]
    for d in loads:
        d.start()
    for d in loads:
        d.wait()
    for d in stores:
        d.start()
    ga = f_ref[0]
    for i in range(3):
        gq[i] = ga[:, i * HB:(i + 1) * HB]
    go[...] = ga[:, 3 * HB:4 * HB].T
    part = HS // n_dp
    share = D // (4 * n_dp)
    off = (j * 4 + t) * share
    rolled = pltpu.roll(sm_ref[0:8, :], lax.rem(D - off, D), 1)
    for i in range(6):
        vec[i] = rolled[i:i + 1, 0:share]
    slots = pltpu.roll(sm_ref[8:16, :], lax.rem(D - j * part, D), 1)
    for i in range(FB // HS):
        ub[i] = slots[0:1, i * HS:i * HS + part]
    for i in range(HPB):
        for b in range(2):
            lo = 2 * b * HB + i * HS
            qb[i, b:b + 1, :] = slots[4:5, lo:lo + part]
    for h in range(2):
        for c in range(nch):
            at = h * nch + c
            size = len_ref[t * 2 * nch + at].astype(f32)
            for k in range(3):
                sums[k, 0:1, at:at + 1] = rm_ref[h, k * nch + c:k * nch + c + 1, 0:1] / size
    for d in stores:
        d.wait()


def run_finish(n_dp, nch, M, lengths, f, sm, rm, lo, dh):
    S = jax.ShapeDtypeStruct
    V = pltpu.VMEM
    dd = D // n_dp
    part = HS // n_dp
    vm = pl.BlockSpec(memory_space=pltpu.VMEM)
    any_ = pl.BlockSpec(memory_space=pl.ANY)
    return pl.pallas_call(
        functools.partial(finish_kernel, n_dp, nch),
        out_shape=(S((2, M, D), bf16), S((2, M, D), bf16), S((dd, FB), f32), S((dd, FB), f32), S((3, dd, HB), f32), S((HPB, 2, part), f32), S((HB, dd), f32),
                   S((FB // HS, 1, part), f32), S((6, 1, D // (4 * n_dp)), f32), S((3, 1, 2 * nch), f32)),
        in_specs=[pl.BlockSpec(memory_space=pltpu.SMEM)] + [any_] * 5,
        out_specs=[any_] * 4 + [vm] * 6,
        scratch_shapes=[V((3, dd, FB), f32), V((16, D), f32), V((2, 16, 128), f32), V((2, M, D), bf16), V((2, M, D), bf16), pltpu.SemaphoreType.DMA((9,))],
        compiler_params=pltpu.CompilerParams(vmem_limit_bytes=60 << 20),
        name="finish",
    )(lengths, f, sm, rm, lo, dh)


def on_device(inputs, lengths, cotangent, w_qkv, qv_bias, w_out, out_bias, ln1_gain, ln1_bias, w_up, up_bias, w_down, down_bias, ln2_gain, ln2_bias):
    s = lax.axis_index("section")
    n_dp = lax.axis_size("dp")
    chains, L, _ = inputs.shape
    nch = chains // 2
    M = nch * L
    x = inputs.reshape(2, M, D)
    dy = cotangent.reshape(2, M, D)
    w_all, sp_all, qkv, a, c, u, inv, g, gp, y, rms = run_k1(
        nch, L, lengths, x, jnp.swapaxes(w_qkv[0], 1, 2), w_out[0], w_up[0], w_down[0], qv_bias[0].transpose(1, 0, 2), up_bias.transpose(1, 0, 2), out_bias, ln1_gain, ln1_bias, down_bias, ln2_gain, ln2_bias)
    grads, sm, lo, dh, rm = run_k2(nch, L, n_dp, w_all, sp_all, qkv, a, c, u, inv, g, gp, y, x, dy, rms)
    if n_dp == 4:
        grads = grads.reshape(3, D // n_dp, 768)
    else:
        mine = grads[s].astype(f32)
        got = lax.ppermute(grads[1 - s], "section", [(0, 1), (1, 0)]).astype(f32)
        both = jnp.stack([jnp.where(s == 0, mine, got), jnp.where(s == 0, got, mine)])
        both = both.transpose(1, 4, 0, 3, 5, 2, 6).reshape(3, D, 768)
        grads = lax.psum_scatter(both, "dp", scatter_dimension=1, tiled=True)
        sm = lax.psum(sm, "dp")
    lo, dh, gu, gd, gq, qb, go, ub, vec, sums = run_finish(n_dp, nch, M, lengths, grads, sm, rm, lo, dh)
    return (lo.reshape(1, chains, L, D), dh.reshape(1, chains, L, D), gq[None], qb.transpose(1, 0, 2)[None], go[None], gu[None],
            ub.transpose(1, 0, 2), gd.T[None], vec.transpose(1, 0, 2), sums.transpose(1, 0, 2))


def solution(mesh):
    in_specs = (
        P(("dp", "tensor"), None, None),
        P("dp"),
        P(("dp", "tensor"), None, None),
        P("section", None, None, "tensor"),
        P("section", None, "tensor", None),
        P("section", "tensor", None),
        P("section", None),
        P("section", None),
        P("section", None),
        P("section", None, "tensor"),
        P("section", "tensor", None),
        P("section", "tensor", None),
        P("section", None),
        P("section", None),
        P("section", None),
    )
    out_specs = (
        P("section", ("dp", "tensor"), None, None),
        P("section", ("dp", "tensor"), None, None),
        P("section", None, "dp", "tensor"),
        P("section", None, "tensor", "dp"),
        P("section", "tensor", "dp"),
        P("section", "dp", "tensor"),
        P("section", "tensor", "dp"),
        P("section", "tensor", "dp"),
        P("section", None, ("dp", "tensor")),
        P("section", None, ("dp", "tensor")),
    )
    return jax.shard_map(on_device, mesh=mesh, in_specs=in_specs, out_specs=out_specs, check_vma=False)
```

```python
import functools

import jax
import jax.numpy as jnp
from jax import lax
from jax.experimental import pallas as pl
from jax.experimental.pallas import tpu as pltpu
from jax.sharding import PartitionSpec as P


f32, bf16 = jnp.float32, jnp.bfloat16
D, FB, HB, HS = 768, 768, 192, 64
NT = (((1,), (1,)), ((), ()))
NN = (((1,), (0,)), ((), ()))
TN = (((0,), (0,)), ((), ()))
EPS_NORM, EPS_ROOT = 1e-12, 1e-6
MASK_FILL = -1e9
ROOT_HALF, INV_ROOT_TWO_PI = 0.7071067811865476, 0.3989422804014327
MESH = pl.DeviceIdType.MESH
KA, KU, KD = 0, 1, 2
HPB = HB // HS


def dot(a, b, dims=NN):
    return lax.dot_general(a, b, dims, preferred_element_type=f32)


def rows(i, n):
    return pl.ds(pl.multiple_of(i * n, n), n)


def mean_last(v):
    return jnp.mean(v, axis=-1, keepdims=True)


def rms_rows(v):
    return jnp.sqrt(mean_last(v * v) + EPS_ROOT)


def norm_step(x, gain, bias):
    c = x - mean_last(x)
    inv = lax.rsqrt(mean_last(c * c) + EPS_NORM)
    u = c * inv
    return u * gain + bias, u, inv


def norm_back(dn, u, inv, gain):
    du = dn * gain
    return inv * (du - mean_last(du) - u * mean_last(du * u))


def part8(v):
    t = v[0:8]
    for i in range(1, v.shape[0] // 8):
        t = t + v[8 * i:8 * (i + 1)]
    return t


def col_sum(v):
    return jnp.sum(part8(v), axis=0, keepdims=True)


def row_block(M):
    for n in (96, 80, 64, 48, 32, 16):
        if M % n == 0:
            return n
    return M


def attn_fwd_block(x_ref, wa_ref, sp_ref, kb_ref, qkv_ref, a_ref, c_ref, acc_ref, nch, L):
    qkv_ref[...] = (dot(x_ref[...], wa_ref[0:3 * HB, :], NT) + sp_ref[1:2, 0:3 * HB]).astype(bf16)
    for c in range(nch):
        rs = slice(c * L, (c + 1) * L)
        qkv = qkv_ref[rs, :]
        kb = kb_ref[c:c + 1, :]

        def head(t, i):
            return qkv[:, t * HB + i * HS:t * HB + (i + 1) * HS]
        scores = [dot(head(0, i), head(1, i), NT) * (HS ** -0.5) + kb for i in range(HPB)]
        probs = []
        for i in range(HPB):
            e = jnp.exp(scores[i] - jnp.max(scores[i], axis=-1, keepdims=True))
            a = (e / jnp.sum(e, axis=-1, keepdims=True)).astype(bf16)
            a_ref[c, i] = a
            probs.append(a)
        c_ref[rs, :] = jnp.concatenate([dot(probs[i], head(2, i)).astype(bf16) for i in range(HPB)], axis=1)
    acc_ref[...] += dot(c_ref[...], wa_ref[3 * HB:4 * HB, :])


def ln1_fwd(x_ref, acc_ref, sp_ref, u_ref, inv_ref, nlow_ref, rms_ref, M):
    rb = M // 3 if M % 48 == 0 else M

    def body(i, _):
        rs = rows(i, rb)
        h = x_ref[rs, :].astype(f32)
        att = acc_ref[rs, :] + sp_ref[2:3, :]
        n, u, inv = norm_step(h + att, sp_ref[3:4, :], sp_ref[4:5, :])
        u_ref[rs, :] = u
        inv_ref[rs, :] = inv
        nlow_ref[rs, :] = n.astype(bf16)
        rms_ref[0, rs, :] = rms_rows(h)
        rms_ref[1, rs, :] = rms_rows(att)
        return 0
    lax.fori_loop(0, M // rb, body, 0)


def up_block(nlow_ref, wu_ref, sp_ref, g_ref, gp_ref):
    for j in range(FB // 256):
        js = slice(256 * j, 256 * (j + 1))
        z = dot(nlow_ref[...], wu_ref[:, js]) + sp_ref[0:1, js]
        cdf = 0.5 * (1.0 + lax.erf(z * ROOT_HALF))
        g_ref[:, js] = (z * cdf).astype(bf16)
        gp_ref[:, js] = cdf + z * (INV_ROOT_TWO_PI * jnp.exp(-0.5 * z * z))


def down_block(g_ref, wd_ref, acc_ref):
    acc_ref[...] += dot(g_ref[...], wd_ref[...])


def ln2_fwd(u1_ref, acc_ref, sp_ref, u_ref, inv_ref, y_ref, rms_ref, M):
    rb = M // 3 if M % 48 == 0 else M

    def body(i, _):
        rs = rows(i, rb)
        n = u1_ref[rs, :] * sp_ref[3:4, :] + sp_ref[4:5, :]
        ffn = acc_ref[rs, :] + sp_ref[5:6, :]
        y, u, inv = norm_step(n + ffn, sp_ref[6:7, :], sp_ref[7:8, :])
        u_ref[rs, :] = u
        inv_ref[rs, :] = inv
        y_ref[rs, :] = y.astype(bf16)
        rms_ref[2, rs, :] = rms_rows(ffn)
        return 0
    lax.fori_loop(0, M // rb, body, 0)


def norm_bwd(dy_ref, u_ref, inv_ref, gain, dx_ref, low_ref, sm_ref, row, M):
    rb = row_block(M)

    def body(i, carry):
        a, b, c = carry
        rs = rows(i, rb)
        dy = dy_ref[rs, :].astype(f32)
        u = u_ref[rs, :]
        dx = norm_back(dy, u, inv_ref[rs, :], gain)
        dx_ref[rs, :] = dx
        low_ref[rs, :] = dx.astype(bf16)
        return (a + part8(dx), b + part8(dy * u), c + part8(dy))
    z = jnp.zeros((8, D), f32)
    sums = lax.fori_loop(0, M // rb, body, (z, z, z))
    for k in range(3):
        sm_ref[row + k:row + k + 1, :] = jnp.sum(sums[k], axis=0, keepdims=True)


def ffn_bwd_block(df_ref, wu_ref, wd_ref, gp_ref, dz_ref, dx_ref, ub_ref):
    for j in range(FB // 256):
        js = slice(256 * j, 256 * (j + 1))
        dz = (dot(df_ref[...], wd_ref[js, :], NT) * gp_ref[:, js]).astype(bf16)
        dz_ref[:, js] = dz
        ub_ref[:, js] = col_sum(dz.astype(f32))
    dx_ref[...] += dot(dz_ref[...], wu_ref[...], NT)


def attn_bwd_block(da_ref, wa_ref, qkv_ref, a_ref, dc_ref, dqkv_ref, dx_ref, qb_ref, nch, L):
    dc_ref[...] = dot(da_ref[...], wa_ref[3 * HB:4 * HB, :], NT).astype(bf16)
    for c in range(nch):
        rs = slice(c * L, (c + 1) * L)
        qkv = qkv_ref[rs, :]
        dc = dc_ref[rs, :]

        def head(t, i):
            return qkv[:, t * HB + i * HS:t * HB + (i + 1) * HS]
        dcs = [dc[:, i * HS:(i + 1) * HS] for i in range(HPB)]
        probs = [a_ref[c, i] for i in range(HPB)]
        drs = [dot(dcs[i], head(2, i), NT) for i in range(HPB)]
        dss = []
        for i in range(HPB):
            af = probs[i].astype(f32)
            t = af * drs[i]
            dss.append(((t - af * jnp.sum(t, axis=-1, keepdims=True)) * (HS ** -0.5)).astype(bf16))
        dqs = [dot(dss[i], head(1, i)) for i in range(HPB)]
        dks = [dot(dss[i], head(0, i), TN) for i in range(HPB)]
        dvs = [dot(probs[i], dcs[i], TN) for i in range(HPB)]
        dqkv_ref[rs, :] = jnp.concatenate(dqs + dks + dvs, axis=1).astype(bf16)
    dx_ref[...] += dot(dqkv_ref[...], wa_ref[0:3 * HB, :])
    qb_ref[:, 0:3 * HB] = col_sum(dqkv_ref[...].astype(f32))
ZR = 192
XY = D - ZR


def k1_kernel(nch, L,
              len_ref, x_in, wq_in, wo_in, wu_in, wd_in, qv_in, ub_in, v0_in, v1_in, v2_in, v3_in, v4_in, v5_in,
              w_out, sp_out, qkv_out, a_out, c_out, u_out, inv_out, g_out, gp_out, y_out, rms_out,
              wv, spv, xb, qkv, a, c, u, inv, g, gp, nlow, acc, rms, rmsv, wa_in, sp_in, qv, ub, vecs, kb_ref,
              recv, send, sp_recv, sp_send, loc, wsave, ssave, pre, go):
    M = nch * L
    s = lax.axis_index("section")
    t = lax.axis_index("tensor")
    xn = {"tensor": t + 1 - 2 * lax.rem(t, 2)}
    yn = {"tensor": t + 2 - 4 * lax.rem(t // 2, 2)}
    j = lax.axis_index("dp")
    sib = {"section": 1 - s}
    zn = {"dp": j + 1 - 2 * lax.rem(j, 2)}
    diag = {"tensor": 3 - t}
    e = lax.rem(j, 2)
    srcs = (wa_in, wu_in, wd_in)

    def remote(src, dst, ss, rs, dev):
        return pltpu.make_async_remote_copy(src_ref=src, dst_ref=dst, send_sem=ss, recv_sem=rs, device_id=dev, device_id_type=MESH)

    def span(start, n):
        return pl.ds(pl.multiple_of(start, 16), n)
    fetched = span(e * ZR, XY)
    half = [span(e * ZR + i * (XY // 2), XY // 2) for i in range(2)]
    given = span(e * XY, ZR)
    taken = span((1 - e) * XY, ZR)

    def view(ref, p):
        if p == 0:
            return ref.at[0]
        if p in (1, 2):
            return ref.at[p, fetched]
        if p in (3, 4):
            return ref.at[3, half[p - 3]]
        return ref.at[p - 4, taken]

    def part(l, k, p):
        return view(wv.at[l, k], p)

    def wait_part(l, k, p):
        ref = part(l, k, p)
        pltpu.make_async_copy(ref, ref, recv.at[l, k, p]).wait()

    def own_sends(l, k):
        return [remote(srcs[k].at[fetched], wv.at[l, k, 1, fetched], send.at[k, 0], recv.at[l, k, 1], xn),
                remote(srcs[k].at[fetched], wv.at[l, k, 2, fetched], send.at[k, 1], recv.at[l, k, 2], yn)]

    def own_local(l, k):
        return remote(srcs[k], wv.at[l, k, 0], send.at[k, 7], recv.at[l, k, 0], sib)

    def fwd_y(l, k):
        return remote(wv.at[l, k, 1, half[0]], wv.at[l, k, 3, half[0]], send.at[k, 2], recv.at[l, k, 3], yn)

    def fwd_x(l, k):
        return remote(wv.at[l, k, 2, half[1]], wv.at[l, k, 3, half[1]], send.at[k, 3], recv.at[l, k, 4], xn)

    def to_z(l, k, slot):
        ref = wv.at[l, k, slot, given]
        return remote(ref, ref, send.at[k, 3 + slot], recv.at[l, k, 4 + slot], zn)

    def to_sib(l, k, p):
        return remote(part(l, k, p), part(l, k, p), send.at[k, 7 + p], recv.at[l, k, p], sib)

    def save_w(l, k, p):
        return pltpu.make_async_copy(part(l, k, p), view(w_out.at[l, k], p), wsave.at[l, k, p])

    def arrive(l, k, p):
        wait_part(l, k, p)

        @pl.when(s == l)
        def _():
            if p == 1:
                fwd_y(l, k).start()
                to_z(l, k, 1).start()
            if p == 2:
                fwd_x(l, k).start()
                to_z(l, k, 2).start()
                if k == KA:
                    for d in own_sends(l, KD):
                        d.start()

                    @pl.when(l == 0)
                    def _():
                        own_local(0, KU).start()
                        own_local(0, KD).start()
            if p in (3, 4):
                @pl.when(e == p - 3)
                def _():
                    to_z(l, k, 3).start()
            if p > 0:
                to_sib(l, k, p).start()
        save_w(l, k, p).start()

    others = [(q, {"section": sec, "tensor": dev["tensor"]}) for q, dev in ((1, xn), (2, yn), (3, diag)) for sec in (s, 1 - s)] + [(0, sib)]

    def sp_sends(l):
        return [remote(sp_in, spv.at[l, q], sp_send.at[i], sp_recv.at[l, q], dev) for i, (q, dev) in enumerate(others)]

    def sp_wait(l):
        for q in range(4):
            pltpu.make_async_copy(spv.at[l, q], spv.at[l, q], sp_recv.at[l, q]).wait()

    loads = [pltpu.make_async_copy(src, dst, pre.at[i]) for i, (src, dst) in enumerate(
        [(wq_in.at[i], wa_in.at[pl.ds(i * HB, HB)]) for i in range(3)] + [(wo_in, wa_in.at[pl.ds(3 * HB, HB)]), (qv_in, qv), (ub_in, ub)] + [(v, vecs.at[i]) for i, v in enumerate((v0_in, v1_in, v2_in, v3_in, v4_in, v5_in))])]
    xcopy = pltpu.make_async_copy(x_in.at[s], xb, loc.at[0])
    for d in loads:
        d.start()
    xcopy.start()
    barrier = pltpu.get_barrier_semaphore()
    for dev in [zn] + [dev for q, dev in others]:
        pl.semaphore_signal(barrier, inc=1, device_id=dev, device_id_type=MESH)
    for d in loads:
        d.wait()
    zeros = jnp.zeros((1, HB), f32)
    sp_in[0:1, :] = jnp.concatenate([ub[i] for i in range(FB // HS)], axis=1)
    sp_in[1:2, :] = jnp.concatenate([qv[i, 0:1, :] for i in range(HPB)] + [zeros] + [qv[i, 1:2, :] for i in range(HPB)] + [zeros], axis=1)
    for i in range(6):
        sp_in[2 + i:3 + i, :] = vecs[i]
    first = (t * 2 + s) * nch
    place = lax.broadcasted_iota(jnp.int32, (1, L), 1)
    for i in range(nch):
        kb_ref[i:i + 1, :] = jnp.where(place < len_ref[first + i], 0.0, MASK_FILL)
    pl.semaphore_wait(barrier, 1 + len(others))

    for l in range(2):
        @pl.when(s == l)
        def _():
            for d in sp_sends(l):
                d.start()
            pltpu.make_async_copy(sp_in, spv.at[l, 0], sp_recv.at[l, 0]).start()
            if l == 0:
                for k in (KA, KU):
                    for d in own_sends(l, k):
                        d.start()
            for k in range(3):
                pltpu.make_async_copy(srcs[k], wv.at[l, k, 0], recv.at[l, k, 0]).start()
                if l == 1 or k == KA:
                    own_local(l, k).start()
    for l in range(2):
        sp_wait(l)
    xcopy.wait()
    spsave = pltpu.make_async_copy(spv, sp_out, loc.at[1])
    spsave.start()

    def saves(l, which):
        pairs = {0: (qkv, qkv_out.at[l]), 1: (a, a_out.at[l]), 2: (c, c_out.at[l]), 3: (u.at[0], u_out.at[l, 0]),
                 4: (inv, inv_out.at[l]), 5: (g, g_out.at[l]), 6: (gp, gp_out.at[l]), 7: (u.at[1], u_out.at[l, 1]), 8: (xb, y_out.at[l])}
        src, dst = pairs[which]
        return pltpu.make_async_copy(src, dst, ssave.at[which])

    def layer(l, _):
        acc[...] = jnp.zeros_like(acc)
        @pl.when(l == 1)
        def _():
            for w in (0, 1, 2):
                saves(0, w).wait()

        def attn_step(r, _):
            @pl.when(r == 0)
            def _():
                arrive(l, KA, 0)
            @pl.when(r == 1)
            def _():
                @pl.when(l == 0)
                def _():
                    arrive(0, KA, 1)
                    arrive(0, KA, 2)
                for k, p in ((KU, 1), (KU, 2), (KA, 5), (KA, 6)):
                    arrive(l, k, p)

            @pl.when(r == 3)
            def _():
                for k, p in ((KA, 3), (KA, 4), (KU, 5), (KU, 6), (KA, 7)):
                    arrive(l, k, p)
            attn_fwd_block(xb, wv.at[l, KA, r], spv.at[l, r], kb_ref, qkv.at[r], a.at[r], c.at[r], acc, nch, L)
            return 0
        lax.fori_loop(0, 4, attn_step, 0)
        arrive(l, KD, 1)
        arrive(l, KD, 2)

        @pl.when((l == 0) & (s == 0))
        def _():
            pl.semaphore_signal(go, inc=1, device_id=sib, device_id_type=MESH)

        @pl.when((l == 0) & (s == 1))
        def _():
            pl.semaphore_wait(go, 1)
            for k in (KA, KU):
                for d in own_sends(1, k):
                    d.start()
        for w in (0, 1, 2):
            saves(l, w).start()
        @pl.when(l == 1)
        def _():
            for w in (3, 4, 5, 6, 7):
                saves(0, w).wait()
        ln1_fwd(xb, acc, spv.at[l, 0], u.at[0], inv.at[0], nlow, rms, M)
        saves(l, 3).start()

        def up_step(r, _):
            @pl.when(r == 0)
            def _():
                arrive(l, KU, 0)

            @pl.when(r == 3)
            def _():
                for k, p in ((KU, 3), (KU, 4), (KD, 5), (KD, 6), (KD, 3), (KD, 4), (KU, 7)):
                    arrive(l, k, p)
            up_block(nlow, wv.at[l, KU, r], spv.at[l, r], g.at[r], gp.at[r])
            return 0
        lax.fori_loop(0, 4, up_step, 0)
        saves(l, 5).start()
        saves(l, 6).start()
        acc[...] = jnp.zeros_like(acc)
        @pl.when(l == 1)
        def _():
            saves(0, 8).wait()

        def down_step(r, _):
            @pl.when(r == 0)
            def _():
                arrive(l, KD, 0)

            @pl.when(r == 3)
            def _():
                arrive(l, KD, 7)

                @pl.when(l == 0)
                def _():
                    arrive(1, KA, 1)
                    arrive(1, KA, 2)
            down_block(g.at[r], wv.at[l, KD, r], acc)
            return 0
        lax.fori_loop(0, 4, down_step, 0)
        ln2_fwd(u.at[0], acc, spv.at[l, 0], u.at[1], inv.at[1], xb, rms, M)
        for w in (4, 7, 8):
            saves(l, w).start()
        for k in range(3):
            for ch in range(nch):
                rs = slice(ch * L, (ch + 1) * L)
                live = lax.broadcasted_iota(jnp.int32, (L, 1), 0) < len_ref[first + ch]
                v = jnp.sum(jnp.where(live, rms[k, rs, :], 0.0), axis=0, keepdims=True)
                rmsv[l, pl.ds(k * nch + ch, 1), :] = jnp.broadcast_to(v, (1, 128))
        return 0
    lax.fori_loop(0, 2, layer, 0)
    for w in range(9):
        saves(1, w).wait()
    rc = pltpu.make_async_copy(rmsv, rms_out, loc.at[0])
    rc.start()
    rc.wait()
    spsave.wait()
    for l in range(2):
        for k in range(3):
            for p in range(8):
                save_w(l, k, p).wait()
        @pl.when(s == l)
        def _():
            for k in range(3):
                for d in own_sends(l, k) + [own_local(l, k), fwd_y(l, k), fwd_x(l, k)] + [to_z(l, k, q) for q in (1, 2, 3)] + [to_sib(l, k, p) for p in range(1, 8)]:
                    d.wait_send()
            for d in sp_sends(l):
                d.wait_send()


def run_k1(nch, L, lengths, x, *ops):
    M = nch * L
    S = jax.ShapeDtypeStruct
    V = pltpu.VMEM
    any_ = pl.BlockSpec(memory_space=pl.ANY)
    outs = (S((2, 3, 4, D, 768), bf16), S((2, 4, 8, D), f32), S((2, 4, M, 3 * HB), bf16), S((2, 4, nch, 3, L, L), bf16), S((2, 4, M, HB), bf16),
            S((2, 2, M, D), f32), S((2, 2, M, 1), f32), S((2, 4, M, FB), bf16), S((2, 4, M, FB), f32), S((2, M, D), bf16), S((2, 16, 128), f32))
    DMA = pltpu.SemaphoreType.DMA
    return pl.pallas_call(
        functools.partial(k1_kernel, nch, L),
        out_shape=outs,
        in_specs=[pl.BlockSpec(memory_space=pltpu.SMEM)] + [any_] * (1 + len(ops)),
        out_specs=[any_] * len(outs),
        scratch_shapes=[V((2, 3, 4, D, 768), bf16), V((2, 4, 8, D), f32), V((M, D), bf16), V((4, M, 3 * HB), bf16), V((4, nch, 3, L, L), bf16), V((4, M, HB), bf16),
                        V((2, M, D), f32), V((2, M, 1), f32), V((4, M, FB), bf16), V((4, M, FB), f32), V((M, D), bf16), V((M, D), f32), V((3, M, 1), f32), V((2, 16, 128), f32),
                        V((D, 768), bf16), V((8, D), f32), V((HPB, 2, HS), f32), V((FB // HS, 1, HS), f32), V((6, 1, D), f32), V((nch, L), f32),
                        DMA((2, 3, 8)), DMA((3, 15)), DMA((2, 4)), DMA((7,)), DMA((2,)), DMA((2, 3, 8)), DMA((9,)), DMA((12,)), pltpu.SemaphoreType.REGULAR],
        compiler_params=pltpu.CompilerParams(collective_id=0, has_side_effects=True, vmem_limit_bytes=62 << 20),
        name="gather_forward",
    )(lengths, x, *ops)

NJ = 4
NC = 2
ZF, HZ = 1, 1
CW = 768 // NC


def k2_kernel(nch, L, n_dp, zin,
              w_in, sp_in, qkv_in, a_in, c_in, u_in, inv_in, g_in, gp_in, y_in, x_in, dy_in, rms_in,
              f_out, sm_out, lo_out, dh_out, rm_out,
              wd, wu, wa, gp, g, qkv, a, c, u, inv, xin, dyv, spv, dx, low, low2, dc, dqkv, xt, xt2,
              pbuf, dbuf, qbuf, xbuf, ybuf, zbuf, fbuf, sm, smr, z0, x0, y0, z0send, z0recv,
              st_g, st_f, st_a, ld, dsend, drecv, xsend, xrecv, ysend, yrecv, zsend, zrecv, fsend, frecv, fl, msend, mrecv, osend, orecv, ol,
              dcred, xcred, ycred):
    M = nch * L
    sub = D // (NJ * 4)
    s = lax.axis_index("section")
    t = lax.axis_index("tensor")
    j = lax.axis_index("dp")
    xn = {"tensor": t + 1 - 2 * lax.rem(t, 2)}
    yn = {"tensor": t + 2 - 4 * lax.rem(t // 2, 2)}
    sib = {"section": 1 - s}
    diag = {"tensor": 3 - t}
    zn = [{"dp": lax.rem(j + d, n_dp)} for d in range(1, n_dp)] if zin else []

    def remote(src, dst, ss, rs, dev):
        return pltpu.make_async_remote_copy(src_ref=src, dst_ref=dst, send_sem=ss, recv_sem=rs, device_id=dev, device_id_type=MESH)

    def arrived(ref, sem):
        pltpu.make_async_copy(ref, ref, sem).wait()

    def where_of(m):
        li = m // 4
        return 1 - li, 3 - (m - 4 * li), lax.rem(m, 2)

    def g_copies(m):
        l, r, b = where_of(m)
        return [pltpu.make_async_copy(g_in.at[l, r], g.at[b], st_g.at[b])]

    def f_copies(m):
        l, r, b = where_of(m)
        return [pltpu.make_async_copy(w_in.at[l, KD, r], wd.at[b], st_f.at[b, 0]),
                pltpu.make_async_copy(w_in.at[l, KU, r], wu.at[b], st_f.at[b, 1]),
                pltpu.make_async_copy(gp_in.at[l, r], gp.at[b], st_f.at[b, 2])]

    def a_copies(m):
        l, r, b = where_of(m)
        return [pltpu.make_async_copy(w_in.at[l, KA, r], wa.at[b], st_a.at[b, 0]),
                pltpu.make_async_copy(qkv_in.at[l, r], qkv.at[b], st_a.at[b, 1]),
                pltpu.make_async_copy(a_in.at[l, r], a.at[b], st_a.at[b, 2]),
                pltpu.make_async_copy(c_in.at[l, r], c.at[b], st_a.at[b, 3])]

    def begin(copies):
        for d in copies:
            d.start()

    def finish(copies):
        for d in copies:
            d.wait()

    def u_copies(l, i):
        return [pltpu.make_async_copy(u_in.at[l, i], u.at[i], ld.at[2 * i]), pltpu.make_async_copy(inv_in.at[l, i], inv.at[i], ld.at[2 * i + 1])]

    def x_copy(src):
        return [pltpu.make_async_copy(src, xin, ld.at[4])]

    first = [pltpu.make_async_copy(dy_in.at[s], dyv, ld.at[5]), pltpu.make_async_copy(sp_in, spv, ld.at[6])]
    begin(first)
    begin(u_copies(1, 1))
    begin(u_copies(1, 0))
    begin(f_copies(0))
    begin(f_copies(1))
    begin(g_copies(0))
    begin(g_copies(1))
    begin(x_copy(y_in.at[0]))
    begin(a_copies(0))
    begin(a_copies(1))

    barrier = pltpu.get_barrier_semaphore()
    for dev in [xn, yn, diag, sib] + zn:
        pl.semaphore_signal(barrier, inc=1, device_id=dev, device_id_type=MESH)

    def out_send(src, dst, i):
        return remote(src.at[1 - s], dst.at[s], osend.at[i], orecv.at[i], sib)

    def out_keep(src, dst, i):
        return pltpu.make_async_copy(src.at[s], dst.at[s], ol.at[i])
    def d_copy(r):
        return remote(pbuf.at[r, 1 - s], dbuf.at[r], dsend.at[r], drecv.at[r], sib)

    def put(n, r, parts):
        @pl.when(n > 0)
        def _():
            d_copy(r).wait_send()
        for k in range(NJ):
            for h in range(2):
                for ab in range(2):
                    lo = ((k * 2 + h) * 2 + ab) * sub
                    pbuf[r, h, ab, k] = parts[lo:lo + sub, :].astype(bf16)

        @pl.when(n > 0)
        def _():
            pl.semaphore_wait(dcred, 1)
        d_copy(r).start()

    def x_copy_of(n, h, i):
        ab, r, dev = ((0, 1, xn), (0, 3, xn), (1, 2, yn), (1, 3, yn))[i]
        return remote(qbuf.at[n, h, ab, r], xbuf.at[lax.rem(n, 3), h, i], xsend.at[n, h, i], xrecv.at[n, h, i], dev)

    def cols(h):
        return slice(h * CW, (h + 1) * CW)

    def d_add(n, r):
        arrived(dbuf.at[r], drecv.at[r])

        def one(ab, _):
            for h in range(NC):
                qbuf[n, h, ab, r] = (pbuf[r, s, ab, :, :, cols(h)].astype(f32) + dbuf[r, ab, :, :, cols(h)].astype(f32)).astype(bf16)
            return 0
        lax.fori_loop(0, 2, one, 0)

        @pl.when(n < 5)
        def _():
            pl.semaphore_signal(dcred, inc=1, device_id=sib, device_id_type=MESH)

        x_sends(n, r)

    def x_sends(n, r):
        if zin:
            go = (n < 5) | (r < 3)
        else:
            go = n >= 0
        send_x(n, r, go)

    def send_x(n, r, go):
        def begin_x(*which):
            for h in range(NC):
                def start_them():
                    for i in which:
                        x_copy_of(n, h, i).start()
                if zin and h < HZ:
                    pl.when(n != ZF)(start_them)
                else:
                    start_them()

        @pl.when(go & (r == 3))
        def _():
            @pl.when(n >= 3)
            def _():
                pl.semaphore_wait(xcred, 1)
                pl.semaphore_wait(ycred, 1)
            begin_x(1, 3)

        @pl.when(go & (r == 2))
        def _():
            begin_x(2)

        @pl.when(go & (r == 1))
        def _():
            begin_x(0)

    def slots(n, step):
        def body(ri, _):
            step(ri, 3 - ri)

            @pl.when(ri > 0)
            def _():
                d_add(n, 4 - ri)
            return 0
        lax.fori_loop(0, 4, body, 0)
        d_add(n, 0)

    def y_copies(n, h):
        return [remote(qbuf.at[n, h, 0, 2], ybuf.at[n, h, 0], ysend.at[n, h, 0], yrecv.at[n, h, 0], yn),
                remote(qbuf.at[n, h, 1, 1], ybuf.at[n, h, 1], ysend.at[n, h, 1], yrecv.at[n, h, 1], xn)]

    def add_to(n, h, ab, r, ref):
        qbuf[n, h, ab, r] = (qbuf[n, h, ab, r].astype(f32) + ref[...].astype(f32)).astype(bf16)

    def ev_x(n, h):
        b = lax.rem(n, 3)
        cs = y_copies(n, h)
        for i, ab, r in ((1, 0, 2), (3, 1, 1), (0, 0, 0), (2, 1, 0)):
            arrived(xbuf.at[b, h, i], xrecv.at[n, h, i])
            add_to(n, h, ab, r, xbuf.at[b, h, i])
            if i in (1, 3):
                cs[i // 2].start()
        if h == NC - 1:
            @pl.when(n < 3)
            def _():
                pl.semaphore_signal(xcred, inc=1, device_id=xn, device_id_type=MESH)
                pl.semaphore_signal(ycred, inc=1, device_id=yn, device_id_type=MESH)

    def z_copies(n, h):
        return [remote(qbuf.at[n, h, :, 0, lax.rem(j + d, n_dp)], zbuf.at[n, h, d - 1], zsend.at[n, h, d - 1], zrecv.at[n, h, d - 1], zn[d - 1]) for d in range(1, n_dp)]

    def q_copy(n, h):
        li = n // 3
        return pltpu.make_async_copy(qbuf.at[n, h, :, 0], f_out.at[1 - li, lax.rem(n + 1, 3), h], fl.at[n, h])

    def ev_y(n, h):
        for i in range(2):
            arrived(ybuf.at[n, h, i], yrecv.at[n, h, i])
            add_to(n, h, i, 0, ybuf.at[n, h, i])
        if zin:
            begin(z_copies(n, h))
        else:
            q_copy(n, h).start()

    def f_keep(n):
        return pltpu.make_async_copy(fbuf.at[n], f_out.at[lax.rem(n + 1, 3), s], fl.at[lax.rem(n, 3), 0])

    def f_send(n):
        return remote(fbuf.at[n], f_out.at[lax.rem(n + 1, 3), s], fsend.at[lax.rem(n, 3)], frecv.at[lax.rem(n, 3)], sib)

    def ship(n):
        mine = (1 - n // 3) == s

        @pl.when(mine)
        def _():
            f_keep(n).start()

        @pl.when(jnp.logical_not(mine))
        def _():
            f_send(n).start()

    def ev_z(n, h):
        if not zin:
            return
        tot = qbuf[n, h, :, 0, j].astype(f32)
        for d in range(n_dp - 1):
            arrived(zbuf.at[n, h, d], zrecv.at[n, h, d])
            tot = tot + zbuf[n, h, d].astype(f32)
        fbuf[n, :, :, cols(h)] = tot
        if h < NC - 1:
            return
        ship(n)

    def first_z(h):
        return [remote(qbuf.at[ZF, h, :, :, lax.rem(j + d, n_dp)], z0.at[h, d - 1], z0send.at[h, d - 1], z0recv.at[h, d - 1], zn[d - 1]) for d in range(1, n_dp)]

    def first_x(h, i):
        ab, r, dev = ((0, 1, xn), (0, 3, xn), (1, 2, yn), (1, 3, yn))[i]
        return remote(qbuf.at[ZF, h, ab, r, j], x0.at[h, i], xsend.at[ZF, h, i], xrecv.at[ZF, h, i], dev)

    def first_y(h):
        return [remote(qbuf.at[ZF, h, 0, 2, j], y0.at[h, 0], ysend.at[ZF, h, 0], yrecv.at[ZF, h, 0], yn),
                remote(qbuf.at[ZF, h, 1, 1, j], y0.at[h, 1], ysend.at[ZF, h, 1], yrecv.at[ZF, h, 1], xn)]

    def add_first(h, ab, r, ref):
        qbuf[ZF, h, ab, r, j] = (qbuf[ZF, h, ab, r, j].astype(f32) + ref[...].astype(f32)).astype(bf16)

    def ev_first_z():
        for h in range(HZ):
            for d in range(n_dp - 1):
                arrived(z0.at[h, d], z0recv.at[h, d])
            for ab in range(2):
                for r in range(4):
                    tot = qbuf[ZF, h, ab, r, j].astype(f32)
                    for d in range(n_dp - 1):
                        tot = tot + z0[h, d, ab, r].astype(f32)
                    qbuf[ZF, h, ab, r, j] = tot.astype(bf16)
            for i in range(4):
                first_x(h, i).start()

    def ev_first_x():
        for h in range(HZ):
            for i, ab, r in ((1, 0, 2), (3, 1, 1), (0, 0, 0), (2, 1, 0)):
                arrived(x0.at[h, i], xrecv.at[ZF, h, i])
                add_first(h, ab, r, x0.at[h, i])
            begin(first_y(h))

    def ev_first_y():
        for h in range(HZ):
            for i in range(2):
                arrived(y0.at[h, i], yrecv.at[ZF, h, i])
                fbuf[ZF, i, :, cols(h)] = qbuf[ZF, h, i, 0, j].astype(f32) + y0[h, i].astype(f32)

    def both(ev, n):
        for h in range(NC):
            ev(n, h)

    def m_copy(i):
        if i == 0:
            return remote(sm.at[1 - s], smr.at[0], msend.at[0], mrecv.at[0], sib)
        return remote(sm.at[s], smr.at[i], msend.at[i], mrecv.at[i], (xn, yn, diag)[i - 1])

    def m_z(d):
        return remote(sm.at[s], smr.at[3 + d], msend.at[3 + d], mrecv.at[3 + d], zn[d - 1])

    def m_add(i, flip):
        arrived(smr.at[i], mrecv.at[i])
        sm[s, 0:8, :] += smr[i, 0:8, :]
        for r in range(4):
            for base in (8, 12):
                sm[s, base + r:base + r + 1, :] += smr[i, base + (r ^ flip):base + (r ^ flip) + 1, :]

    def rest(ev, n):
        for h in range(HZ if zin else 0, NC):
            ev(n, h)

    def start_layer(l):
        finish(u_copies(l, 1))
        norm_bwd(dyv, u.at[1], inv.at[1], spv[l, 0, 6:7, :], dx, low, sm.at[l], 3, M)
        xt2[...] = low[...].T

    finish(first)
    sm[...] = jnp.zeros_like(sm)
    start_layer(1)
    begin(u_copies(0, 1))
    pl.semaphore_wait(barrier, 4 + len(zn))
    for src, dst, i in ((y_in, lo_out, 0), (rms_in, rm_out, 1)):
        out_send(src, dst, i).start()
        out_keep(src, dst, i).start()

    def layer(li, _):
        l = 1 - li
        n0 = 3 * li
        spl = spv.at[l, 0]
        sml = sm.at[l]
        finish(u_copies(l, 0))
        low2[...] = (u[0] * spl[3:4, :] + spl[4:5, :]).astype(bf16)
        xt[...] = low2[...].T

        def up_step(ri, r):
            m = 4 * li + ri
            b = lax.rem(m, 2)
            finish(f_copies(m))
            ffn_bwd_block(low, wu.at[b], wd.at[b], gp.at[b], low2, dx, sml.at[pl.ds(8 + r, 1)])
            put(n0, r, dot(xt[...], low2[...]))

            @pl.when(m + 2 < 8)
            def _():
                begin(f_copies(m + 2))
        slots(n0, up_step)

        @pl.when(li == 1)
        def _():
            both(ev_x, 2)

        def down_step(ri, r):
            m = 4 * li + ri
            finish(g_copies(m))
            put(n0 + 1, r, dot(xt2[...], g[lax.rem(m, 2)]))

            @pl.when(m + 2 < 8)
            def _():
                begin(g_copies(m + 2))
        slots(n0 + 1, down_step)

        if zin:
            @pl.when(li == 1)
            def _():
                ev_first_z()

        if zin:
            @pl.when(li == 0)
            def _():
                for h in range(HZ):
                    begin(first_z(h))
        norm_bwd(dx, u.at[0], inv.at[0], spl[3:4, :], dx, low, sml, 0, M)

        @pl.when(li == 0)
        def _():
            begin(u_copies(0, 0))
        xt2[...] = low[...].T
        finish(x_copy(x_in.at[s]))
        xt[...] = xin[...].T

        @pl.when(li == 0)
        def _():
            begin(x_copy(x_in.at[s]))

        def attn_step(ri, r):
            m = 4 * li + ri
            b = lax.rem(m, 2)
            finish(a_copies(m))
            attn_bwd_block(low, wa.at[b], qkv.at[b], a.at[b], dc, dqkv, dx, sml.at[pl.ds(12 + r, 1)], nch, L)
            put(n0 + 2, r, jnp.concatenate([dot(xt[...], dqkv[...]), dot(xt2[...], c[b])], axis=1))

            @pl.when(m + 2 < 8)
            def _():
                begin(a_copies(m + 2))

            @pl.when((li == 0) & (ri == 0))
            def _():
                both(ev_x, 0)

            @pl.when((li == 0) & (ri == 1))
            def _():
                rest(ev_x, 1)

            @pl.when((li == 0) & (ri == 2))
            def _():
                both(ev_y, 0)

            @pl.when((li == 0) & (ri == 3))
            def _():
                rest(ev_y, 1)

            @pl.when((li == 1) & (ri == 0))
            def _():
                both(ev_x, 3)

            @pl.when((li == 1) & (ri == 1))
            def _():
                both(ev_y, 2)

            @pl.when((li == 1) & (ri == 2))
            def _():
                both(ev_x, 4)
                if zin:
                    send_x(5, 3, True)

            @pl.when((li == 1) & (ri == 3))
            def _():
                both(ev_y, 3)
                if zin:
                    ev_first_x()
        slots(n0 + 2, attn_step)
        dyv[...] = dx[...].astype(bf16)
        own = l == s

        @pl.when(own)
        def _():
            dh_keep().start()

        @pl.when(jnp.logical_not(own))
        def _():
            dh_send().start()

        @pl.when(own & (li == 0))
        def _():
            dh_keep().wait()

        @pl.when(jnp.logical_not(own) & (li == 0))
        def _():
            dh_send().wait_send()

        @pl.when(li == 0)
        def _():
            start_layer(0)
        return 0

    def dh_keep():
        return pltpu.make_async_copy(dyv, dh_out.at[s], ol.at[2])

    def dh_send():
        return remote(dyv, dh_out.at[s], osend.at[2], orecv.at[2], sib)

    lax.fori_loop(0, 2, layer, 0)

    m_copy(0).start()
    both(ev_y, 4)
    m_add(0, 0)
    for i in (1, 2, 3):
        m_copy(i).start()
    both(ev_x, 5)
    if zin:
        ev_first_y()
    both(ev_z, 0)
    rest(ev_z, 1)
    both(ev_z, 2)
    for i in (1, 2, 3):
        m_copy(i).wait_send()
    for i in (1, 2, 3):
        m_add(i, i)
    if zin:
        for d in range(1, n_dp):
            m_z(d).start()
    both(ev_y, 5)
    both(ev_z, 3)
    both(ev_z, 4)
    if zin:
        for d in range(1, n_dp):
            m_z(d).wait_send()
        for d in range(1, n_dp):
            m_add(3 + d, 0)
    smc = pltpu.make_async_copy(sm.at[s], sm_out, ld.at[5])
    smc.start()
    both(ev_z, 5)

    smc.wait()
    m_copy(0).wait_send()
    for r in range(4):
        d_copy(r).wait_send()
    for n in range(6):
        for h in range(NC):
            if zin and n == ZF and h < HZ:
                for d in first_z(h) + [first_x(h, i) for i in range(4)] + first_y(h):
                    d.wait_send()
                continue
            for d in [x_copy_of(n, h, i) for i in range(4)] + y_copies(n, h):
                d.wait_send()
            if zin:
                for d in z_copies(n, h):
                    d.wait_send()
            else:
                q_copy(n, h).wait()
    for src, dst, i in ((y_in, lo_out, 0), (rms_in, rm_out, 1)):
        out_send(src, dst, i).wait()
        out_keep(src, dst, i).wait()
    @pl.when(s == 0)
    def _():
        dh_keep().wait()
    @pl.when(s == 1)
    def _():
        dh_send().wait_send()
    arrived(dh_out.at[1 - s], orecv.at[2])
    if zin:
        for k in range(3):
            arrived(f_out.at[(k + 1) % 3, 1 - s], frecv.at[k])
            f_keep(k).wait()
            f_send(k).wait_send()


def run_k2(nch, L, n_dp, *ops):
    M = nch * L
    zin = n_dp == 4
    sub = D // (NJ * 4)
    S = jax.ShapeDtypeStruct
    V = pltpu.VMEM
    any_ = pl.BlockSpec(memory_space=pl.ANY)
    outs = (S((3, 2, 2, sub, 768), f32) if zin else S((2, 3, NC, 2, NJ, sub, CW), bf16), S((16, 768), f32), S((2, M, D), bf16), S((2, M, D), bf16), S((2, 16, 128), f32))
    DMA = pltpu.SemaphoreType.DMA
    REG = pltpu.SemaphoreType.REGULAR
    bufs = [V((2, D, 768), bf16), V((2, D, 768), bf16), V((2, D, 768), bf16), V((2, M, FB), f32), V((2, M, FB), bf16), V((2, M, 3 * HB), bf16), V((2, nch, HPB, L, L), bf16), V((2, M, HB), bf16),
            V((2, M, D), f32), V((2, M, 1), f32), V((M, D), bf16), V((M, D), bf16), V((2, 4, 8, D), f32), V((M, D), f32), V((M, D), bf16), V((M, D), bf16), V((M, HB), bf16), V((M, 3 * HB), bf16), V((D, M), bf16), V((D, M), bf16),
            V((4, 2, 2, NJ, sub, 768), bf16), V((4, 2, NJ, sub, 768), bf16), V((6, NC, 2, 4, NJ, sub, CW), bf16), V((3, NC, 4, NJ, sub, CW), bf16), V((6, NC, 2, NJ, sub, CW), bf16),
            V((6, NC, 3, 2, sub, CW) if zin else (8, 128), bf16), V((6, 2, sub, 768) if zin else (8, 128), f32), V((2, 16, 768), f32), V((7, 16, 768), f32),
            V((HZ, 3, 2, 4, sub, CW) if zin else (8, 128), bf16), V((NC, 4, sub, CW), bf16), V((NC, 2, sub, CW), bf16), pltpu.SemaphoreType.DMA((NC, 3)), pltpu.SemaphoreType.DMA((NC, 3))]
    sems = [DMA((2,)), DMA((2, 3)), DMA((2, 4)), DMA((7,)), DMA((4,)), DMA((4,)), DMA((6, NC, 4)), DMA((6, NC, 4)), DMA((6, NC, 2)), DMA((6, NC, 2)), DMA((6, NC, 3)), DMA((6, NC, 3)), DMA((3,)), DMA((3,)), DMA((6, NC)), DMA((7,)), DMA((7,)),
            DMA((3,)), DMA((3,)), DMA((3,)), REG, REG, REG]
    return pl.pallas_call(
        functools.partial(k2_kernel, nch, L, n_dp, zin),
        out_shape=outs,
        in_specs=[any_] * 13,
        out_specs=[any_] * len(outs),
        scratch_shapes=bufs + sems,
        compiler_params=pltpu.CompilerParams(collective_id=1, has_side_effects=True, vmem_limit_bytes=63 << 20),
        name="backward_reduce",
    )(*ops)

def finish_kernel(n_dp, nch, len_ref, f_in, sm_in, rm_in, lo_in, dh_in, lo_out, dh_out, gu, gd, gq, qb, go, ub, vec, sums, f_ref, sm_ref, rm_ref, lo_ref, dh_ref, sem):
    t = lax.axis_index("tensor")
    j = lax.axis_index("dp")
    loads = [pltpu.make_async_copy(src, dst, sem.at[i]) for i, (src, dst) in enumerate(((f_in.at[0], f_ref.at[0]), (sm_in, sm_ref), (rm_in, rm_ref), (lo_in, lo_ref), (dh_in, dh_ref), (f_in.at[1], f_ref.at[1]), (f_in.at[2], f_ref.at[2])))]
    stores = [pltpu.make_async_copy(src, dst, sem.at[7 + i]) for i, (src, dst) in enumerate(((lo_ref, lo_out), (dh_ref, dh_out), (f_ref.at[1], gu), (f_ref.at[2], gd)))]
    for d in loads:
        d.start()
    loads[0].wait()
    ga = f_ref[0]
    for i in range(3):
        gq[i] = ga[:, i * HB:(i + 1) * HB]
    go[...] = ga[:, 3 * HB:4 * HB].T
    for i in range(4):
        loads[3 + i].wait()
        stores[i].start()
    loads[1].wait()
    loads[2].wait()
    part = HS // n_dp
    share = D // (4 * n_dp)
    off = (j * 4 + t) * share
    rolled = pltpu.roll(sm_ref[0:8, :], lax.rem(D - off, D), 1)
    for i in range(6):
        vec[i] = rolled[i:i + 1, 0:share]
    slots = pltpu.roll(sm_ref[8:16, :], lax.rem(D - j * part, D), 1)
    for i in range(FB // HS):
        ub[i] = slots[0:1, i * HS:i * HS + part]
    for i in range(HPB):
        for b in range(2):
            lo = 2 * b * HB + i * HS
            qb[i, b:b + 1, :] = slots[4:5, lo:lo + part]
    for h in range(2):
        for c in range(nch):
            at = h * nch + c
            size = len_ref[t * 2 * nch + at].astype(f32)
            for k in range(3):
                sums[k, 0:1, at:at + 1] = rm_ref[h, k * nch + c:k * nch + c + 1, 0:1] / size
    for d in stores:
        d.wait()


def run_finish(n_dp, nch, M, lengths, f, sm, rm, lo, dh):
    S = jax.ShapeDtypeStruct
    V = pltpu.VMEM
    dd = D // n_dp
    part = HS // n_dp
    vm = pl.BlockSpec(memory_space=pltpu.VMEM)
    any_ = pl.BlockSpec(memory_space=pl.ANY)
    return pl.pallas_call(
        functools.partial(finish_kernel, n_dp, nch),
        out_shape=(S((2, M, D), bf16), S((2, M, D), bf16), S((dd, FB), f32), S((dd, FB), f32), S((3, dd, HB), f32), S((HPB, 2, part), f32), S((HB, dd), f32),
                   S((FB // HS, 1, part), f32), S((6, 1, D // (4 * n_dp)), f32), S((3, 1, 2 * nch), f32)),
        in_specs=[pl.BlockSpec(memory_space=pltpu.SMEM)] + [any_] * 5,
        out_specs=[any_] * 4 + [vm] * 6,
        scratch_shapes=[V((3, dd, FB), f32), V((16, D), f32), V((2, 16, 128), f32), V((2, M, D), bf16), V((2, M, D), bf16), pltpu.SemaphoreType.DMA((11,))],
        compiler_params=pltpu.CompilerParams(vmem_limit_bytes=60 << 20),
        name="finish",
    )(lengths, f, sm, rm, lo, dh)


def on_device(inputs, lengths, cotangent, w_qkv, qv_bias, w_out, out_bias, ln1_gain, ln1_bias, w_up, up_bias, w_down, down_bias, ln2_gain, ln2_bias):
    s = lax.axis_index("section")
    n_dp = lax.axis_size("dp")
    chains, L, _ = inputs.shape
    nch = chains // 2
    M = nch * L
    x = inputs.reshape(2, M, D)
    dy = cotangent.reshape(2, M, D)
    w_all, sp_all, qkv, a, c, u, inv, g, gp, y, rms = run_k1(
        nch, L, lengths, x, jnp.swapaxes(w_qkv[0], 1, 2), w_out[0], w_up[0], w_down[0], qv_bias[0].transpose(1, 0, 2), up_bias.transpose(1, 0, 2), out_bias, ln1_gain, ln1_bias, down_bias, ln2_gain, ln2_bias)
    grads, sm, lo, dh, rm = run_k2(nch, L, n_dp, w_all, sp_all, qkv, a, c, u, inv, g, gp, y, x, dy, rms)
    if n_dp == 4:
        grads = grads.reshape(3, D // n_dp, 768)
    else:
        mine = grads[s].astype(f32)
        got = lax.ppermute(grads[1 - s], "section", [(0, 1), (1, 0)]).astype(f32)
        both = jnp.stack([jnp.where(s == 0, mine, got), jnp.where(s == 0, got, mine)])
        both = both.transpose(1, 4, 0, 3, 5, 2, 6).reshape(3, D, 768)
        grads = lax.psum_scatter(both, "dp", scatter_dimension=1, tiled=True)
        sm = lax.psum(sm, "dp")
    lo, dh, gu, gd, gq, qb, go, ub, vec, sums = run_finish(n_dp, nch, M, lengths, grads, sm, rm, lo, dh)
    return (lo.reshape(1, chains, L, D), dh.reshape(1, chains, L, D), gq[None], qb.transpose(1, 0, 2)[None], go[None], gu[None],
            ub.transpose(1, 0, 2), gd.T[None], vec.transpose(1, 0, 2), sums.transpose(1, 0, 2))


def solution(mesh):
    in_specs = (
        P(("dp", "tensor"), None, None),
        P("dp"),
        P(("dp", "tensor"), None, None),
        P("section", None, None, "tensor"),
        P("section", None, "tensor", None),
        P("section", "tensor", None),
        P("section", None),
        P("section", None),
        P("section", None),
        P("section", None, "tensor"),
        P("section", "tensor", None),
        P("section", "tensor", None),
        P("section", None),
        P("section", None),
        P("section", None),
    )
    out_specs = (
        P("section", ("dp", "tensor"), None, None),
        P("section", ("dp", "tensor"), None, None),
        P("section", None, "dp", "tensor"),
        P("section", None, "tensor", "dp"),
        P("section", "tensor", "dp"),
        P("section", "dp", "tensor"),
        P("section", "tensor", "dp"),
        P("section", "tensor", "dp"),
        P("section", None, ("dp", "tensor")),
        P("section", None, ("dp", "tensor")),
    )
    return jax.shard_map(on_device, mesh=mesh, in_specs=in_specs, out_specs=out_specs, check_vma=False)
```
